128 devices in a mesh: grp: 8 (over x, y_lo), loss: 16 (over z, y_hi, core).
Axes of the slice: x: 4, y: 4 (y_hi: 2, y_lo: 2; y = y_hi * 2 + y_lo), z: 4, core: 2. Of those that a mesh axis runs over, the one named last changes fastest.
Arguments:
- image_embeds: bfloat16 [65536, 1152], P(('grp', 'loss')), parts along dimension 0, may hold values from -0.8 to 0.8
- text_embeds: bfloat16 [65536, 1152], P(('grp', 'loss')), parts along dimension 0, may hold values from -0.8 to 0.8
- log_scale: float32 [8], P('grp'), parts along dimension 0, may hold values from 2 to 2.5
- bias: float32 [8], P('grp'), parts along dimension 0, may hold values from -3 to -1
Outputs:
- loss_rows: float32 [65536], P(('grp', 'loss')), parts along dimension 0
- grad_image: bfloat16 [65536, 1152], P(('grp', 'loss')), parts along dimension 0
- grad_text: bfloat16 [65536, 1152], P(('grp', 'loss')), parts along dimension 0
The draws below stay inside these ranges and needn't reach their ends.
There are 8 independent parts, one for each index of `grp`. The reference program is written for one: setup_inputs(seed, part) draws one part's arguments, and reference() takes and returns one part's arrays. A program takes and returns all parts, laid end to end along the dimension named above; each array names one. Nothing has to cross between parts.
All inputs are finite; a program needn't handle non-finite values.
Results may differ from the reference program's by a relative error of at most 0.0034.
Values may be sent and summed in bfloat16 or wider, within the bound.
No kernel may reach another device: no remote copies, remote signals or barrier semaphores. Data moves between devices by JAX's collectives and lax.ppermute only.
A program may use at most 192 MiB of HBM per device.

```python
import jax
import jax.numpy as jnp
from jax import lax

E = 1152
TOTAL = 8192


def mixed_noise(key):
    key_normal = jax.random.fold_in(key, 0)
    normal_part = jax.random.normal(key_normal, (TOTAL, E), jnp.float32)
    return normal_part


def row_factor(key, spread):
    level = jax.random.uniform(key, (TOTAL, 1), jnp.float32, -1.0, 1.0)
    return jnp.exp(level * jnp.log(spread))


def pair_fields(key, spread):
    parts = jax.random.split(key, 9)
    centers = jax.random.normal(parts[0], (64, E), jnp.float32)
    picks = jax.random.randint(parts[1], (TOTAL,), 0, 64)
    strength = jax.random.uniform(parts[2], (TOTAL, 1), jnp.float32, 0.3, 0.9)
    image_raw = strength * jnp.take(centers, picks, axis=0) + mixed_noise(parts[4])
    pairing = jax.random.uniform(parts[5], (TOTAL, 1), jnp.float32, 0.5, 1.5)
    text_raw = pairing * image_raw + mixed_noise(parts[6])
    image = jnp.clip(0.03 * image_raw * row_factor(parts[7], spread), -0.8, 0.8)
    text = jnp.clip(0.03 * text_raw * row_factor(parts[8], spread), -0.8, 0.8)
    return (image, text)


def draw_image_embeds(key, part):
    image, text = pair_fields(key, 1.0)
    return image.astype(jnp.bfloat16)


def draw_text_embeds(key, part):
    image, text = pair_fields(key, 1.0)
    return text.astype(jnp.bfloat16)


def setup_inputs(seed: int = 0, part: int = 0) -> dict:
    splits = jax.random.split(jax.random.key(seed), 5)
    part_keys = jax.random.split(jax.random.fold_in(splits[4], part), 5)
    image_embeds = draw_image_embeds(jax.random.fold_in(jax.random.fold_in(splits[4], part), 71), part)
    text_embeds = draw_text_embeds(jax.random.fold_in(jax.random.fold_in(splits[4], part), 71), part)
    log_scale = jnp.clip(jax.random.uniform(part_keys[2], (1,), jnp.float32, 2.0, 2.5), 2.0, 2.5)
    bias = jnp.clip(jax.random.uniform(part_keys[3], (1,), jnp.float32, -3.0, -1.0), -3.0, -1.0)
    return {"image_embeds": image_embeds, "text_embeds": text_embeds, "log_scale": log_scale, "bias": bias}


def normalize(raw):
    wide = raw.astype(jnp.float32)
    recip = lax.rsqrt(lax.optimization_barrier(jnp.sum(wide * wide, axis=1, keepdims=True)) + 1e-06)
    return (wide * recip, recip)

def tangent(grad_unit, unit, recip):
    along = lax.optimization_barrier(jnp.sum(unit * grad_unit, axis=1, keepdims=True))
    return ((grad_unit - unit * along) * recip).astype(jnp.bfloat16)

def reference(image_embeds, text_embeds, log_scale, bias):
    scale = jnp.exp(log_scale[0])
    img_unit, img_recip = normalize(image_embeds)
    txt_unit, txt_recip = normalize(text_embeds)
    img_half = img_unit.astype(jnp.bfloat16)
    txt_half = txt_unit.astype(jnp.bfloat16)
    logits = scale * lax.dot_general(img_half, txt_half, (((1,), (1,)), ((), ())), preferred_element_type=jnp.float32) + bias[0]
    positions = jnp.arange(TOTAL, dtype=jnp.int32)
    diagonal = positions[:, None] == positions[None, :]
    signs = jnp.where(diagonal, 1.0, -1.0).astype(jnp.float32)
    loss_rows = lax.optimization_barrier(jnp.sum(jax.nn.softplus(-signs * logits), axis=1)) / TOTAL
    weights = (jax.nn.sigmoid(logits) - diagonal.astype(jnp.float32)).astype(jnp.bfloat16)
    grad_img_unit = scale * jnp.dot(weights, txt_half, preferred_element_type=jnp.float32)
    grad_txt_unit = scale * lax.dot_general(weights, img_half, (((0,), (0,)), ((), ())), preferred_element_type=jnp.float32)
    return (loss_rows, tangent(grad_img_unit, img_unit, img_recip), tangent(grad_txt_unit, txt_unit, txt_recip))
```

```python
import functools
import math

import jax
import jax.numpy as jnp
from jax import lax
from jax.experimental import pallas as pl
from jax.experimental.pallas import tpu as pltpu
from jax.sharding import PartitionSpec as P

BF, F32 = jnp.bfloat16, jnp.float32
ANY = pl.BlockSpec(memory_space=pl.ANY)
SMEM = pl.BlockSpec(memory_space=pltpu.SMEM)
VMEM = pl.BlockSpec(memory_space=pltpu.VMEM)
PAD = 16
PARAMS = pltpu.CompilerParams(vmem_limit_bytes=56 * 2**20)
NT = (((1,), (1,)), ((), ()))
TN = (((0,), (0,)), ((), ()))


def recip_of(wide):
    return lax.rsqrt(jnp.sum(wide * wide, axis=1, keepdims=True) + 1e-06)


def normalize_kernel(a_ref, b_ref, oa_ref, ob_ref):
    for ref, out in ((a_ref, oa_ref), (b_ref, ob_ref)):
        wide = ref[...].astype(F32)
        out[...] = (wide * recip_of(wide)).astype(BF)


def normalize(a, b):
    rows, width = a.shape
    spec = pl.BlockSpec((rows // 2, width), lambda i: (i, 0))
    return pl.pallas_call(
        normalize_kernel,
        grid=(2,),
        in_specs=[spec, spec],
        out_specs=[spec, spec],
        out_shape=[jax.ShapeDtypeStruct(a.shape, BF)] * 2,
        compiler_params=PARAMS,
    )(a, b)


def pair_terms(logits, scale, bias, flip):
    z = logits * scale + bias
    if flip is not None:
        z = z * flip
    e = jnp.exp2(z)
    u = 1.0 + e
    w = e * pl.reciprocal(u, approx=True)
    if flip is not None:
        w = w * flip
    q = logits.shape[1] // 4
    e0, e1, e2, e3 = (e[:, k * q : (k + 1) * q] for k in range(4))
    u0, u1, u2 = (u[:, k * q : (k + 1) * q] for k in range(3))
    s = (e0 + e1 * u0) + (e2 + e3 * u2) * (u0 * u1)
    terms = jnp.log1p(s)
    total = terms[:, :128]
    for k in range(1, q // 128):
        total = total + terms[:, k * 128 : (k + 1) * 128]
    return w.astype(BF), total


def rows_kernel(n_i, n_t, own, far, scal, *refs):
    i_in, t_in = refs[:n_i], refs[n_i : n_i + n_t]
    outs = refs[n_i + n_t : n_i + n_t + 3]
    i_buf, t_buf, w_buf, ga_buf, gb_buf, in_sem, out_sem = refs[n_i + n_t + 3 :]
    rows, width = i_buf.shape
    block = t_buf.shape[0] // n_t
    part = rows // n_i
    w_out = outs[0]
    i_copies = [
        pltpu.make_async_copy(i_in[k], i_buf.at[pl.ds(k * part, part), :], in_sem.at[k]) for k in range(n_i)
    ]
    t_copies = [
        pltpu.make_async_copy(t_in[k], t_buf.at[pl.ds(k * block, block), :], in_sem.at[n_i + k])
        for k in range(n_t)
    ]
    for c in i_copies + t_copies:
        c.start()
    for c in i_copies:
        c.wait()
    a = i_buf[...]
    scale, bias = scal[0], scal[1]
    acc = loss = None
    w_copies = []
    for k in range(n_t):
        t_copies[k].wait()
        t = t_buf[k * block : (k + 1) * block, :]
        logits = lax.dot_general(a, t, NT, preferred_element_type=F32)
        flip = None
        if own and k == 0:
            r = lax.broadcasted_iota(jnp.int32, logits.shape, 0)
            c = lax.broadcasted_iota(jnp.int32, logits.shape, 1)
            flip = jnp.where(r == c, -1.0, 1.0).astype(F32)
        w, lane = pair_terms(logits, scale, bias, flip)
        w_buf[:, k * block : (k + 1) * block] = w
        cols = pl.ds(k * block, block)
        w_copies.append(pltpu.make_async_copy(w_buf.at[:, cols], w_out.at[:, cols], out_sem.at[k]))
        w_copies[-1].start()
        prod = jnp.dot(w, t, preferred_element_type=F32)
        acc = prod if acc is None else acc + prod
        loss = lane if loss is None else loss + lane
    line = jnp.sum(jnp.transpose(loss), axis=0, keepdims=True)
    if own:
        ga_buf[...] = acc
        gb_buf[...] = jnp.broadcast_to(line, gb_buf.shape)
    else:
        half = rows // 2
        r = lax.broadcasted_iota(jnp.int32, (PAD, width), 0)
        first = 2 if far else 0
        for k, buf in enumerate((ga_buf, gb_buf)):
            buf[:half, :] = acc[k * half : (k + 1) * half].astype(BF)
            piece = line[:, k * half : (k + 1) * half]
            hi = piece.astype(BF).astype(F32)
            blank = jnp.zeros((1, width - half), F32)
            hi_row = jnp.concatenate([hi, blank], axis=1)
            lo_row = jnp.concatenate([piece - hi, blank], axis=1)
            pad = jnp.where(r == first, hi_row, jnp.where(r == first + 1, lo_row, 0.0))
            buf[half:, :] = pad.astype(BF)
    g_copies = [
        pltpu.make_async_copy(ga_buf, outs[1], out_sem.at[n_t]),
        pltpu.make_async_copy(gb_buf, outs[2], out_sem.at[n_t + 1]),
    ]
    for c in g_copies:
        c.start()
    for c in w_copies + g_copies:
        c.wait()


def rows_step(scal, pieces, texts, own=False, far=False):
    width = pieces[0].shape[1]
    rows = sum(p.shape[0] for p in pieces)
    cols = sum(t.shape[0] for t in texts)
    n_i, n_t = len(pieces), len(texts)
    if own:
        grads = [jax.ShapeDtypeStruct((rows, width), F32), jax.ShapeDtypeStruct((8, rows), F32)]
    else:
        grads = [jax.ShapeDtypeStruct((rows // 2 + PAD, width), BF)] * 2
    return pl.pallas_call(
        functools.partial(rows_kernel, n_i, n_t, own, far),
        in_specs=[SMEM] + [ANY] * (n_i + n_t),
        out_specs=[ANY] * 3,
        out_shape=[jax.ShapeDtypeStruct((rows, cols), BF)] + grads,
        scratch_shapes=[
            pltpu.VMEM((rows, width), BF),
            pltpu.VMEM((cols, width), BF),
            pltpu.VMEM((rows, cols), BF),
            pltpu.VMEM(grads[0].shape, grads[0].dtype),
            pltpu.VMEM(grads[1].shape, grads[1].dtype),
            pltpu.SemaphoreType.DMA((n_i + n_t,)),
            pltpu.SemaphoreType.DMA((n_t + 2,)),
        ],
        compiler_params=PARAMS,
    )(scal, *pieces, *texts)


def cols_kernel(n_w, n_i, first, wide, *refs):
    w_in, i_in = refs[:n_w], refs[n_w : n_w + n_i]
    outs = refs[n_w + n_i : n_w + n_i + 2]
    w_buf, i_buf, oa_buf, ob_buf, in_sem, out_sem = refs[n_w + n_i + 2 :]
    rows = w_buf.shape[1]
    block = w_buf.shape[2] // 2
    w_copies = [
        pltpu.make_async_copy(w_in[k].at[:, pl.ds(first, 2 * block)], w_buf.at[k], in_sem.at[k])
        for k in range(n_w)
    ]
    i_copies, at = [], 0
    for k in range(n_i):
        size = i_in[k].shape[0]
        i_copies.append(
            pltpu.make_async_copy(i_in[k], i_buf.at[pl.ds(at, size), :], in_sem.at[n_w + k])
        )
        at += size
    for c in w_copies + i_copies:
        c.start()
    for c in w_copies + i_copies:
        c.wait()
    out_copies = []
    for h, buf in enumerate((oa_buf, ob_buf)):
        acc = None
        for k in range(n_w):
            prod = lax.dot_general(
                w_buf[k, :, h * block : (h + 1) * block],
                i_buf[k * rows : (k + 1) * rows, :],
                TN,
                preferred_element_type=F32,
            )
            acc = prod if acc is None else acc + prod
        buf[...] = acc.astype(buf.dtype)
        out_copies.append(pltpu.make_async_copy(buf, outs[h], out_sem.at[h]))
        out_copies[-1].start()
    for c in out_copies:
        c.wait()


def cols_step(weights, images, first, dtypes):
    width = images[0].shape[1]
    rows = weights[0].shape[0]
    total = sum(i.shape[0] for i in images)
    block = weights[0].shape[1] // 4
    n_w, n_i = len(weights), len(images)
    shapes = [jax.ShapeDtypeStruct((block, width), d) for d in dtypes]
    return pl.pallas_call(
        functools.partial(cols_kernel, n_w, n_i, first * block, None),
        in_specs=[ANY] * (n_w + n_i),
        out_specs=[ANY] * 2,
        out_shape=shapes,
        scratch_shapes=[
            pltpu.VMEM((n_w, rows, 2 * block), BF),
            pltpu.VMEM((total, width), BF),
            pltpu.VMEM(shapes[0].shape, shapes[0].dtype),
            pltpu.VMEM(shapes[1].shape, shapes[1].dtype),
            pltpu.SemaphoreType.DMA((n_w + n_i,)),
            pltpu.SemaphoreType.DMA((2,)),
        ],
        compiler_params=PARAMS,
    )(*weights, *images)


def tangent(total, raw):
    wide = raw.astype(F32)
    recip = recip_of(wide)
    unit = wide * recip
    along = jnp.sum(unit * total, axis=1, keepdims=True)
    return ((total - unit * along) * recip).astype(BF)


def image_kernel(count, scal, raw, own, loss, s_ref, r_ref, grad_ref, loss_ref):
    rows = raw.shape[0]
    total = own[...] + s_ref[:rows, :].astype(F32) + r_ref[:rows, :].astype(F32)
    grad_ref[...] = tangent(total * scal[2], raw[...])
    tail = s_ref[rows:, :rows].astype(F32) + r_ref[rows:, :rows].astype(F32)
    loss_ref[...] = (loss[...] + jnp.sum(tail, axis=0, keepdims=True)) * (1.0 / count)


def image_step(scal, raw, own, loss, summed, near, half, count):
    rows, width = raw.shape
    part = rows // 2
    mine = pl.BlockSpec((part, width), lambda i: (half, 0))
    whole = pl.BlockSpec((part + PAD, width), lambda i: (0, 0))
    line = pl.BlockSpec((8, part), lambda i: (0, half))
    return pl.pallas_call(
        functools.partial(image_kernel, count),
        grid=(1,),
        in_specs=[SMEM, mine, mine, line, whole, whole],
        out_specs=[pl.BlockSpec((part, width), lambda i: (0, 0)), pl.BlockSpec((8, part), lambda i: (0, 0))],
        out_shape=[jax.ShapeDtypeStruct((part, width), BF), jax.ShapeDtypeStruct((8, part), F32)],
        compiler_params=PARAMS,
    )(scal, raw, own, loss, summed, near)


def text_kernel(scal, raw, own, a_ref, b_ref, grad_ref):
    total = own[...] + a_ref[...].astype(F32) + b_ref[...].astype(F32)
    grad_ref[...] = tangent(total * scal[2], raw[...])


def text_step(scal, raw, own, a, b):
    rows, width = raw.shape
    spec = pl.BlockSpec((rows // 2, width), lambda i: (i, 0))
    return pl.pallas_call(
        text_kernel,
        grid=(2,),
        in_specs=[SMEM] + [spec] * 4,
        out_specs=spec,
        out_shape=jax.ShapeDtypeStruct((rows, width), BF),
        compiler_params=PARAMS,
    )(scal, raw, own, a, b)


def per_device(total, image_embeds, text_embeds, log_scale, bias):
    def move(value, dz=0, dy=0, dc=0):
        pairs = [
            (z * 4 + y * 2 + c, (z + dz) % 4 * 4 + (y + dy) % 2 * 2 + (c + dc) % 2)
            for z in range(4)
            for y in range(2)
            for c in range(2)
        ]
        return lax.ppermute(value, "loss", pairs)

    scale = jnp.exp(log_scale[0])
    scal = jnp.stack([scale * (1.0 / math.log(2.0)), bias[0] * (1.0 / math.log(2.0)), scale])
    img, txt = normalize(image_embeds, text_embeds)
    half = img.shape[0] // 2
    a, b = img[:half], img[half:]
    prev_a, next_b = move(a, dz=1), move(b, dz=-1)
    txt_y = move(txt, dy=1)
    txt_c = move(txt, dc=1)
    far_a, far_b = move(prev_a, dz=1), move(next_b, dz=-1)
    txt_yc = move(txt_y, dc=1)
    prev_b, next_a = move(b, dz=1), move(a, dz=-1)
    texts = [txt, txt_c, txt_y, txt_yc]

    w_own, g_own, l_own = rows_step(scal, [img], texts, own=True)
    w_first, g_prev_a, g_next_b = rows_step(scal, [prev_a, next_b], texts)
    w_far, g_far_a, g_far_b = rows_step(scal, [far_a, far_b], texts, far=True)
    w_last, g_prev_b, g_next_a = rows_step(scal, [prev_b, next_a], texts)

    through_a, through_b = move(g_far_a, dz=-1), move(g_far_b, dz=1)
    near_b, near_a = move(g_prev_b, dz=-1), move(g_next_a, dz=1)
    sum_a = move(g_prev_a + through_a, dz=-1)
    sum_b = move(g_next_b + through_b, dz=1)

    weights = [w_own, w_first, w_far, w_last]
    images = [img, prev_a, next_b, far_a, far_b, prev_b, next_a]
    gt_y, gt_yc = cols_step(weights, images, 2, (BF, BF))
    text_y = move(gt_y + move(gt_yc, dc=1), dy=1)
    gt_own, gt_c = cols_step(weights, images, 0, (F32, BF))
    text_c = move(gt_c, dc=1)

    grad_a, loss_a = image_step(scal, image_embeds, g_own, l_own, sum_a, near_a, 0, total)
    grad_b, loss_b = image_step(scal, image_embeds, g_own, l_own, sum_b, near_b, 1, total)
    grad_text = text_step(scal, text_embeds, gt_own, text_c, text_y)
    loss_rows = jnp.concatenate([loss_a[0], loss_b[0]])
    return loss_rows, jnp.concatenate([grad_a, grad_b]), grad_text


def solution(mesh):
    placed = (P(("grp", "loss"), None), P(("grp", "loss"), None), P("grp"), P("grp"))

    def whole(image_embeds, text_embeds, log_scale, bias):
        total = image_embeds.shape[0] // mesh.shape["grp"]
        return jax.shard_map(
            functools.partial(per_device, total),
            mesh=mesh,
            in_specs=placed,
            out_specs=(P(("grp", "loss")), P(("grp", "loss"), None), P(("grp", "loss"), None)),
            check_vma=False,
        )(image_embeds, text_embeds, log_scale, bias)

    return whole
```

```python
import functools
import math

import jax
import jax.numpy as jnp
from jax import lax
from jax.experimental import pallas as pl
from jax.experimental.pallas import tpu as pltpu
from jax.sharding import PartitionSpec as P

BF, F32 = jnp.bfloat16, jnp.float32
SMEM = pl.BlockSpec(memory_space=pltpu.SMEM)
VMEM = pl.BlockSpec(memory_space=pltpu.VMEM)
COST = 2 * 10**10
PAD = 16
NT = (((1,), (1,)), ((), ()))
TN = (((0,), (0,)), ((), ()))


def call(kernel, name, inputs, outs, after=(), scoped=16, cost=COST):
    count = len(inputs)
    inputs = [*inputs, *after]
    specs = [SMEM if x.ndim == 1 else VMEM for x in inputs]

    def body(*refs):
        kernel(*refs[:count], *refs[len(inputs) :])

    return pl.pallas_call(
        body,
        name=name,
        in_specs=specs,
        out_specs=[VMEM] * len(outs),
        out_shape=outs,
        cost_estimate=pl.CostEstimate(flops=cost, bytes_accessed=0, transcendentals=0),
        compiler_params=pltpu.CompilerParams(vmem_limit_bytes=scoped * 2**20),
    )(*[x if x.ndim == 1 else pltpu.with_memory_space_constraint(x, pltpu.VMEM) for x in inputs])


def recip_of(wide):
    return lax.rsqrt(jnp.sum(wide * wide, axis=1, keepdims=True) + 1e-06)


def normalize_kernel(raw, *outs):
    wide = raw[...].astype(F32)
    unit = (wide * recip_of(wide)).astype(BF)
    rows = unit.shape[0] // len(outs)
    for k, out in enumerate(outs):
        out[...] = unit[k * rows : (k + 1) * rows]


def normalize(raw, count, name):
    rows, width = raw.shape
    return call(normalize_kernel, name, [raw], [pltpu.VMEM((rows // count, width), BF)] * count)


def pair_terms(logits, scale, bias, flip):
    z = logits * scale + bias
    if flip is not None:
        z = z * flip
    e = jnp.exp2(z)
    u = 1.0 + e
    w = e * pl.reciprocal(u, approx=True)
    if flip is not None:
        w = w * flip
    q = logits.shape[1] // 4
    e0, e1, e2, e3 = (e[:, k * q : (k + 1) * q] for k in range(4))
    u0, u1, u2 = (u[:, k * q : (k + 1) * q] for k in range(3))
    s = (e0 + e1 * u0) + (e2 + e3 * u2) * (u0 * u1)
    terms = jnp.log1p(s)
    total = terms[:, :128]
    for k in range(1, q // 128):
        total = total + terms[:, k * 128 : (k + 1) * 128]
    return w.astype(BF), total


def rows_kernel(n_i, n_t, diag, state, finish, scal, *refs):
    refs = list(refs)
    images, texts = refs[:n_i], refs[n_i : n_i + n_t]
    refs = refs[n_i + n_t :]
    acc = loss = None
    if state:
        acc, loss = refs[0][...], refs[1][...]
        refs = refs[2:]
    w_out, outs = refs[0], refs[1:]
    a = jnp.concatenate([r[...] for r in images], axis=0) if n_i > 1 else images[0][...]
    rows, width = a.shape
    block = texts[0].shape[0]
    scale, bias = scal[0], scal[1]
    for k in range(n_t):
        t = texts[k][...]
        logits = lax.dot_general(a, t, NT, preferred_element_type=F32)
        flip = None
        if diag and k == 0:
            r = lax.broadcasted_iota(jnp.int32, logits.shape, 0)
            c = lax.broadcasted_iota(jnp.int32, logits.shape, 1)
            flip = jnp.where(r == c, -1.0, 1.0).astype(F32)
        w, lane = pair_terms(logits, scale, bias, flip)
        w_out[:, k * block : (k + 1) * block] = w
        prod = jnp.dot(w, t, preferred_element_type=F32)
        acc = prod if acc is None else acc + prod
        loss = lane if loss is None else loss + lane
    if finish is None:
        outs[0][...] = acc
        outs[1][...] = loss
        return
    line = jnp.sum(jnp.transpose(loss), axis=0, keepdims=True)
    if finish == "own":
        outs[0][...] = acc
        outs[1][...] = jnp.broadcast_to(line, outs[1].shape)
        return
    half = rows // 2
    r = lax.broadcasted_iota(jnp.int32, (PAD, width), 0)
    first = 2 if finish == "far" else 0
    for k, buf in enumerate(outs):
        buf[:half, :] = acc[k * half : (k + 1) * half].astype(BF)
        piece = line[:, k * half : (k + 1) * half]
        hi = piece.astype(BF).astype(F32)
        blank = jnp.zeros((1, width - half), F32)
        hi_row = jnp.concatenate([hi, blank], axis=1)
        lo_row = jnp.concatenate([piece - hi, blank], axis=1)
        buf[half:, :] = jnp.where(r == first, hi_row, jnp.where(r == first + 1, lo_row, 0.0)).astype(BF)


def rows_step(name, scal, images, texts, state=(), diag=False, finish=None, after=()):
    width = images[0].shape[1]
    rows = sum(p.shape[0] for p in images)
    cols = sum(t.shape[0] for t in texts)
    if finish in ("near", "far"):
        grads = [pltpu.VMEM((rows // 2 + PAD, width), BF)] * 2
    else:
        grads = [pltpu.VMEM((rows, width), F32), pltpu.VMEM((8, rows) if finish else (rows, 128), F32)]
    return call(
        functools.partial(rows_kernel, len(images), len(texts), diag, bool(state), finish),
        name,
        [scal, *images, *texts, *state],
        [pltpu.VMEM((rows, cols), BF)] + grads,
        after,
    )


def cols_kernel(n_w, n_i, halves, state, *refs):
    refs = list(refs)
    weights, images = refs[:n_w], refs[n_w : n_w + n_i]
    refs = refs[n_w + n_i :]
    given, outs = (refs[: len(halves)], refs[len(halves) :]) if state else (None, refs)
    block = weights[0].shape[1] // 2
    rows = weights[0].shape[0]
    for k, (h, out) in enumerate(zip(halves, outs, strict=True)):
        acc = given[k][...] if state else None
        at = 0
        for w in weights:
            parts, size = [], 0
            while size < rows:
                parts.append(images[at][...])
                size += images[at].shape[0]
                at += 1
            a = jnp.concatenate(parts, axis=0) if len(parts) > 1 else parts[0]
            prod = lax.dot_general(
                w[:, h * block : (h + 1) * block], a, TN, preferred_element_type=F32
            )
            acc = prod if acc is None else acc + prod
        out[...] = acc.astype(out.dtype)


def cols_step(name, weights, images, dtypes, state=(), after=(), halves=(0, 1)):
    width = images[0].shape[1]
    rows, cols = weights[0].shape
    return call(
        functools.partial(cols_kernel, len(weights), len(images), halves, bool(state)),
        name,
        [*weights, *images, *state],
        [pltpu.VMEM((cols // 2, width), d) for d in dtypes],
        after,
    )


def hold_kernel(*refs):
    n = len(refs) // 2
    for k in range(n):
        refs[n + k][...] = refs[k][...]


def hold(name, values, after):
    return call(hold_kernel, name, list(values), [pltpu.VMEM(v.shape, v.dtype) for v in values], after, cost=1000)


def add_kernel(a, b, out):
    out[...] = (a[...].astype(F32) + b[...].astype(F32)).astype(BF)


def add(name, a, b):
    return call(add_kernel, name, [a, b], [pltpu.VMEM(a.shape, BF)])[0]


def join_kernel(a, b, near, out):
    rows = a.shape[0]
    out[:rows, :] = (a[...].astype(F32) + b[...].astype(F32)).astype(BF)
    out[rows:, :] = near[...]


def join(name, a, b, near, after):
    out = pltpu.VMEM((2 * a.shape[0], a.shape[1]), BF)
    return call(join_kernel, name, [a, b, near], [out], [after])[0]


def tangent(total, raw):
    wide = raw.astype(F32)
    recip = recip_of(wide)
    unit = wide * recip
    along = jnp.sum(unit * total, axis=1, keepdims=True)
    return ((total - unit * along) * recip).astype(BF)


def image_kernel(count, scal, raw, own, loss, from_next, from_prev, grad_ref, loss_ref):
    half = raw.shape[0] // 2
    size = half + PAD
    lines = []
    for k, (s, r) in enumerate(((from_next, from_prev), (from_prev, from_next))):
        at = slice(k * half, (k + 1) * half)
        total = own[at, :] + s[:half, :].astype(F32) + r[size : size + half, :].astype(F32)
        grad_ref[at, :] = tangent(total * scal[2], raw[at, :])
        tail = s[half:size, :half].astype(F32) + r[size + half :, :half].astype(F32)
        lines.append(jnp.sum(tail, axis=0, keepdims=True))
    line = loss[:1, :] + jnp.concatenate(lines, axis=1)
    loss_ref[...] = line * (1.0 / count)


def text_kernel(scal, raw, own, a_ref, b_ref, grad_ref):
    total = own[...] + a_ref[...].astype(F32) + b_ref[...].astype(F32)
    grad_ref[...] = tangent(total * scal[2], raw[...])


def per_device(total, image_embeds, text_embeds, log_scale, bias):
    def move(value, dz=0, dy=0, dc=0):
        pairs = [
            (z * 4 + y * 2 + c, (z + dz) % 4 * 4 + (y + dy) % 2 * 2 + (c + dc) % 2)
            for z in range(4)
            for y in range(2)
            for c in range(2)
        ]
        return lax.ppermute(value, "loss", pairs)

    rows, width = image_embeds.shape
    scale = jnp.exp(log_scale[0])
    scal = jnp.stack([scale * (1.0 / math.log(2.0)), bias[0] * (1.0 / math.log(2.0)), scale])
    a, b = normalize(image_embeds, 2, "norm_image")
    (txt,) = normalize(text_embeds, 1, "norm_text")
    prev_a, next_b = move(a, dz=1), move(b, dz=-1)
    txt_y, txt_c = move(txt, dy=1), move(txt, dc=1)
    near_t = [txt, txt_c]
    w_own_c, *s_own = rows_step("own_c", scal, [a, b], near_t, diag=True)
    prev_a, next_b = hold("hold_far", [prev_a, next_b], s_own[1:])
    far_a, far_b = move(prev_a, dz=1), move(next_b, dz=-1)
    first, far = [prev_a, next_b], [far_a, far_b]
    w_first_c, *s_first = rows_step("first_c", scal, first, near_t, after=s_own[1:])
    a, b = hold("hold_last", [a, b], [far_a, far_b])
    prev_b, next_a = move(b, dz=1), move(a, dz=-1)
    own, last = [a, b], [prev_b, next_a]
    (txt_y,) = hold("hold_text", [txt_y], s_first[1:])
    far_t = [txt_y, move(txt_y, dc=1)]
    w_far_c, *s_far = rows_step("far_c", scal, far, near_t, after=s_first[1:])
    w_far_y, g_far_a, g_far_b = rows_step("far_y", scal, far, far_t, s_far, finish="far")
    w_first_y, g_prev_a, g_next_b = rows_step(
        "first_y", scal, first, far_t, s_first, finish="near", after=[g_far_a]
    )
    w_own_y, g_own, l_own = rows_step("own_y", scal, own, far_t, s_own, finish="own", after=[g_prev_a])
    g_far_a, g_far_b = hold("hold_back", [g_far_a, g_far_b], [l_own])
    through_a, through_b = move(g_far_a, dz=-1), move(g_far_b, dz=1)
    part = cols_step("cols_y0", [w_own_y, w_first_y, w_far_y], own + first + far, (F32, F32))
    w_last_y, *s_last = rows_step("last_y", scal, last, far_t, after=part[:1])
    gt_y, gt_yc = cols_step("cols_y1", [w_last_y], last, (BF, BF), part)
    through_y = move(gt_yc, dc=1)
    w_last_c, g_prev_b, g_next_a = rows_step(
        "last_c", scal, last, near_t, s_last, finish="near", after=[gt_y]
    )
    sum_y = add("add_y", gt_y, through_y)
    text_y = move(sum_y, dy=1)
    to_prev = join("join_a", g_prev_a, through_a, g_prev_b, sum_y)
    to_next = join("join_b", g_next_b, through_b, g_next_a, sum_y)
    from_next, from_prev = move(to_prev, dz=-1), move(to_next, dz=1)
    weights_c = [w_own_c, w_first_c, w_far_c, w_last_c]
    images = own + first + far + last
    (gt_c,) = cols_step("cols_c", weights_c, images, (BF,), after=[sum_y, to_prev, to_next], halves=(1,))
    text_c = move(gt_c, dc=1)
    (gt_own,) = cols_step("cols_own", weights_c, images, (F32,), after=[gt_c], halves=(0,))

    grad_image, loss = call(
        functools.partial(image_kernel, total),
        "image",
        [scal, image_embeds, g_own, l_own, from_next, from_prev],
        [jax.ShapeDtypeStruct((rows, width), BF), jax.ShapeDtypeStruct((1, rows), F32)],
        cost=1000,
    )
    (grad_text,) = call(
        text_kernel,
        "text",
        [scal, text_embeds, gt_own, text_c, text_y],
        [jax.ShapeDtypeStruct((rows, width), BF)],
        cost=1000,
    )
    return loss.reshape(rows), grad_image, grad_text


def solution(mesh):
    placed = (P(("grp", "loss"), None), P(("grp", "loss"), None), P("grp"), P("grp"))

    def whole(image_embeds, text_embeds, log_scale, bias):
        total = image_embeds.shape[0] // mesh.shape["grp"]
        return jax.shard_map(
            functools.partial(per_device, total),
            mesh=mesh,
            in_specs=placed,
            out_specs=(P(("grp", "loss")), P(("grp", "loss"), None), P(("grp", "loss"), None)),
            check_vma=False,
        )(image_embeds, text_embeds, log_scale, bias)

    return whole
```

```python
import functools
import math

import jax
import jax.numpy as jnp
from jax import lax
from jax.experimental import pallas as pl
from jax.experimental.pallas import tpu as pltpu
from jax.sharding import PartitionSpec as P

BF, F32 = jnp.bfloat16, jnp.float32
SMEM = pl.BlockSpec(memory_space=pltpu.SMEM)
VMEM = pl.BlockSpec(memory_space=pltpu.VMEM)
COST = 2 * 10**10
STEP = 256
CHUNK = 128
PAD = 16
NT = (((1,), (1,)), ((), ()))
TN = (((0,), (0,)), ((), ()))


def call(kernel, name, inputs, outs, after=(), scoped=16, cost=COST):
    count = len(inputs)
    inputs = [*inputs, *after]
    specs = [SMEM if x.ndim == 1 else VMEM for x in inputs]

    def body(*refs):
        kernel(*refs[:count], *refs[len(inputs) :])

    return pl.pallas_call(
        body,
        name=name,
        in_specs=specs,
        out_specs=[VMEM] * len(outs),
        out_shape=outs,
        cost_estimate=pl.CostEstimate(flops=cost, bytes_accessed=0, transcendentals=0),
        compiler_params=pltpu.CompilerParams(vmem_limit_bytes=scoped * 2**20),
    )(*[x if x.ndim == 1 else pltpu.with_memory_space_constraint(x, pltpu.VMEM) for x in inputs])


def recip_of(wide):
    return lax.rsqrt(jnp.sum(wide * wide, axis=1, keepdims=True) + 1e-06)


def normalize_kernel(raw, *outs):
    at = 0
    for out in outs:
        rows = out.shape[0]
        wide = raw[at : at + rows, :].astype(F32)
        out[...] = (wide * recip_of(wide)).astype(BF)
        at += rows


def normalize(raw, count, name, after=()):
    rows, width = raw.shape
    return call(normalize_kernel, name, [raw], [pltpu.VMEM((rows // count, width), BF)] * count, after, cost=1000)


def pair_terms(logits, scale, bias, flip):
    z = logits * scale + bias
    if flip is not None:
        z = z * flip
    e = jnp.exp2(z)
    u = 1.0 + e
    w = e * pl.reciprocal(u, approx=True)
    if flip is not None:
        w = w * flip
    half = logits.shape[1] // 2
    terms = jnp.log1p(e[:, :half] + e[:, half:] * u[:, :half])
    total = terms[:, :128]
    for k in range(1, half // 128):
        total = total + terms[:, k * 128 : (k + 1) * 128]
    return w.astype(BF), total


def loss_rows_of(line, width, first):
    hi = line.astype(BF).astype(F32)
    blank = jnp.zeros((1, width - line.shape[1]), F32)
    hi_row = jnp.concatenate([hi, blank], axis=1)
    lo_row = jnp.concatenate([line - hi, blank], axis=1)
    r = lax.broadcasted_iota(jnp.int32, (PAD, width), 0)
    return jnp.where(r == first, hi_row, jnp.where(r == first + 1, lo_row, 0.0))


def line_of(lanes):
    return jnp.sum(jnp.transpose(lanes), axis=0, keepdims=True)


def rows_kernel(n_i, n_t, diag, state, finish, scal, *refs):
    refs = list(refs)
    images, texts = refs[:n_i], refs[n_i : n_i + n_t]
    refs = refs[n_i + n_t :]
    given = None
    if state:
        given, refs = refs[:2], refs[2:]
    w_out, outs = refs[0], refs[1:]
    width = images[0].shape[1]
    block = texts[0].shape[0]
    scale, bias = scal[0], scal[1]
    at = 0
    for k, image in enumerate(images):
        a = image[...]
        rows = a.shape[0]
        mine = slice(at, at + rows)
        acc = given[0][mine, :] if state else None
        loss = given[1][mine, :] if state else None
        steps = [(j, c) for j in range(n_t) for c in range(0, block, STEP)]

        def text(step, texts=texts):
            j, c = step
            return texts[j][c : c + STEP, :]

        def dot(step, a=a, text=text):
            return lax.dot_general(a, text(step), NT, preferred_element_type=F32)

        logits, ready = dot(steps[0]), None
        for n, (j, c) in enumerate(steps):
            following = dot(steps[n + 1]) if n + 1 < len(steps) else None
            if ready is not None:
                prod = jnp.dot(ready, text(steps[n - 1]), preferred_element_type=F32)
                acc = prod if acc is None else acc + prod
            flip = None
            if diag and j == 0 and at <= c < at + rows:
                r = lax.broadcasted_iota(jnp.int32, logits.shape, 0) + at
                q = lax.broadcasted_iota(jnp.int32, logits.shape, 1) + c
                flip = jnp.where(r == q, -1.0, 1.0).astype(F32)
            ready, lane = pair_terms(logits, scale, bias, flip)
            w_out[mine, j * block + c : j * block + c + STEP] = ready
            loss = lane if loss is None else loss + lane
            logits = following
        acc = acc + jnp.dot(ready, text(steps[-1]), preferred_element_type=F32)
        if finish is None:
            outs[0][mine, :] = acc
            outs[1][mine, :] = loss
        else:
            outs[k][:rows, :] = acc.astype(BF)
            outs[k][rows:, :] = loss_rows_of(line_of(loss), width, 2 if finish == "far" else 0).astype(BF)
        at += rows


def rows_step(name, scal, images, texts, state=(), diag=False, finish=None, after=(), cost=COST):
    width = images[0].shape[1]
    rows = sum(p.shape[0] for p in images)
    cols = sum(t.shape[0] for t in texts)
    if finish:
        grads = [pltpu.VMEM((p.shape[0] + PAD, width), BF) for p in images]
    else:
        grads = [pltpu.VMEM((rows, width), F32), pltpu.VMEM((rows, 128), F32)]
    return call(
        functools.partial(rows_kernel, len(images), len(texts), diag, bool(state), finish),
        name,
        [scal, *images, *texts, *state],
        [pltpu.VMEM((rows, cols), BF)] + grads,
        after,
        cost=cost,
    )


def cols_kernel(n_w, n_i, halves, state, *refs):
    refs = list(refs)
    weights, images = refs[:n_w], refs[n_w : n_w + n_i]
    refs = refs[n_w + n_i :]
    given, outs = (refs[: len(halves)], refs[len(halves) :]) if state else (None, refs)
    block = weights[0].shape[1] // 2
    rows = weights[0].shape[0]
    for k, (h, out) in enumerate(zip(halves, outs, strict=True)):
        acc = given[k][...] if state else None
        at = 0
        for w in weights:
            parts, size = [], 0
            while size < rows:
                parts.append(images[at][...])
                size += images[at].shape[0]
                at += 1
            a = jnp.concatenate(parts, axis=0) if len(parts) > 1 else parts[0]
            prod = lax.dot_general(
                w[:, h * block : (h + 1) * block], a, TN, preferred_element_type=F32
            )
            acc = prod if acc is None else acc + prod
        out[...] = acc.astype(out.dtype)


def cols_step(name, weights, images, dtypes, state=(), after=(), halves=(0, 1)):
    width = images[0].shape[1]
    rows, cols = weights[0].shape
    return call(
        functools.partial(cols_kernel, len(weights), len(images), halves, bool(state)),
        name,
        [*weights, *images, *state],
        [pltpu.VMEM((cols // 2, width), d) for d in dtypes],
        after,
    )


def hold_kernel(*refs):
    count = len(refs) // 2
    for k in range(count):
        refs[count + k][...] = refs[k][...]


def hold(name, values, after):
    return call(hold_kernel, name, list(values), [pltpu.VMEM(v.shape, v.dtype) for v in values], after, cost=1000)


def add_kernel(a, b, out):
    out[...] = (a[...] + b[...].astype(F32)).astype(BF)


def add(name, a, b, after=()):
    return call(add_kernel, name, [a, b], [pltpu.VMEM(a.shape, BF)], after)[0]


def sums_kernel(own, lanes, *refs):
    given, outs = refs[:2], refs[2:]
    half = own.shape[0] // 2
    for k in range(2):
        mine = slice(k * half, (k + 1) * half)
        outs[k][:half, :] = (own[mine, :] + given[k][:half, :].astype(F32)).astype(BF)
        pad = loss_rows_of(line_of(lanes[mine, :]), own.shape[1], 0)
        outs[k][half:, :] = (pad + given[k][half:, :].astype(F32)).astype(BF)


def sums(name, state, given, after):
    return call(sums_kernel, name, [*state, *given], [pltpu.VMEM(g.shape, BF) for g in given], after)


def tangent(total, raw):
    wide = raw.astype(F32)
    recip = recip_of(wide)
    unit = wide * recip
    along = jnp.sum(unit * total, axis=1, keepdims=True)
    return ((total - unit * along) * recip).astype(BF)


def store_rows(rows, value_of, out, buf, sem):
    copies = []
    for at in range(0, rows, CHUNK):
        for r in range(at, at + CHUNK, 32):
            buf[r : r + 32, :] = value_of(r)
        chunk = pl.ds(at, CHUNK)
        copies.append(pltpu.make_async_copy(buf.at[chunk, :], out.at[chunk, :], sem.at[at // CHUNK]))
        copies[-1].start()
    for copy in copies:
        copy.wait()


def image_kernel(count, scal, raw, own, lanes, sum_a, near_a, sum_b, near_b, grad_ref, loss_ref, buf, sem):
    rows = raw.shape[0]
    half = rows // 2
    pairs = ((sum_a, near_a), (sum_b, near_b))
    lines = [
        jnp.sum(s[half:, :half].astype(F32) + r[half:, :half].astype(F32), axis=0, keepdims=True)
        for s, r in pairs
    ]
    loss_ref[...] = (line_of(lanes[...]) + jnp.concatenate(lines, axis=1)) * (1.0 / count)

    def value_of(r):
        s, n = pairs[r // half]
        at = r % half
        total = own[r : r + 32, :] + s[at : at + 32, :].astype(F32) + n[at : at + 32, :].astype(F32)
        return tangent(total * scal[2], raw[r : r + 32, :])

    store_rows(rows, value_of, grad_ref, buf, sem)


def text_kernel(scal, raw, own, a_ref, b_ref, grad_ref, buf, sem):
    def value_of(r):
        at = slice(r, r + 32)
        total = own[at, :] + a_ref[at, :].astype(F32) + b_ref[at, :].astype(F32)
        return tangent(total * scal[2], raw[at, :])

    store_rows(raw.shape[0], value_of, grad_ref, buf, sem)


def final(kernel, name, inputs, shape, more=()):
    return pl.pallas_call(
        kernel,
        name=name,
        in_specs=[SMEM if x.ndim == 1 else VMEM for x in inputs],
        out_specs=[pl.BlockSpec(memory_space=pl.ANY)] + [VMEM] * len(more),
        out_shape=[jax.ShapeDtypeStruct(shape, BF), *more],
        scratch_shapes=[pltpu.VMEM(shape, BF), pltpu.SemaphoreType.DMA((shape[0] // CHUNK,))],
        cost_estimate=pl.CostEstimate(flops=1000, bytes_accessed=0, transcendentals=0),
        compiler_params=pltpu.CompilerParams(vmem_limit_bytes=8 * 2**20),
    )(*[x if x.ndim == 1 else pltpu.with_memory_space_constraint(x, pltpu.VMEM) for x in inputs])


def per_device(total, image_embeds, text_embeds, log_scale, bias):
    def move(value, dz=0, dy=0, dc=0):
        pairs = [
            (z * 4 + y * 2 + c, (z + dz) % 4 * 4 + (y + dy) % 2 * 2 + (c + dc) % 2)
            for z in range(4)
            for y in range(2)
            for c in range(2)
        ]
        return lax.ppermute(value, "loss", pairs)

    rows, width = image_embeds.shape
    scale = jnp.exp(log_scale[0])
    scal = jnp.stack([scale * (1.0 / math.log(2.0)), bias[0] * (1.0 / math.log(2.0)), scale])
    a, b = normalize(image_embeds, 2, "norm_image")
    prev_a, next_b = move(a, dz=1), move(b, dz=-1)
    (txt,) = normalize(text_embeds, 1, "norm_text", after=[a])
    txt_y, txt_c = move(txt, dy=1), move(txt, dc=1)
    a, b = hold("hold_last", [a, b], [txt])
    prev_b, next_a = move(b, dz=1), move(a, dz=-1)
    own, last, near_t = [a, b], [prev_b, next_a], [txt, txt_c]
    w_own_c, *s_own = rows_step("own_c", scal, own, near_t, diag=True, cost=1000)
    prev_a, next_b = hold("hold_far", [prev_a, next_b], s_own[1:])
    far_a, far_b = move(prev_a, dz=1), move(next_b, dz=-1)
    first, far = [prev_a, next_b], [far_a, far_b]
    w_first_c, *s_first = rows_step("first_c", scal, first, near_t)
    (txt_y,) = hold("hold_text", [txt_y], s_first[1:])
    far_t = [txt_y, move(txt_y, dc=1)]
    w_last_c, *s_last = rows_step("last_c", scal, last, near_t, after=[txt_y])
    w_last_y, g_prev_b, g_next_a = rows_step("last_y", scal, last, far_t, s_last, finish="near")
    near_b, near_a = move(g_prev_b, dz=-1), move(g_next_a, dz=1)
    w_own_y, *s_own = rows_step("own_y", scal, own, far_t, s_own, after=[g_prev_b])
    w_first_y, *s_first = rows_step("first_y", scal, first, far_t, s_first, after=s_own[1:])
    part = cols_step("cols_y0", [w_own_y, w_first_y, w_last_y], own + first + last, (F32, F32))
    w_far_y, *s_far = rows_step("far_y", scal, far, far_t, after=part[:1])
    gt_y, gt_yc = cols_step("cols_y1", [w_far_y], far, (F32, BF), part)
    through_y = move(gt_yc, dc=1)
    w_far_c, g_far_a, g_far_b = rows_step(
        "far_c", scal, far, near_t, s_far, finish="far", after=[gt_yc]
    )
    through_a, through_b = move(g_far_a, dz=-1), move(g_far_b, dz=1)
    sum_y = add("add_y", gt_y, through_y, after=[g_far_a])
    text_y = move(sum_y, dy=1)
    weights_c = [w_own_c, w_first_c, w_last_c, w_far_c]
    images = own + first + last + far
    (gt_c,) = cols_step("cols_c", weights_c, images, (BF,), after=[sum_y, near_a, near_b], halves=(1,))
    text_c = move(gt_c, dc=1)
    (gt_own,) = cols_step("cols_own", weights_c, images, (F32,), after=[gt_c], halves=(0,))
    to_prev, to_next = sums("sums", s_first, [through_a, through_b], [gt_own])
    sum_a, sum_b = move(to_prev, dz=-1), move(to_next, dz=1)

    grad_image, loss = final(
        functools.partial(image_kernel, total),
        "image",
        [scal, image_embeds, *s_own, sum_a, near_a, sum_b, near_b],
        (rows, width),
        [jax.ShapeDtypeStruct((1, rows), F32)],
    )
    (grad_text,) = final(
        text_kernel, "text", [scal, text_embeds, gt_own, text_c, text_y], (rows, width)
    )
    return loss.reshape(rows), grad_image, grad_text


def solution(mesh):
    placed = (P(("grp", "loss"), None), P(("grp", "loss"), None), P("grp"), P("grp"))

    def whole(image_embeds, text_embeds, log_scale, bias):
        total = image_embeds.shape[0] // mesh.shape["grp"]
        return jax.shard_map(
            functools.partial(per_device, total),
            mesh=mesh,
            in_specs=placed,
            out_specs=(P(("grp", "loss")), P(("grp", "loss"), None), P(("grp", "loss"), None)),
            check_vma=False,
        )(image_embeds, text_embeds, log_scale, bias)

    return whole
```

```python
import functools
import math

import jax
import jax.numpy as jnp
from jax import lax
from jax.experimental import pallas as pl
from jax.experimental.pallas import tpu as pltpu
from jax.sharding import PartitionSpec as P

BF, F32 = jnp.bfloat16, jnp.float32
SMEM = pl.BlockSpec(memory_space=pltpu.SMEM)
VMEM = pl.BlockSpec(memory_space=pltpu.VMEM)
COST = 2 * 10**10
STEP = 256
CHUNK = 128
PAD = 16
NT = (((1,), (1,)), ((), ()))
TN = (((0,), (0,)), ((), ()))


def call(kernel, name, inputs, outs, after=(), scoped=16, cost=COST):
    count = len(inputs)
    inputs = [*inputs, *after]
    specs = [SMEM if x.ndim == 1 else VMEM for x in inputs]

    def body(*refs):
        kernel(*refs[:count], *refs[len(inputs) :])

    return pl.pallas_call(
        body,
        name=name,
        in_specs=specs,
        out_specs=[VMEM] * len(outs),
        out_shape=outs,
        cost_estimate=pl.CostEstimate(flops=cost, bytes_accessed=0, transcendentals=0),
        compiler_params=pltpu.CompilerParams(vmem_limit_bytes=scoped * 2**20),
    )(*[x if x.ndim == 1 else pltpu.with_memory_space_constraint(x, pltpu.VMEM) for x in inputs])


def recip_of(wide):
    return lax.rsqrt(jnp.sum(wide * wide, axis=1, keepdims=True) + 1e-06)


def normalize_kernel(raw, *outs):
    wide = raw[...].astype(F32)
    unit = (wide * recip_of(wide)).astype(BF)
    at = 0
    for out in outs:
        rows = out.shape[0]
        if rows == unit.shape[0]:
            out[...] = unit
        else:
            out[...] = unit[at : at + rows]
            at += rows


def normalize(raw, parts, name, after=()):
    rows, width = raw.shape
    return call(normalize_kernel, name, [raw], [pltpu.VMEM((rows // p, width), BF) for p in parts], after)


def prepare_kernel(scal, raw, unit, factor):
    wide = raw[...].astype(F32)
    recip = recip_of(wide)
    unit[...] = wide * recip
    factor[...] = jnp.broadcast_to(recip * scal[2], factor.shape)


def prepare(scal, raw, name, after):
    rows, width = raw.shape
    outs = [pltpu.VMEM((rows, width), F32), pltpu.VMEM((rows, 128), F32)]
    return call(prepare_kernel, name, [scal, raw], outs, after)


def pair_terms(logits, scale, bias, flip):
    z = logits * scale + bias
    if flip is not None:
        z = z * flip
    e = jnp.exp2(z)
    u = 1.0 + e
    w = e * pl.reciprocal(u, approx=True)
    if flip is not None:
        w = w * flip
    half = logits.shape[1] // 2
    terms = jnp.log1p(e[:, :half] + e[:, half:] * u[:, :half])
    total = terms[:, :128]
    for k in range(1, half // 128):
        total = total + terms[:, k * 128 : (k + 1) * 128]
    return w.astype(BF), total


def loss_rows_of(line, width, first):
    hi = line.astype(BF).astype(F32)
    blank = jnp.zeros((1, width - line.shape[1]), F32)
    hi_row = jnp.concatenate([hi, blank], axis=1)
    lo_row = jnp.concatenate([line - hi, blank], axis=1)
    r = lax.broadcasted_iota(jnp.int32, (PAD, width), 0)
    return jnp.where(r == first, hi_row, jnp.where(r == first + 1, lo_row, 0.0))


def line_of(lanes):
    return jnp.sum(jnp.transpose(lanes), axis=0, keepdims=True)


def rows_kernel(n_i, n_t, diag, state, finish, scal, *refs):
    refs = list(refs)
    images, texts = refs[:n_i], refs[n_i : n_i + n_t]
    refs = refs[n_i + n_t :]
    given = None
    if state:
        given, refs = refs[:2], refs[2:]
    w_outs, outs = refs[:n_t], refs[n_t:]
    width = images[0].shape[1]
    scale, bias = scal[0], scal[1]
    at = 0
    for k, image in enumerate(images):
        a = image[...]
        rows = a.shape[0]
        mine = slice(at, at + rows)
        acc = given[0][mine, :] if state else None
        loss = given[1][mine, :] if state else None
        steps = [(j, c) for j in range(n_t) for c in range(0, texts[j].shape[0], STEP)]

        def text(step, texts=texts):
            j, c = step
            return texts[j][c : c + STEP, :]

        def dot(step, a=a, text=text):
            return lax.dot_general(a, text(step), NT, preferred_element_type=F32)

        logits, ready = dot(steps[0]), None
        for n, (j, c) in enumerate(steps):
            following = dot(steps[n + 1]) if n + 1 < len(steps) else None
            if ready is not None:
                prod = jnp.dot(ready, text(steps[n - 1]), preferred_element_type=F32)
                acc = prod if acc is None else acc + prod
            flip = None
            if diag and j == 0 and at <= c < at + rows:
                r = lax.broadcasted_iota(jnp.int32, logits.shape, 0) + at
                q = lax.broadcasted_iota(jnp.int32, logits.shape, 1) + c
                flip = jnp.where(r == q, -1.0, 1.0).astype(F32)
            ready, lane = pair_terms(logits, scale, bias, flip)
            w_outs[j][mine, c : c + STEP] = ready
            loss = lane if loss is None else loss + lane
            logits = following
        acc = acc + jnp.dot(ready, text(steps[-1]), preferred_element_type=F32)
        if finish is None:
            outs[0][mine, :] = acc
            outs[1][mine, :] = loss
        else:
            outs[k][:rows, :] = acc.astype(BF)
            outs[k][rows:, :] = loss_rows_of(line_of(loss), width, 2 if finish == "far" else 0).astype(BF)
        at += rows


def rows_step(name, scal, images, texts, state=(), diag=False, finish=None, after=(), cost=COST):
    width = images[0].shape[1]
    rows = sum(p.shape[0] for p in images)
    if finish:
        grads = [pltpu.VMEM((p.shape[0] + PAD, width), BF) for p in images]
    else:
        grads = [pltpu.VMEM((rows, width), F32), pltpu.VMEM((rows, 128), F32)]
    outs = call(
        functools.partial(rows_kernel, len(images), len(texts), diag, bool(state), finish),
        name,
        [scal, *images, *texts, *state],
        [pltpu.VMEM((rows, t.shape[0]), BF) for t in texts] + grads,
        after,
        cost=cost,
    )
    return outs[: len(texts)], outs[len(texts) :]


def cols_kernel(n_s, n_w, n_i, *refs):
    weights, images, outs = refs[: n_s * n_w], refs[n_s * n_w : n_s * n_w + n_i], refs[n_s * n_w + n_i :]
    rows = weights[0].shape[0]
    acc, at = None, 0
    for k in range(n_s):
        parts, size = [], 0
        while size < rows:
            parts.append(images[at][...])
            size += images[at].shape[0]
            at += 1
        w = [r[...] for r in weights[k * n_w : (k + 1) * n_w]]
        prod = lax.dot_general(
            jnp.concatenate(w, axis=1) if n_w > 1 else w[0],
            jnp.concatenate(parts, axis=0) if len(parts) > 1 else parts[0],
            TN,
            preferred_element_type=F32,
        )
        acc = prod if acc is None else acc + prod
    at = 0
    for out in outs:
        out[...] = acc[at : at + out.shape[0]].astype(out.dtype)
        at += out.shape[0]


def cols_step(name, weights, images, dtypes, after=()):
    width = images[0].shape[1]
    size = sum(w.shape[1] for w in weights[0])
    return call(
        functools.partial(cols_kernel, len(weights), len(weights[0]), len(images)),
        name,
        [w for group in weights for w in group] + list(images),
        [pltpu.VMEM((size // len(dtypes), width), d) for d in dtypes],
        after,
    )


def hold_kernel(*refs):
    count = len(refs) // 2
    for k in range(count):
        refs[count + k][...] = refs[k][...]


def hold(name, values, after):
    return call(hold_kernel, name, list(values), [pltpu.VMEM(v.shape, v.dtype) for v in values], after, cost=1000)


def add_kernel(a, b, out):
    out[...] = (a[...] + b[...].astype(F32)).astype(BF)


def add(name, a, b, after=()):
    return call(add_kernel, name, [a, b], [pltpu.VMEM(a.shape, BF)], after)[0]


def sums_kernel(own, lanes, *refs):
    given, outs = refs[:2], refs[2:]
    half = own.shape[0] // 2
    for k in range(2):
        mine = slice(k * half, (k + 1) * half)
        outs[k][:half, :] = (own[mine, :] + given[k][:half, :].astype(F32)).astype(BF)
        pad = loss_rows_of(line_of(lanes[mine, :]), own.shape[1], 0)
        outs[k][half:, :] = (pad + given[k][half:, :].astype(F32)).astype(BF)


def sums(name, state, given, after):
    return call(sums_kernel, name, [*state, *given], [pltpu.VMEM(g.shape, BF) for g in given], after)


def image_base_kernel(own, lanes, near_a, near_b, base, line):
    half = own.shape[0] // 2
    lines = []
    for k, near in enumerate((near_a, near_b)):
        mine = slice(k * half, (k + 1) * half)
        base[mine, :] = own[mine, :] + near[:half, :].astype(F32)
        lines.append(jnp.sum(near[half:, :half].astype(F32), axis=0, keepdims=True))
    line[...] = jnp.broadcast_to(line_of(lanes[...]) + jnp.concatenate(lines, axis=1), line.shape)


def text_base_kernel(own, more, base):
    base[...] = own[...] + more[...].astype(F32)


def tangent_rows(base, late, unit, factor, out, buf, sem):
    copies, at = [], 0
    for more, size in late:
        for r in range(0, size, CHUNK):
            rows = slice(at, at + CHUNK)
            total = base[rows, :] + more[r : r + CHUNK, :].astype(F32)
            u = unit[rows, :]
            along = jnp.sum(u * total, axis=1, keepdims=True)
            buf[rows, :] = ((total - u * along) * factor[rows, :1]).astype(BF)
            chunk = pl.ds(at, CHUNK)
            copies.append(pltpu.make_async_copy(buf.at[chunk, :], out.at[chunk, :], sem.at[at // CHUNK]))
            copies[-1].start()
            at += CHUNK
    for copy in copies:
        copy.wait()


def image_kernel(count, base, line, unit, factor, sum_a, sum_b, grad_ref, loss_ref, done, buf, sem):
    half = base.shape[0] // 2
    done[...] = jnp.zeros(done.shape, F32)
    lines = [jnp.sum(s[half:, :half].astype(F32), axis=0, keepdims=True) for s in (sum_a, sum_b)]
    loss_ref[...] = (line[:1, :] + jnp.concatenate(lines, axis=1)) * (1.0 / count)
    tangent_rows(base, [(sum_a, half), (sum_b, half)], unit, factor, grad_ref, buf, sem)


def text_kernel(base, unit, factor, late, done, grad_ref, buf, sem):
    tangent_rows(base, [(late, base.shape[0])], unit, factor, grad_ref, buf, sem)


def final(kernel, name, inputs, shape, more):
    return pl.pallas_call(
        kernel,
        name=name,
        in_specs=[VMEM] * len(inputs),
        out_specs=[pl.BlockSpec(memory_space=pl.ANY)] + [VMEM] * len(more),
        out_shape=[jax.ShapeDtypeStruct(shape, BF), *more],
        scratch_shapes=[pltpu.VMEM(shape, BF), pltpu.SemaphoreType.DMA((shape[0] // CHUNK,))],
        cost_estimate=pl.CostEstimate(flops=1000, bytes_accessed=0, transcendentals=0),
        compiler_params=pltpu.CompilerParams(vmem_limit_bytes=8 * 2**20),
    )(*[pltpu.with_memory_space_constraint(x, pltpu.VMEM) for x in inputs])


def per_device(total, image_embeds, text_embeds, log_scale, bias):
    def move(value, dz=0, dy=0, dc=0):
        pairs = [
            (z * 4 + y * 2 + c, (z + dz) % 4 * 4 + (y + dy) % 2 * 2 + (c + dc) % 2)
            for z in range(4)
            for y in range(2)
            for c in range(2)
        ]
        return lax.ppermute(value, "loss", pairs)

    rows, width = image_embeds.shape
    scale = jnp.exp(log_scale[0])
    scal = jnp.stack([scale * (1.0 / math.log(2.0)), bias[0] * (1.0 / math.log(2.0)), scale])
    txt, txt_a, txt_b = normalize(text_embeds, (1, 2, 2), "norm_text")
    y_a = move(txt_a, dy=1)
    txt_c = move(txt, dc=1)
    a, b = normalize(image_embeds, (2, 2), "norm_image", after=[txt_a])
    prev_a, next_b = move(a, dz=1), move(b, dz=-1)
    (txt_b,) = hold("hold_1", [txt_b], [txt_c])
    y_b = move(txt_b, dy=1)
    near_t = [txt, txt_c]
    (own_0, own_c), s_own = rows_step("own_c", scal, [a, b], near_t, diag=True, after=[txt_b])
    (y_a,) = hold("hold_2", [y_a], s_own[1:])
    yc_a = move(y_a, dc=1)
    i_unit, i_factor = prepare(scal, image_embeds, "prep_image", [y_a])
    a, b = hold("hold_3", [a, b], [yc_a, i_factor])
    prev_b, next_a = move(b, dz=1), move(a, dz=-1)
    own, last = [a, b], [prev_b, next_a]
    own_ya, s_own = rows_step("own_ya", scal, own, [y_a, yc_a], s_own, after=[i_factor])
    prev_a, next_b = hold("hold_far", [prev_a, next_b], s_own[1:])
    far_a, far_b = move(prev_a, dz=1), move(next_b, dz=-1)
    first, far = [prev_a, next_b], [far_a, far_b]
    (first_0, first_c), s_first = rows_step("first_c", scal, first, near_t)
    first_ya, s_first = rows_step("first_ya", scal, first, [y_a, yc_a], s_first)
    t_unit, t_factor = prepare(scal, text_embeds, "prep_text", s_first[1:])
    (y_b,) = hold("hold_yb", [y_b], [t_factor])
    yc_b = move(y_b, dc=1)
    (last_0, last_c), s_last = rows_step("last_c", scal, last, near_t, after=[y_b])
    last_y, (g_prev_b, g_next_a) = rows_step(
        "last_y", scal, last, [y_a, yc_a, y_b, yc_b], s_last, finish="near"
    )
    near_b, near_a = move(g_prev_b, dz=-1), move(g_next_a, dz=1)
    own_yb, s_own = rows_step("own_yb", scal, own, [y_b, yc_b], s_own, after=[g_prev_b])
    first_yb, s_first = rows_step("first_yb", scal, first, [y_b, yc_b], s_first, after=s_own[1:])
    far_y, s_far = rows_step("far_y", scal, far, [y_a, yc_a, y_b, yc_b], after=s_first[1:])
    images = own + first + last + far
    weights_y = [
        [u[k] for u, k in ((group, 0), (group, 2), (group, 1), (group, 3))]
        for group in (own_ya + own_yb, first_ya + first_yb, last_y, far_y)
    ]
    gt_y, gt_yc = cols_step("cols_y", weights_y, images, (F32, BF))
    through_y = move(gt_yc, dc=1)
    (far_0, far_c), (g_far_a, g_far_b) = rows_step(
        "far_c", scal, far, near_t, s_far, finish="far", after=[gt_yc]
    )
    through_a, through_b = move(g_far_a, dz=-1), move(g_far_b, dz=1)
    sum_y = add("add_y", gt_y, through_y, after=[g_far_a])
    text_y = move(sum_y, dy=1)
    (gt_c,) = cols_step(
        "cols_c", [[own_c], [first_c], [last_c], [far_c]], images, (BF,), after=[sum_y, near_a, near_b]
    )
    text_c = move(gt_c, dc=1)
    (gt_own,) = cols_step(
        "cols_own", [[own_0], [first_0], [last_0], [far_0]], images, (F32,), after=[gt_c]
    )
    (t_base,) = call(
        text_base_kernel, "text_base", [gt_own, text_c], [pltpu.VMEM((rows, width), F32)], cost=1000
    )
    i_base, line = call(
        image_base_kernel,
        "image_base",
        [*s_own, near_a, near_b],
        [pltpu.VMEM((rows, width), F32), pltpu.VMEM((8, rows), F32)],
        [t_base],
        cost=1000,
    )
    to_prev, to_next = sums("sums", s_first, [through_a, through_b], [i_base])
    sum_a, sum_b = move(to_prev, dz=-1), move(to_next, dz=1)
    grad_image, loss, done = final(
        functools.partial(image_kernel, total),
        "image",
        [i_base, line, i_unit, i_factor, sum_a, sum_b],
        (rows, width),
        [jax.ShapeDtypeStruct((1, rows), F32), pltpu.VMEM((8, 128), F32)],
    )
    (grad_text,) = final(
        text_kernel, "text", [t_base, t_unit, t_factor, text_y, done], (rows, width), []
    )
    return loss.reshape(rows), grad_image, grad_text


def solution(mesh):
    placed = (P(("grp", "loss"), None), P(("grp", "loss"), None), P("grp"), P("grp"))

    def whole(image_embeds, text_embeds, log_scale, bias):
        total = image_embeds.shape[0] // mesh.shape["grp"]
        return jax.shard_map(
            functools.partial(per_device, total),
            mesh=mesh,
            in_specs=placed,
            out_specs=(P(("grp", "loss")), P(("grp", "loss"), None), P(("grp", "loss"), None)),
            check_vma=False,
        )(image_embeds, text_embeds, log_scale, bias)

    return whole
```

```python
import functools
import math

import jax
import jax.numpy as jnp
from jax import lax
from jax.experimental import pallas as pl
from jax.experimental.pallas import tpu as pltpu
from jax.sharding import PartitionSpec as P

BF, F32 = jnp.bfloat16, jnp.float32
SMEM = pl.BlockSpec(memory_space=pltpu.SMEM)
VMEM = pl.BlockSpec(memory_space=pltpu.VMEM)
COST = 2 * 10**10
STEP = 256
CHUNK = 128
PAD = 16
NT = (((1,), (1,)), ((), ()))
TN = (((0,), (0,)), ((), ()))


def call(kernel, name, inputs, outs, after=(), scoped=16, cost=COST, scratch=()):
    count = len(inputs)
    inputs = [*inputs, *after]
    specs = [SMEM if x.ndim == 1 else VMEM for x in inputs]

    def body(*refs):
        kernel(*refs[:count], *refs[len(inputs) :])

    return pl.pallas_call(
        body,
        name=name,
        in_specs=specs,
        out_specs=[VMEM] * len(outs),
        out_shape=outs,
        scratch_shapes=scratch,
        cost_estimate=pl.CostEstimate(flops=cost, bytes_accessed=0, transcendentals=0),
        compiler_params=pltpu.CompilerParams(vmem_limit_bytes=scoped * 2**20),
    )(*[x if x.ndim == 1 else pltpu.with_memory_space_constraint(x, pltpu.VMEM) for x in inputs])


def recip_of(wide):
    return lax.rsqrt(jnp.sum(wide * wide, axis=1, keepdims=True) + 1e-06)


def in_chunks(rows, body):
    lax.fori_loop(0, rows // CHUNK, lambda k, none: body(pl.ds(pl.multiple_of(k * CHUNK, CHUNK), CHUNK)), None)


def normalize_kernel(raw, whole, *halves):
    rows = raw.shape[0]

    def body(at):
        wide = raw[at, :].astype(F32)
        whole[at, :] = (wide * recip_of(wide)).astype(BF)

    in_chunks(rows, body)
    for k, out in enumerate(halves):
        out[...] = whole[k * (rows // 2) : (k + 1) * (rows // 2), :]


def normalize(raw, name, after=()):
    rows, width = raw.shape
    outs = [pltpu.VMEM((rows // p, width), BF) for p in (1, 2, 2)]
    return call(normalize_kernel, name, [raw], outs, after)


def prepare_kernel(scal, raw, unit, factor):
    def body(at):
        wide = raw[at, :].astype(F32)
        recip = recip_of(wide)
        unit[at, :] = wide * recip
        factor[at, :] = jnp.broadcast_to(recip * scal[2], (CHUNK, factor.shape[1]))

    in_chunks(raw.shape[0], body)


def prepare(scal, raw, name, after):
    rows, width = raw.shape
    outs = [pltpu.VMEM((rows, width), F32), pltpu.VMEM((rows, 128), F32)]
    return call(prepare_kernel, name, [scal, raw], outs, after)


def pair_terms(logits, scale, bias, flip):
    z = logits * scale + bias
    if flip is not None:
        z = z * flip
    e = jnp.exp2(z)
    u = 1.0 + e
    w = e * pl.reciprocal(u, approx=True)
    if flip is not None:
        w = w * flip
    half = logits.shape[1] // 2
    terms = jnp.log1p(e[:, :half] + e[:, half:] * u[:, :half])
    total = terms[:, :128]
    for k in range(1, half // 128):
        total = total + terms[:, k * 128 : (k + 1) * 128]
    return w.astype(BF), total


def loss_rows_of(line, width, first):
    hi = line.astype(BF).astype(F32)
    blank = jnp.zeros((1, width - line.shape[1]), F32)
    hi_row = jnp.concatenate([hi, blank], axis=1)
    lo_row = jnp.concatenate([line - hi, blank], axis=1)
    r = lax.broadcasted_iota(jnp.int32, (PAD, width), 0)
    return jnp.where(r == first, hi_row, jnp.where(r == first + 1, lo_row, 0.0))


def line_of(lanes):
    return jnp.sum(jnp.transpose(lanes), axis=0, keepdims=True)


def rows_kernel(n_t, diag, state, finish, scal, images, *refs):
    texts, refs = refs[:n_t], refs[n_t:]
    given, refs = (refs[:2], refs[2:]) if state else (None, refs)
    w_outs, refs = refs[:n_t], refs[n_t:]
    sums, lanes = refs[-2:]
    half = images.shape[0] // 2
    scale, bias = scal[0], scal[1]
    steps = [(j, c) for j in range(n_t) for c in range(0, texts[j].shape[0], STEP)]

    def text(step):
        j, c = step
        return texts[j][c : c + STEP, :]

    def body(k, none):
        at = pl.multiple_of(k * half, half)
        mine = pl.ds(at, half)
        a = images[mine, :]
        acc = given[0][mine, :] if state else None
        loss = given[1][mine, :] if state else None

        def dot(step):
            return lax.dot_general(a, text(step), NT, preferred_element_type=F32)

        logits, ready = dot(steps[0]), None
        for n, (j, c) in enumerate(steps):
            following = dot(steps[n + 1]) if n + 1 < len(steps) else None
            if ready is not None:
                prod = jnp.dot(ready, text(steps[n - 1]), preferred_element_type=F32)
                acc = prod if acc is None else acc + prod
            flip = None
            if diag and j == 0:
                r = lax.broadcasted_iota(jnp.int32, logits.shape, 0) + at
                q = lax.broadcasted_iota(jnp.int32, logits.shape, 1) + c
                flip = jnp.where(r == q, -1.0, 1.0).astype(F32)
            ready, lane = pair_terms(logits, scale, bias, flip)
            w_outs[j][mine, c : c + STEP] = ready
            loss = lane if loss is None else loss + lane
            logits = following
        sums[mine, :] = acc + jnp.dot(ready, text(steps[-1]), preferred_element_type=F32)
        lanes[mine, :] = loss
        return none

    lax.fori_loop(0, 2, body, None)
    if finish:
        for k, out in enumerate(refs[:2]):
            mine = slice(k * half, (k + 1) * half)
            out[:half, :] = sums[mine, :].astype(BF)
            line = line_of(lanes[mine, :])
            out[half:, :] = loss_rows_of(line, sums.shape[1], 2 if finish == "far" else 0).astype(BF)


def rows_step(name, scal, images, texts, state=(), diag=False, finish=None, after=()):
    rows, width = images.shape
    grads = [((rows, width), F32), ((rows, 128), F32)]
    if finish:
        outs, scratch = [((rows // 2 + PAD, width), BF)] * 2, grads
    else:
        outs, scratch = grads, []
    outs = call(
        functools.partial(rows_kernel, len(texts), diag, bool(state), finish),
        name,
        [scal, images, *texts, *state],
        [pltpu.VMEM((rows, t.shape[0]), BF) for t in texts] + [pltpu.VMEM(*g) for g in outs],
        after,
        scratch=[pltpu.VMEM(*g) for g in scratch],
    )
    return outs[: len(texts)], outs[len(texts) :]


def cols_kernel(n_s, n_w, *refs):
    weights, images, outs = refs[: n_s * n_w], refs[n_s * n_w : n_s * (n_w + 1)], refs[n_s * (n_w + 1) :]
    for h in range(n_w):
        acc = None
        for k in range(n_s):
            prod = lax.dot_general(
                weights[k * n_w + h][...], images[k][...], TN, preferred_element_type=F32
            )
            acc = prod if acc is None else acc + prod
        size = acc.shape[0] // len(outs)
        for k, out in enumerate(outs):
            out[h * size : (h + 1) * size, :] = acc[k * size : (k + 1) * size].astype(out.dtype)


def cols_step(name, weights, images, dtypes, after=()):
    width = images[0].shape[1]
    size = sum(w.shape[1] for w in weights[0]) // len(dtypes)
    return call(
        functools.partial(cols_kernel, len(weights), len(weights[0])),
        name,
        [w for group in weights for w in group] + list(images),
        [pltpu.VMEM((size, width), d) for d in dtypes],
        after,
    )


def hold_kernel(*refs):
    count = len(refs) // 2
    for k in range(count):
        refs[count + k][...] = refs[k][...]


def hold(name, values, after):
    return call(hold_kernel, name, list(values), [pltpu.VMEM(v.shape, v.dtype) for v in values], after, cost=1000)


def merge_kernel(a, b, *outs):
    rows = a.shape[0]
    outs[0][:rows, :] = a[...]
    outs[0][rows:, :] = b[...]
    for out, ref in zip(outs[1:], (a, b)):
        out[...] = ref[...]


def merge(name, a, b, after=(), copies=False):
    rows, width = a.shape
    outs = [pltpu.VMEM((2 * rows, width), BF)] + [pltpu.VMEM(a.shape, BF)] * (2 if copies else 0)
    return call(merge_kernel, name, [a, b], outs, after, cost=1000)


def add_kernel(a, b, out):
    out[...] = (a[...] + b[...].astype(F32)).astype(BF)


def add(name, a, b, after=()):
    return call(add_kernel, name, [a, b], [pltpu.VMEM(a.shape, BF)], after)[0]


def sums_kernel(own, lanes, *refs):
    given, outs = refs[:2], refs[2:]
    half = own.shape[0] // 2
    for k in range(2):
        mine = slice(k * half, (k + 1) * half)
        outs[k][:half, :] = (own[mine, :] + given[k][:half, :].astype(F32)).astype(BF)
        pad = loss_rows_of(line_of(lanes[mine, :]), own.shape[1], 0)
        outs[k][half:, :] = (pad + given[k][half:, :].astype(F32)).astype(BF)


def sums(name, state, given, after):
    return call(sums_kernel, name, [*state, *given], [pltpu.VMEM(g.shape, BF) for g in given], after)


def image_base_kernel(own, lanes, near_a, near_b, base, line):
    half = own.shape[0] // 2
    lines = []
    for k, near in enumerate((near_a, near_b)):
        mine = slice(k * half, (k + 1) * half)
        base[mine, :] = own[mine, :] + near[:half, :].astype(F32)
        lines.append(jnp.sum(near[half:, :half].astype(F32), axis=0, keepdims=True))
    line[...] = jnp.broadcast_to(line_of(lanes[...]) + jnp.concatenate(lines, axis=1), line.shape)


def text_base_kernel(own, more, base):
    base[...] = own[...] + more[...].astype(F32)


def tangent_rows(base, late, unit, factor, out, buf, sem):
    half = base.shape[0] // 2
    for k, (more, first) in enumerate(late):

        def body(j, none, k=k, more=more, first=first):
            at = pl.multiple_of(k * half + j * CHUNK, CHUNK)
            rows = pl.ds(at, CHUNK)
            here = pl.ds(pl.multiple_of(first + j * CHUNK, CHUNK), CHUNK)
            total = base[rows, :] + more[here, :].astype(F32)
            u = unit[rows, :]
            along = jnp.sum(u * total, axis=1, keepdims=True)
            buf[rows, :] = ((total - u * along) * factor[rows, :][:, :1]).astype(BF)
            pltpu.make_async_copy(buf.at[rows, :], out.at[rows, :], sem.at[k]).start()
            return none

        lax.fori_loop(0, half // CHUNK, body, None)
    for k in range(2):
        mine = pl.ds(k * half, half)
        pltpu.make_async_copy(buf.at[mine, :], out.at[mine, :], sem.at[k]).wait()


def image_kernel(count, base, line, unit, factor, sum_a, sum_b, grad_ref, loss_ref, done, buf, sem):
    half = base.shape[0] // 2
    done[...] = jnp.zeros(done.shape, F32)
    lines = [jnp.sum(s[half:, :half].astype(F32), axis=0, keepdims=True) for s in (sum_a, sum_b)]
    loss_ref[...] = (line[:1, :] + jnp.concatenate(lines, axis=1)) * (1.0 / count)
    tangent_rows(base, [(sum_a, 0), (sum_b, 0)], unit, factor, grad_ref, buf, sem)


def text_kernel(base, unit, factor, late, done, grad_ref, buf, sem):
    tangent_rows(base, [(late, 0), (late, base.shape[0] // 2)], unit, factor, grad_ref, buf, sem)


def final(kernel, name, inputs, shape, more):
    return pl.pallas_call(
        kernel,
        name=name,
        in_specs=[VMEM] * len(inputs),
        out_specs=[pl.BlockSpec(memory_space=pl.ANY)] + [VMEM] * len(more),
        out_shape=[jax.ShapeDtypeStruct(shape, BF), *more],
        scratch_shapes=[pltpu.VMEM(shape, BF), pltpu.SemaphoreType.DMA((2,))],
        cost_estimate=pl.CostEstimate(flops=1000, bytes_accessed=0, transcendentals=0),
        compiler_params=pltpu.CompilerParams(vmem_limit_bytes=8 * 2**20),
    )(*[pltpu.with_memory_space_constraint(x, pltpu.VMEM) for x in inputs])


def per_device(total, image_embeds, text_embeds, log_scale, bias):
    def move(value, dz=0, dy=0, dc=0):
        pairs = [
            (z * 4 + y * 2 + c, (z + dz) % 4 * 4 + (y + dy) % 2 * 2 + (c + dc) % 2)
            for z in range(4)
            for y in range(2)
            for c in range(2)
        ]
        return lax.ppermute(value, "loss", pairs)

    rows, width = image_embeds.shape
    scale = jnp.exp(log_scale[0])
    scal = jnp.stack([scale * (1.0 / math.log(2.0)), bias[0] * (1.0 / math.log(2.0)), scale])
    txt, txt_a, txt_b = normalize(text_embeds, "norm_text")
    y_a, txt_c = move(txt_a, dy=1), move(txt, dc=1)
    own, a, b = normalize(image_embeds, "norm_image", after=[txt_a])
    prev_a, next_b = move(a, dz=1), move(b, dz=-1)
    a, b = hold("hold_last", [a, b], [txt_c])
    prev_b, next_a = move(b, dz=1), move(a, dz=-1)
    near_t = [txt, txt_c]
    (own_0, own_c), s_own = rows_step("own_c", scal, own, near_t, diag=True, after=[a])
    (y_a,) = hold("hold_ya", [y_a], s_own[1:])
    yc_a = move(y_a, dc=1)
    i_unit, i_factor = prepare(scal, image_embeds, "prep_image", [y_a])
    (txt_b,) = hold("hold_yb", [txt_b], [yc_a, i_factor])
    y_b = move(txt_b, dy=1)
    (far_t_a,) = merge("merge_ya", y_a, yc_a, [txt_b])
    (own_ya,), s_own = rows_step("own_ya", scal, own, [far_t_a], s_own)
    first, prev_a, next_b = merge("merge_first", prev_a, next_b, s_own[1:], copies=True)
    far_a, far_b = move(prev_a, dz=1), move(next_b, dz=-1)
    (first_0, first_c), s_first = rows_step("first_c", scal, first, near_t)
    (first_ya,), s_first = rows_step("first_ya", scal, first, [far_t_a], s_first)
    t_unit, t_factor = prepare(scal, text_embeds, "prep_text", s_first[1:])
    (y_b,) = hold("hold_text", [y_b], [t_factor])
    yc_b = move(y_b, dc=1)
    (last,) = merge("merge_last", prev_b, next_a, [y_b])
    (last_0, last_c), s_last = rows_step("last_c", scal, last, near_t)
    (far_t_b,) = merge("merge_yb", y_b, yc_b, s_last[1:])
    far_t = [far_t_a, far_t_b]
    last_y, (g_prev_b, g_next_a) = rows_step("last_y", scal, last, far_t, s_last, finish="near")
    near_b, near_a = move(g_prev_b, dz=-1), move(g_next_a, dz=1)
    (own_yb,), s_own = rows_step("own_yb", scal, own, [far_t_b], s_own, after=[g_prev_b])
    (first_yb,), s_first = rows_step("first_yb", scal, first, [far_t_b], s_first, after=s_own[1:])
    (far,) = merge("merge_far", far_a, far_b, s_first[1:])
    far_y, s_far = rows_step("far_y", scal, far, far_t)
    images = [own, first, last, far]
    gt_y, gt_yc = cols_step(
        "cols_y", [[own_ya, own_yb], [first_ya, first_yb], last_y, far_y], images, (F32, BF)
    )
    through_y = move(gt_yc, dc=1)
    (far_0, far_c), (g_far_a, g_far_b) = rows_step(
        "far_c", scal, far, near_t, s_far, finish="far", after=[gt_yc]
    )
    through_a, through_b = move(g_far_a, dz=-1), move(g_far_b, dz=1)
    sum_y = add("add_y", gt_y, through_y, after=[g_far_a])
    text_y = move(sum_y, dy=1)
    (gt_c,) = cols_step(
        "cols_c", [[own_c], [first_c], [last_c], [far_c]], images, (BF,), after=[sum_y, near_a, near_b]
    )
    text_c = move(gt_c, dc=1)
    (gt_own,) = cols_step(
        "cols_own", [[own_0], [first_0], [last_0], [far_0]], images, (F32,), after=[gt_c]
    )
    (t_base,) = call(
        text_base_kernel, "text_base", [gt_own, text_c], [pltpu.VMEM((rows, width), F32)], cost=1000
    )
    i_base, line = call(
        image_base_kernel,
        "image_base",
        [*s_own, near_a, near_b],
        [pltpu.VMEM((rows, width), F32), pltpu.VMEM((8, rows), F32)],
        [t_base],
        cost=1000,
    )
    to_prev, to_next = sums("sums", s_first, [through_a, through_b], [i_base])
    sum_a, sum_b = move(to_prev, dz=-1), move(to_next, dz=1)
    grad_image, loss, done = final(
        functools.partial(image_kernel, total),
        "image",
        [i_base, line, i_unit, i_factor, sum_a, sum_b],
        (rows, width),
        [jax.ShapeDtypeStruct((1, rows), F32), pltpu.VMEM((8, 128), F32)],
    )
    (grad_text,) = final(
        text_kernel, "text", [t_base, t_unit, t_factor, text_y, done], (rows, width), []
    )
    return loss.reshape(rows), grad_image, grad_text


def solution(mesh):
    placed = (P(("grp", "loss"), None), P(("grp", "loss"), None), P("grp"), P("grp"))

    def whole(image_embeds, text_embeds, log_scale, bias):
        total = image_embeds.shape[0] // mesh.shape["grp"]
        return jax.shard_map(
            functools.partial(per_device, total),
            mesh=mesh,
            in_specs=placed,
            out_specs=(P(("grp", "loss")), P(("grp", "loss"), None), P(("grp", "loss"), None)),
            check_vma=False,
        )(image_embeds, text_embeds, log_scale, bias)

    return whole
```

```python
import functools
import math

import jax
import jax.numpy as jnp
from jax import lax
from jax.experimental import pallas as pl
from jax.experimental.pallas import tpu as pltpu
from jax.sharding import PartitionSpec as P

BF, F32 = jnp.bfloat16, jnp.float32
SMEM = pl.BlockSpec(memory_space=pltpu.SMEM)
VMEM = pl.BlockSpec(memory_space=pltpu.VMEM)
COST = 2 * 10**10
STEP = 256
CHUNK = 128
PAD = 16
NT = (((1,), (1,)), ((), ()))
TN = (((0,), (0,)), ((), ()))


def call(kernel, name, inputs, outs, after=(), scoped=16, cost=COST, scratch=()):
    count = len(inputs)
    inputs = [*inputs, *after]
    specs = [SMEM if x.ndim == 1 else VMEM for x in inputs]

    def body(*refs):
        kernel(*refs[:count], *refs[len(inputs) :])

    return pl.pallas_call(
        body,
        name=name,
        in_specs=specs,
        out_specs=[VMEM] * len(outs),
        out_shape=outs,
        scratch_shapes=scratch,
        cost_estimate=pl.CostEstimate(flops=cost, bytes_accessed=0, transcendentals=0),
        compiler_params=pltpu.CompilerParams(vmem_limit_bytes=scoped * 2**20),
    )(*[x if x.ndim == 1 else pltpu.with_memory_space_constraint(x, pltpu.VMEM) for x in inputs])


def recip_of(wide):
    return lax.rsqrt(jnp.sum(wide * wide, axis=1, keepdims=True) + 1e-06)


def in_chunks(rows, body):
    lax.fori_loop(0, rows // CHUNK, lambda k, none: body(pl.ds(pl.multiple_of(k * CHUNK, CHUNK), CHUNK)), None)


def normalize_kernel(raw, whole, *halves):
    rows = raw.shape[0]

    def body(at):
        wide = raw[at, :].astype(F32)
        whole[at, :] = (wide * recip_of(wide)).astype(BF)

    in_chunks(rows, body)
    for k, out in enumerate(halves):
        out[...] = whole[k * (rows // 2) : (k + 1) * (rows // 2), :]


def normalize(raw, name, halves, after=()):
    rows, width = raw.shape
    outs = [pltpu.VMEM((rows // p, width), BF) for p in ((1, 2, 2) if halves else (1,))]
    return call(normalize_kernel, name, [raw], outs, after)


def prepare_kernel(scal, raw, unit, factor):
    def body(at):
        wide = raw[at, :].astype(F32)
        recip = recip_of(wide)
        unit[at, :] = wide * recip
        factor[at, :] = jnp.broadcast_to(recip * scal[2], (CHUNK, factor.shape[1]))

    in_chunks(raw.shape[0], body)


def prepare(scal, raw, name, after):
    rows, width = raw.shape
    outs = [pltpu.VMEM((rows, width), F32), pltpu.VMEM((rows, 128), F32)]
    return call(prepare_kernel, name, [scal, raw], outs, after)


def pair_terms(logits, scale, bias, flip):
    z = logits * scale + bias
    if flip is not None:
        z = z * flip
    e = jnp.exp2(z)
    u = 1.0 + e
    w = e * pl.reciprocal(u, approx=True)
    if flip is not None:
        w = w * flip
    half = logits.shape[1] // 2
    terms = jnp.log1p(e[:, :half] + e[:, half:] * u[:, :half])
    total = terms[:, :128]
    for k in range(1, half // 128):
        total = total + terms[:, k * 128 : (k + 1) * 128]
    return w.astype(BF), total


def loss_rows_of(line, width):
    hi = line.astype(BF).astype(F32)
    blank = jnp.zeros((1, width - line.shape[1]), F32)
    hi_row = jnp.concatenate([hi, blank], axis=1)
    lo_row = jnp.concatenate([line - hi, blank], axis=1)
    r = lax.broadcasted_iota(jnp.int32, (PAD, width), 0)
    return jnp.where(r == 0, hi_row, jnp.where(r == 1, lo_row, 0.0)).astype(BF)


def line_of(lanes):
    return jnp.sum(jnp.transpose(lanes), axis=0, keepdims=True)


def rows_kernel(n_t, diag, state, scal, images, *refs):
    texts, refs = refs[:n_t], refs[n_t:]
    given, refs = (refs[:2], refs[2:]) if state else (None, refs)
    w_outs, refs = refs[:n_t], refs[n_t:]
    sums, lanes = refs[-2:]
    half = images.shape[0] // 2
    scale, bias = scal[0], scal[1]
    steps = [(j, c) for j in range(n_t) for c in range(0, texts[j].shape[0], STEP)]

    def text(step):
        j, c = step
        return texts[j][c : c + STEP, :]

    def body(k, none):
        at = pl.multiple_of(k * half, half)
        mine = pl.ds(at, half)
        a = images[mine, :]
        acc = given[0][mine, :] if state else None
        loss = given[1][mine, :] if state else None

        def dot(step):
            return lax.dot_general(a, text(step), NT, preferred_element_type=F32)

        logits, ready = dot(steps[0]), None
        for n, (j, c) in enumerate(steps):
            following = dot(steps[n + 1]) if n + 1 < len(steps) else None
            if ready is not None:
                prod = jnp.dot(ready, text(steps[n - 1]), preferred_element_type=F32)
                acc = prod if acc is None else acc + prod
            flip = None
            if diag and j == 0:
                r = lax.broadcasted_iota(jnp.int32, logits.shape, 0) + at
                q = lax.broadcasted_iota(jnp.int32, logits.shape, 1) + c
                flip = jnp.where(r == q, -1.0, 1.0).astype(F32)
            ready, lane = pair_terms(logits, scale, bias, flip)
            w_outs[j][mine, c : c + STEP] = ready
            loss = lane if loss is None else loss + lane
            logits = following
        sums[mine, :] = acc + jnp.dot(ready, text(steps[-1]), preferred_element_type=F32)
        lanes[mine, :] = loss
        return none

    lax.fori_loop(0, 2, body, None)
    for k, out in enumerate(refs[:-2]):
        rows = out.shape[0] - PAD
        mine = slice(k * rows, (k + 1) * rows)
        out[:rows, :] = sums[mine, :].astype(BF)
        out[rows:, :] = loss_rows_of(line_of(lanes[mine, :]), sums.shape[1])


def rows_step(name, scal, images, texts, state=(), diag=False, finish=0, after=()):
    rows, width = images.shape
    grads = [((rows, width), F32), ((rows, 128), F32)]
    if finish:
        outs, scratch = [((rows // finish + PAD, width), BF)] * finish, grads
    else:
        outs, scratch = grads, []
    outs = call(
        functools.partial(rows_kernel, len(texts), diag, bool(state)),
        name,
        [scal, images, *texts, *state],
        [pltpu.VMEM((rows, t.shape[0]), BF) for t in texts] + [pltpu.VMEM(*g) for g in outs],
        after,
        scratch=[pltpu.VMEM(*g) for g in scratch],
    )
    return outs[: len(texts)], outs[len(texts) :]


def cols_kernel(n_s, n_w, *refs):
    weights, images, outs = refs[: n_s * n_w], refs[n_s * n_w : n_s * (n_w + 1)], refs[n_s * (n_w + 1) :]
    for h in range(n_w):
        acc = None
        for k in range(n_s):
            prod = lax.dot_general(
                weights[k * n_w + h][...], images[k][...], TN, preferred_element_type=F32
            )
            acc = prod if acc is None else acc + prod
        size = acc.shape[0] // len(outs)
        for k, out in enumerate(outs):
            out[h * size : (h + 1) * size, :] = acc[k * size : (k + 1) * size].astype(out.dtype)


def cols_step(name, weights, images, dtypes, after=()):
    width = images[0].shape[1]
    size = sum(w.shape[1] for w in weights[0]) // len(dtypes)
    return call(
        functools.partial(cols_kernel, len(weights), len(weights[0])),
        name,
        [w for group in weights for w in group] + list(images),
        [pltpu.VMEM((size, width), d) for d in dtypes],
        after,
    )


def hold_kernel(*refs):
    count = len(refs) // 2
    for k in range(count):
        refs[count + k][...] = refs[k][...]


def hold(name, values, after):
    return call(hold_kernel, name, list(values), [pltpu.VMEM(v.shape, v.dtype) for v in values], after, cost=1000)


def merge_kernel(a, b, *outs):
    rows = a.shape[0]
    outs[0][:rows, :] = a[...]
    outs[0][rows:, :] = b[...]
    for out, ref in zip(outs[1:], (a, b)):
        out[...] = ref[...]


def merge(name, a, b, after=(), copies=False):
    rows, width = a.shape
    outs = [pltpu.VMEM((2 * rows, width), BF)] + [pltpu.VMEM(a.shape, BF)] * (2 if copies else 0)
    return call(merge_kernel, name, [a, b], outs, after, cost=1000)


def add_kernel(a, b, out):
    out[...] = (a[...] + b[...].astype(F32)).astype(BF)


def add(name, a, b, after=()):
    return call(add_kernel, name, [a, b], [pltpu.VMEM(a.shape, BF)], after)[0]


def image_base_kernel(own, lanes, a_0, a_1, b_0, b_1, base, line):
    half = own.shape[0] // 2
    lines = []
    for k, (p, q) in enumerate(((a_0, a_1), (b_0, b_1))):
        mine = slice(k * half, (k + 1) * half)
        base[mine, :] = own[mine, :] + p[:half, :].astype(F32) + q[:half, :].astype(F32)
        tail = p[half:, :half].astype(F32) + q[half:, :half].astype(F32)
        lines.append(jnp.sum(tail, axis=0, keepdims=True))
    line[...] = jnp.broadcast_to(line_of(lanes[...]) + jnp.concatenate(lines, axis=1), line.shape)


def text_base_kernel(own, more, base):
    base[...] = own[...] + more[...].astype(F32)


def tangent_rows(base, late, unit, factor, out, buf, sem):
    def body(at):
        total = base[at, :] + late[at, :].astype(F32)
        u = unit[at, :]
        along = jnp.sum(u * total, axis=1, keepdims=True)
        buf[at, :] = ((total - u * along) * factor[at, :][:, :1]).astype(BF)
        pltpu.make_async_copy(buf.at[at, :], out.at[at, :], sem).start()

    in_chunks(base.shape[0], body)
    pltpu.make_async_copy(buf, out, sem).wait()


def image_kernel(count, base, line, unit, factor, late, done, grad_ref, loss_ref, buf, sem):
    rows = base.shape[0]
    tail = jnp.sum(late[rows:, :rows].astype(F32), axis=0, keepdims=True)
    loss_ref[...] = (line[:1, :] + tail) * (1.0 / count)
    tangent_rows(base, late, unit, factor, grad_ref, buf, sem)


def text_kernel(base, unit, factor, late, grad_ref, done, buf, sem):
    done[...] = jnp.zeros(done.shape, F32)
    tangent_rows(base, late, unit, factor, grad_ref, buf, sem)


def final(kernel, name, inputs, shape, more):
    return pl.pallas_call(
        kernel,
        name=name,
        in_specs=[VMEM] * len(inputs),
        out_specs=[pl.BlockSpec(memory_space=pl.ANY)] + [VMEM] * len(more),
        out_shape=[jax.ShapeDtypeStruct(shape, BF), *more],
        scratch_shapes=[pltpu.VMEM(shape, BF), pltpu.SemaphoreType.DMA(())],
        cost_estimate=pl.CostEstimate(flops=1000, bytes_accessed=0, transcendentals=0),
        compiler_params=pltpu.CompilerParams(vmem_limit_bytes=8 * 2**20),
    )(*[pltpu.with_memory_space_constraint(x, pltpu.VMEM) for x in inputs])


def per_device(total, image_embeds, text_embeds, log_scale, bias):
    def move(value, dz=0, dy=0, dc=0):
        pairs = [
            (z * 4 + y * 2 + c, (z + dz) % 4 * 4 + (y + dy) % 2 * 2 + (c + dc) % 2)
            for z in range(4)
            for y in range(2)
            for c in range(2)
        ]
        return lax.ppermute(value, "loss", pairs)

    rows, width = image_embeds.shape
    scale = jnp.exp(log_scale[0])
    scal = jnp.stack([scale * (1.0 / math.log(2.0)), bias[0] * (1.0 / math.log(2.0)), scale])
    (txt,) = normalize(text_embeds, "norm_text", False)
    txt_y, txt_c = move(txt, dy=1), move(txt, dc=1)
    own, a, b = normalize(image_embeds, "norm_image", True, after=[txt])
    prev_a, next_b = move(a, dz=1), move(b, dz=-1)
    a, b = hold("hold_last", [a, b], [txt_c])
    prev_b, next_a = move(b, dz=1), move(a, dz=-1)
    near_t = [txt, txt_c]
    (own_0, own_c), s_own = rows_step("own_c", scal, own, near_t, diag=True, after=[a])
    first, prev_a, next_b = merge("merge_first", prev_a, next_b, s_own[1:], copies=True)
    far_a, far_b = move(prev_a, dz=1), move(next_b, dz=-1)
    (first_0, first_c), s_first = rows_step("first_c", scal, first, near_t)
    i_unit, i_factor = prepare(scal, image_embeds, "prep_image", s_first[1:])
    (txt_y,) = hold("hold_text", [txt_y], [i_factor])
    far_t = [txt_y, move(txt_y, dc=1)]
    t_unit, t_factor = prepare(scal, text_embeds, "prep_text", [txt_y])
    (own_y, own_yc), s_own = rows_step("own_y", scal, own, far_t, s_own, after=[t_factor])
    (first_y, first_yc), (g_prev_a, g_next_b) = rows_step(
        "first_y", scal, first, far_t, s_first, finish=2, after=s_own[1:]
    )
    home_a0, home_b0 = move(g_prev_a, dz=-1), move(g_next_b, dz=1)
    (last,) = merge("merge_last", prev_b, next_a, [g_prev_a])
    (last_0, last_c), s_last = rows_step("last_c", scal, last, near_t)
    (last_y, last_yc), (g_prev_b, g_next_a) = rows_step("last_y", scal, last, far_t, s_last, finish=2)
    home_b1, home_a1 = move(g_prev_b, dz=-1), move(g_next_a, dz=1)
    (far,) = merge("merge_far", far_a, far_b, [g_prev_b])
    (far_y, far_yc), s_far = rows_step("far_y", scal, far, far_t)
    images = [own, first, last, far]
    (gt_yc,) = cols_step("cols_yc", [[own_yc], [first_yc], [last_yc], [far_yc]], images, (BF,))
    through_y = move(gt_yc, dc=1)
    (gt_y,) = cols_step("cols_y", [[own_y], [first_y], [last_y], [far_y]], images, (F32,), after=[gt_yc])
    (far_0, far_c), (g_far,) = rows_step("far_c", scal, far, near_t, s_far, finish=1, after=[gt_y])
    sum_y = add("add_y", gt_y, through_y, after=[g_far, home_a0, home_b0])
    text_y = move(sum_y, dy=1)
    home_far = move(g_far, dz=2)
    (gt_c,) = cols_step("cols_c", [[own_c], [first_c], [last_c], [far_c]], images, (BF,), after=[sum_y])
    text_c = move(gt_c, dc=1)
    (gt_own,) = cols_step(
        "cols_own", [[own_0], [first_0], [last_0], [far_0]], images, (F32,), after=[gt_c]
    )
    i_base, line = call(
        image_base_kernel,
        "image_base",
        [*s_own, home_a0, home_a1, home_b0, home_b1],
        [pltpu.VMEM((rows, width), F32), pltpu.VMEM((8, rows), F32)],
        [gt_own],
        cost=1000,
    )
    (t_base,) = call(
        text_base_kernel, "text_base", [gt_own, text_c], [pltpu.VMEM((rows, width), F32)], [line], cost=1000
    )
    grad_text, done = final(
        text_kernel, "text", [t_base, t_unit, t_factor, text_y], (rows, width), [pltpu.VMEM((8, 128), F32)]
    )
    grad_image, loss = final(
        functools.partial(image_kernel, total),
        "image",
        [i_base, line, i_unit, i_factor, home_far, done],
        (rows, width),
        [jax.ShapeDtypeStruct((1, rows), F32)],
    )
    return loss.reshape(rows), grad_image, grad_text


def solution(mesh):
    placed = (P(("grp", "loss"), None), P(("grp", "loss"), None), P("grp"), P("grp"))

    def whole(image_embeds, text_embeds, log_scale, bias):
        total = image_embeds.shape[0] // mesh.shape["grp"]
        return jax.shard_map(
            functools.partial(per_device, total),
            mesh=mesh,
            in_specs=placed,
            out_specs=(P(("grp", "loss")), P(("grp", "loss"), None), P(("grp", "loss"), None)),
            check_vma=False,
        )(image_embeds, text_embeds, log_scale, bias)

    return whole
```

```python
import functools
import math

import jax
import jax.numpy as jnp
from jax import lax
from jax.experimental import pallas as pl
from jax.experimental.pallas import tpu as pltpu
from jax.sharding import PartitionSpec as P

BF, F32 = jnp.bfloat16, jnp.float32
SMEM = pl.BlockSpec(memory_space=pltpu.SMEM)
VMEM = pl.BlockSpec(memory_space=pltpu.VMEM)
COST = 2 * 10**10
STEP = 256
CHUNK = 128
PAD = 16
NT = (((1,), (1,)), ((), ()))
TN = (((0,), (0,)), ((), ()))


def call(kernel, name, inputs, outs, after=(), scoped=16, cost=COST, scratch=()):
    count = len(inputs)
    inputs = [*inputs, *after]
    specs = [SMEM if x.ndim == 1 else VMEM for x in inputs]

    def body(*refs):
        kernel(*refs[:count], *refs[len(inputs) :])

    return pl.pallas_call(
        body,
        name=name,
        in_specs=specs,
        out_specs=[VMEM] * len(outs),
        out_shape=outs,
        scratch_shapes=scratch,
        cost_estimate=pl.CostEstimate(flops=cost, bytes_accessed=0, transcendentals=0),
        compiler_params=pltpu.CompilerParams(vmem_limit_bytes=scoped * 2**20),
    )(*[x if x.ndim == 1 else pltpu.with_memory_space_constraint(x, pltpu.VMEM) for x in inputs])


def recip_of(wide):
    return lax.rsqrt(jnp.sum(wide * wide, axis=1, keepdims=True) + 1e-06)


def in_chunks(rows, body):
    lax.fori_loop(0, rows // CHUNK, lambda k, none: body(pl.ds(pl.multiple_of(k * CHUNK, CHUNK), CHUNK)), None)


def normalize_kernel(raw, whole, *halves):
    rows = raw.shape[0]

    def body(at):
        wide = raw[at, :].astype(F32)
        whole[at, :] = (wide * recip_of(wide)).astype(BF)

    in_chunks(rows, body)
    for k, out in enumerate(halves):
        out[...] = whole[k * (rows // 2) : (k + 1) * (rows // 2), :]


def normalize(raw, name, halves, after=()):
    rows, width = raw.shape
    outs = [pltpu.VMEM((rows // p, width), BF) for p in ((1, 2, 2) if halves else (1,))]
    return call(normalize_kernel, name, [raw], outs, after)


def prepare_kernel(scal, raw, unit, factor):
    def body(at):
        wide = raw[at, :].astype(F32)
        recip = recip_of(wide)
        unit[at, :] = wide * recip
        factor[at, :] = jnp.broadcast_to(recip * scal[2], (CHUNK, factor.shape[1]))

    in_chunks(raw.shape[0], body)


def prepare(scal, raw, name, after):
    rows, width = raw.shape
    outs = [pltpu.VMEM((rows, width), F32), pltpu.VMEM((rows, 128), F32)]
    return call(prepare_kernel, name, [scal, raw], outs, after)


def pair_terms(logits, scale, bias, flip):
    z = logits * scale + bias
    if flip is not None:
        z = z * flip
    e = jnp.exp2(z)
    u = 1.0 + e
    w = e * pl.reciprocal(u, approx=True)
    if flip is not None:
        w = w * flip
    half = logits.shape[1] // 2
    terms = jnp.log1p(e[:, :half] + e[:, half:] * u[:, :half])
    total = terms[:, :128]
    for k in range(1, half // 128):
        total = total + terms[:, k * 128 : (k + 1) * 128]
    return w.astype(BF), total


def loss_rows_of(line, width):
    hi = line.astype(BF).astype(F32)
    blank = jnp.zeros((1, width - line.shape[1]), F32)
    hi_row = jnp.concatenate([hi, blank], axis=1)
    lo_row = jnp.concatenate([line - hi, blank], axis=1)
    r = lax.broadcasted_iota(jnp.int32, (PAD, width), 0)
    return jnp.where(r == 0, hi_row, jnp.where(r == 1, lo_row, 0.0)).astype(BF)


def line_of(lanes):
    return jnp.sum(jnp.transpose(lanes), axis=0, keepdims=True)


def rows_kernel(n_t, diag, state, finish, scal, images, *refs):
    texts, refs = refs[:n_t], refs[n_t:]
    given, refs = (refs[:2], refs[2:]) if state else (None, refs)
    w_outs, refs = refs[:n_t], refs[n_t:]
    half = images.shape[0] // 2
    scale, bias = scal[0], scal[1]
    steps = [(j, c) for j in range(n_t) for c in range(0, texts[j].shape[0], STEP)]

    def text(step):
        j, c = step
        return texts[j][c : c + STEP, :]

    def body(k, none):
        at = pl.multiple_of(k * half, half)
        mine = pl.ds(at, half)
        a = images[mine, :]
        acc = given[0][mine, :] if state else None
        loss = given[1][mine, :] if state else None

        def dot(step):
            return lax.dot_general(a, text(step), NT, preferred_element_type=F32)

        logits, ready = dot(steps[0]), None
        for n, (j, c) in enumerate(steps):
            following = dot(steps[n + 1]) if n + 1 < len(steps) else None
            if ready is not None:
                prod = jnp.dot(ready, text(steps[n - 1]), preferred_element_type=F32)
                acc = prod if acc is None else acc + prod
            flip = None
            if diag and j == 0:
                r = lax.broadcasted_iota(jnp.int32, logits.shape, 0) + at
                q = lax.broadcasted_iota(jnp.int32, logits.shape, 1) + c
                flip = jnp.where(r == q, -1.0, 1.0).astype(F32)
            ready, lane = pair_terms(logits, scale, bias, flip)
            w_outs[j][mine, c : c + STEP] = ready
            loss = lane if loss is None else loss + lane
            logits = following
        acc = acc + jnp.dot(ready, text(steps[-1]), preferred_element_type=F32)
        if finish == 2:
            for i, out in enumerate(refs):

                @pl.when(k == i)
                def _(out=out):
                    out[:half, :] = acc.astype(BF)
                    out[half:, :] = loss_rows_of(line_of(loss), acc.shape[1])

        elif finish == 1:
            refs[0][mine, :] = acc.astype(BF)
            refs[1][mine, :] = loss
        else:
            refs[0][mine, :] = acc
            refs[1][mine, :] = loss
        return none

    lax.fori_loop(0, 2, body, None)
    if finish == 1:
        refs[0][2 * half :, :] = loss_rows_of(line_of(refs[1][...]), images.shape[1])


def rows_step(name, scal, images, texts, state=(), diag=False, finish=0, after=()):
    rows, width = images.shape
    grads = [((rows, width), F32), ((rows, 128), F32)]
    if finish:
        outs, scratch = [((rows // finish + PAD, width), BF)] * finish, grads[1:] if finish == 1 else []
    else:
        outs, scratch = grads, []
    outs = call(
        functools.partial(rows_kernel, len(texts), diag, bool(state), finish),
        name,
        [scal, images, *texts, *state],
        [pltpu.VMEM((rows, t.shape[0]), BF) for t in texts] + [pltpu.VMEM(*g) for g in outs],
        after,
        scratch=[pltpu.VMEM(*g) for g in scratch],
    )
    return outs[: len(texts)], outs[len(texts) :]


def cols_kernel(n_s, n_w, *refs):
    weights, images, outs = refs[: n_s * n_w], refs[n_s * n_w : n_s * (n_w + 1)], refs[n_s * (n_w + 1) :]
    for h in range(n_w):
        acc = None
        for k in range(n_s):
            prod = lax.dot_general(
                weights[k * n_w + h][...], images[k][...], TN, preferred_element_type=F32
            )
            acc = prod if acc is None else acc + prod
        size = acc.shape[0] // len(outs)
        for k, out in enumerate(outs):
            out[h * size : (h + 1) * size, :] = acc[k * size : (k + 1) * size].astype(out.dtype)


def cols_step(name, weights, images, dtypes, after=()):
    width = images[0].shape[1]
    size = sum(w.shape[1] for w in weights[0]) // len(dtypes)
    return call(
        functools.partial(cols_kernel, len(weights), len(weights[0])),
        name,
        [w for group in weights for w in group] + list(images),
        [pltpu.VMEM((size, width), d) for d in dtypes],
        after,
    )


def hold_kernel(*refs):
    count = len(refs) // 2
    for k in range(count):
        refs[count + k][...] = refs[k][...]


def hold(name, values, after):
    return call(hold_kernel, name, list(values), [pltpu.VMEM(v.shape, v.dtype) for v in values], after, cost=1000)


def merge_kernel(a, b, *outs):
    rows = a.shape[0]
    outs[0][:rows, :] = a[...]
    outs[0][rows:, :] = b[...]
    for out, ref in zip(outs[1:], (a, b)):
        out[...] = ref[...]


def merge(name, a, b, after=(), copies=False):
    rows, width = a.shape
    outs = [pltpu.VMEM((2 * rows, width), BF)] + [pltpu.VMEM(a.shape, BF)] * (2 if copies else 0)
    return call(merge_kernel, name, [a, b], outs, after, cost=1000)


def add_kernel(a, b, out):
    out[...] = (a[...] + b[...].astype(F32)).astype(BF)


def add(name, a, b, after=()):
    return call(add_kernel, name, [a, b], [pltpu.VMEM(a.shape, BF)], after)[0]


def image_base_kernel(own, lanes, a_0, a_1, b_0, b_1, base, line):
    half = own.shape[0] // 2
    lines = []
    for k, (p, q) in enumerate(((a_0, a_1), (b_0, b_1))):
        mine = slice(k * half, (k + 1) * half)
        base[mine, :] = own[mine, :] + p[:half, :].astype(F32) + q[:half, :].astype(F32)
        tail = p[half:, :half].astype(F32) + q[half:, :half].astype(F32)
        lines.append(jnp.sum(tail, axis=0, keepdims=True))
    line[...] = jnp.broadcast_to(line_of(lanes[...]) + jnp.concatenate(lines, axis=1), line.shape)


def text_base_kernel(own, more, base):
    base[...] = own[...] + more[...].astype(F32)


def tangent_rows(base, late, unit, factor, out, buf, sem):
    def body(at):
        total = base[at, :] + late[at, :].astype(F32)
        u = unit[at, :]
        along = jnp.sum(u * total, axis=1, keepdims=True)
        buf[at, :] = ((total - u * along) * factor[at, :][:, :1]).astype(BF)
        pltpu.make_async_copy(buf.at[at, :], out.at[at, :], sem).start()

    in_chunks(base.shape[0], body)
    pltpu.make_async_copy(buf, out, sem).wait()


def image_kernel(count, base, line, unit, factor, late, ready, grad_ref, loss_ref, done, buf, sem):
    rows = base.shape[0]
    done[...] = jnp.zeros(done.shape, F32)
    tail = jnp.sum(late[rows:, :rows].astype(F32), axis=0, keepdims=True)
    loss_ref[...] = (line[:1, :] + tail) * (1.0 / count)
    tangent_rows(base, late, unit, factor, grad_ref, buf, sem)


def text_kernel(base, unit, factor, late, done, grad_ref, buf, sem):
    tangent_rows(base, late, unit, factor, grad_ref, buf, sem)


def final(kernel, name, inputs, shape, more):
    return pl.pallas_call(
        kernel,
        name=name,
        in_specs=[VMEM] * len(inputs),
        out_specs=[pl.BlockSpec(memory_space=pl.ANY)] + [VMEM] * len(more),
        out_shape=[jax.ShapeDtypeStruct(shape, BF), *more],
        scratch_shapes=[pltpu.VMEM(shape, BF), pltpu.SemaphoreType.DMA(())],
        cost_estimate=pl.CostEstimate(flops=1000, bytes_accessed=0, transcendentals=0),
        compiler_params=pltpu.CompilerParams(vmem_limit_bytes=8 * 2**20),
    )(*[pltpu.with_memory_space_constraint(x, pltpu.VMEM) for x in inputs])


def per_device(total, image_embeds, text_embeds, log_scale, bias):
    def move(value, dz=0, dy=0, dc=0):
        pairs = [
            (z * 4 + y * 2 + c, (z + dz) % 4 * 4 + (y + dy) % 2 * 2 + (c + dc) % 2)
            for z in range(4)
            for y in range(2)
            for c in range(2)
        ]
        return lax.ppermute(value, "loss", pairs)

    rows, width = image_embeds.shape
    scale = jnp.exp(log_scale[0])
    scal = jnp.stack([scale * (1.0 / math.log(2.0)), bias[0] * (1.0 / math.log(2.0)), scale])
    raw_y, raw_c = move(text_embeds, dy=1), move(text_embeds, dc=1)
    own, a, b = normalize(image_embeds, "norm_image", True)
    prev_a, next_b = move(a, dz=1), move(b, dz=-1)
    (txt,) = normalize(text_embeds, "norm_text", False, after=[a])
    (txt_c,) = normalize(raw_c, "norm_c", False, after=[txt])
    a, b = hold("hold_last", [a, b], [txt_c])
    prev_b, next_a = move(b, dz=1), move(a, dz=-1)
    near_t = [txt, txt_c]
    (own_0, own_c), s_own = rows_step("own_c", scal, own, near_t, diag=True, after=[a])
    first, prev_a, next_b = merge("merge_first", prev_a, next_b, s_own[1:], copies=True)
    far_a, far_b = move(prev_a, dz=1), move(next_b, dz=-1)
    (first_0, first_c), s_first = rows_step("first_c", scal, first, near_t)
    (txt_y,) = normalize(raw_y, "norm_y", False, after=s_first[1:])
    far_t = [txt_y, move(txt_y, dc=1)]
    (last,) = merge("merge_last", prev_b, next_a, [txt_y])
    (last_0, last_c), s_last = rows_step("last_c", scal, last, near_t)
    (own_y, own_yc), s_own = rows_step("own_y", scal, own, far_t, s_own, after=s_last[1:])
    (first_y, first_yc), (g_prev_a, g_next_b) = rows_step(
        "first_y", scal, first, far_t, s_first, finish=2, after=s_own[1:]
    )
    home_a0, home_b0 = move(g_prev_a, dz=-1), move(g_next_b, dz=1)
    (last_y, last_yc), (g_prev_b, g_next_a) = rows_step(
        "last_y", scal, last, far_t, s_last, finish=2, after=[g_prev_a]
    )
    home_b1, home_a1 = move(g_prev_b, dz=-1), move(g_next_a, dz=1)
    (far,) = merge("merge_far", far_a, far_b, [g_prev_b])
    (far_y, far_yc), s_far = rows_step("far_y", scal, far, far_t)
    images = [own, first, last, far]
    (gt_yc,) = cols_step("cols_yc", [[own_yc], [first_yc], [last_yc], [far_yc]], images, (BF,))
    through_y = move(gt_yc, dc=1)
    (gt_y,) = cols_step("cols_y", [[own_y], [first_y], [last_y], [far_y]], images, (F32,), after=[gt_yc])
    (far_0, far_c), (g_far,) = rows_step("far_c", scal, far, near_t, s_far, finish=1, after=[gt_y])
    sum_y = add("add_y", gt_y, through_y, after=[g_far, home_a0, home_b0])
    text_y = move(sum_y, dy=1)
    home_far = move(g_far, dz=2)
    (gt_c,) = cols_step("cols_c", [[own_c], [first_c], [last_c], [far_c]], images, (BF,), after=[sum_y])
    text_c = move(gt_c, dc=1)
    (gt_own,) = cols_step(
        "cols_own", [[own_0], [first_0], [last_0], [far_0]], images, (F32,), after=[gt_c]
    )
    i_base, line = call(
        image_base_kernel,
        "image_base",
        [*s_own, home_a0, home_a1, home_b0, home_b1],
        [pltpu.VMEM((rows, width), F32), pltpu.VMEM((8, rows), F32)],
        [gt_own],
        cost=1000,
    )
    (t_base,) = call(
        text_base_kernel, "text_base", [gt_own, text_c], [pltpu.VMEM((rows, width), F32)], [line], cost=1000
    )
    i_unit, i_factor = prepare(scal, image_embeds, "prep_image", [t_base])
    t_unit, t_factor = prepare(scal, text_embeds, "prep_text", [i_factor])
    grad_image, loss, done = final(
        functools.partial(image_kernel, total),
        "image",
        [i_base, line, i_unit, i_factor, home_far, t_factor],
        (rows, width),
        [jax.ShapeDtypeStruct((1, rows), F32), pltpu.VMEM((8, 128), F32)],
    )
    (grad_text,) = final(text_kernel, "text", [t_base, t_unit, t_factor, text_y, done], (rows, width), [])
    return loss.reshape(rows), grad_image, grad_text


def solution(mesh):
    placed = (P(("grp", "loss"), None), P(("grp", "loss"), None), P("grp"), P("grp"))

    def whole(image_embeds, text_embeds, log_scale, bias):
        total = image_embeds.shape[0] // mesh.shape["grp"]
        return jax.shard_map(
            functools.partial(per_device, total),
            mesh=mesh,
            in_specs=placed,
            out_specs=(P(("grp", "loss")), P(("grp", "loss"), None), P(("grp", "loss"), None)),
            check_vma=False,
        )(image_embeds, text_embeds, log_scale, bias)

    return whole
```

```python
import functools
import math

import jax
import jax.numpy as jnp
from jax import lax
from jax.experimental import pallas as pl
from jax.experimental.pallas import tpu as pltpu
from jax.sharding import PartitionSpec as P

BF, F32 = jnp.bfloat16, jnp.float32
SMEM = pl.BlockSpec(memory_space=pltpu.SMEM)
VMEM = pl.BlockSpec(memory_space=pltpu.VMEM)
COST = 2 * 10**10
STEP = 256
CHUNK = 128
PAD = 16
NT = (((1,), (1,)), ((), ()))
TN = (((0,), (0,)), ((), ()))


def call(kernel, name, inputs, outs, after=(), scoped=16, cost=COST, scratch=()):
    count = len(inputs)
    inputs = [*inputs, *after]
    specs = [SMEM if x.ndim == 1 else VMEM for x in inputs]

    def body(*refs):
        kernel(*refs[:count], *refs[len(inputs) :])

    return pl.pallas_call(
        body,
        name=name,
        in_specs=specs,
        out_specs=[VMEM] * len(outs),
        out_shape=outs,
        scratch_shapes=scratch,
        cost_estimate=pl.CostEstimate(flops=cost, bytes_accessed=0, transcendentals=0),
        compiler_params=pltpu.CompilerParams(vmem_limit_bytes=scoped * 2**20),
    )(*[x if x.ndim == 1 else pltpu.with_memory_space_constraint(x, pltpu.VMEM) for x in inputs])


def recip_of(wide):
    return lax.rsqrt(jnp.sum(wide * wide, axis=1, keepdims=True) + 1e-06)


def in_chunks(rows, body):
    lax.fori_loop(0, rows // CHUNK, lambda k, none: body(pl.ds(pl.multiple_of(k * CHUNK, CHUNK), CHUNK)), None)


def normalize_kernel(raw, whole, *halves):
    rows = raw.shape[0]

    def body(at):
        wide = raw[at, :].astype(F32)
        whole[at, :] = (wide * recip_of(wide)).astype(BF)

    in_chunks(rows, body)
    for k, out in enumerate(halves):
        out[...] = whole[k * (rows // 2) : (k + 1) * (rows // 2), :]


def normalize(raw, name, halves, after=()):
    rows, width = raw.shape
    outs = [pltpu.VMEM((rows // p, width), BF) for p in ((1, 2, 2) if halves else (1,))]
    return call(normalize_kernel, name, [raw], outs, after)


def prepare_kernel(scal, raw, unit, factor):
    def body(at):
        wide = raw[at, :].astype(F32)
        recip = recip_of(wide)
        unit[at, :] = wide * recip
        factor[at, :] = jnp.broadcast_to(recip * scal[2], (CHUNK, factor.shape[1]))

    in_chunks(raw.shape[0], body)


def prepare(scal, raw, name, after):
    rows, width = raw.shape
    outs = [pltpu.VMEM((rows, width), F32), pltpu.VMEM((rows, 128), F32)]
    return call(prepare_kernel, name, [scal, raw], outs, after)


def pair_terms(logits, scale, bias, flip):
    z = logits * scale + bias
    if flip is not None:
        z = z * flip
    e = jnp.exp2(z)
    u = 1.0 + e
    w = e * pl.reciprocal(u, approx=True)
    if flip is not None:
        w = w * flip
    half = logits.shape[1] // 2
    terms = jnp.log1p(e[:, :half] + e[:, half:] * u[:, :half])
    total = terms[:, :128]
    for k in range(1, half // 128):
        total = total + terms[:, k * 128 : (k + 1) * 128]
    return w.astype(BF), total


def loss_rows_of(line, width):
    hi = line.astype(BF).astype(F32)
    blank = jnp.zeros((1, width - line.shape[1]), F32)
    hi_row = jnp.concatenate([hi, blank], axis=1)
    lo_row = jnp.concatenate([line - hi, blank], axis=1)
    r = lax.broadcasted_iota(jnp.int32, (PAD, width), 0)
    return jnp.where(r == 0, hi_row, jnp.where(r == 1, lo_row, 0.0)).astype(BF)


def line_of(lanes):
    return jnp.sum(jnp.transpose(lanes), axis=0, keepdims=True)


def rows_kernel(n_t, diag, state, scal, images, *refs):
    texts, refs = refs[:n_t], refs[n_t:]
    given, refs = (refs[:2], refs[2:]) if state else (None, refs)
    w_outs, refs = refs[:n_t], refs[n_t:]
    sums, lanes = refs[-2:]
    half = images.shape[0] // 2
    scale, bias = scal[0], scal[1]
    steps = [(j, c) for j in range(n_t) for c in range(0, texts[j].shape[0], STEP)]

    def text(step):
        j, c = step
        return texts[j][c : c + STEP, :]

    def body(k, none):
        at = pl.multiple_of(k * half, half)
        mine = pl.ds(at, half)
        a = images[mine, :]
        acc = given[0][mine, :] if state else None
        loss = given[1][mine, :] if state else None

        def dot(step):
            return lax.dot_general(a, text(step), NT, preferred_element_type=F32)

        logits, ready = dot(steps[0]), None
        for n, (j, c) in enumerate(steps):
            following = dot(steps[n + 1]) if n + 1 < len(steps) else None
            if ready is not None:
                prod = jnp.dot(ready, text(steps[n - 1]), preferred_element_type=F32)
                acc = prod if acc is None else acc + prod
            flip = None
            if diag and j == 0:
                r = lax.broadcasted_iota(jnp.int32, logits.shape, 0) + at
                q = lax.broadcasted_iota(jnp.int32, logits.shape, 1) + c
                flip = jnp.where(r == q, -1.0, 1.0).astype(F32)
            ready, lane = pair_terms(logits, scale, bias, flip)
            w_outs[j][mine, c : c + STEP] = ready
            loss = lane if loss is None else loss + lane
            logits = following
        sums[mine, :] = acc + jnp.dot(ready, text(steps[-1]), preferred_element_type=F32)
        lanes[mine, :] = loss
        return none

    lax.fori_loop(0, 2, body, None)
    for k, out in enumerate(refs[:-2]):
        rows = out.shape[0] - PAD
        mine = slice(k * rows, (k + 1) * rows)
        out[:rows, :] = sums[mine, :].astype(BF)
        out[rows:, :] = loss_rows_of(line_of(lanes[mine, :]), sums.shape[1])


def rows_step(name, scal, images, texts, state=(), diag=False, finish=0, after=()):
    rows, width = images.shape
    grads = [((rows, width), F32), ((rows, 128), F32)]
    if finish:
        outs, scratch = [((rows // finish + PAD, width), BF)] * finish, grads
    else:
        outs, scratch = grads, []
    outs = call(
        functools.partial(rows_kernel, len(texts), diag, bool(state)),
        name,
        [scal, images, *texts, *state],
        [pltpu.VMEM((rows, t.shape[0]), BF) for t in texts] + [pltpu.VMEM(*g) for g in outs],
        after,
        scratch=[pltpu.VMEM(*g) for g in scratch],
    )
    return outs[: len(texts)], outs[len(texts) :]


def cols_kernel(n_s, n_w, *refs):
    weights, images, outs = refs[: n_s * n_w], refs[n_s * n_w : n_s * (n_w + 1)], refs[n_s * (n_w + 1) :]
    for h in range(n_w):
        acc = None
        for k in range(n_s):
            prod = lax.dot_general(
                weights[k * n_w + h][...], images[k][...], TN, preferred_element_type=F32
            )
            acc = prod if acc is None else acc + prod
        size = acc.shape[0] // len(outs)
        for k, out in enumerate(outs):
            out[h * size : (h + 1) * size, :] = acc[k * size : (k + 1) * size].astype(out.dtype)


def cols_step(name, weights, images, dtypes, after=()):
    width = images[0].shape[1]
    size = sum(w.shape[1] for w in weights[0]) // len(dtypes)
    return call(
        functools.partial(cols_kernel, len(weights), len(weights[0])),
        name,
        [w for group in weights for w in group] + list(images),
        [pltpu.VMEM((size, width), d) for d in dtypes],
        after,
    )


def hold_kernel(*refs):
    count = len(refs) // 2
    for k in range(count):
        refs[count + k][...] = refs[k][...]


def hold(name, values, after):
    return call(hold_kernel, name, list(values), [pltpu.VMEM(v.shape, v.dtype) for v in values], after, cost=1000)


def merge_kernel(a, b, *outs):
    rows = a.shape[0]
    outs[0][:rows, :] = a[...]
    outs[0][rows:, :] = b[...]
    for out, ref in zip(outs[1:], (a, b)):
        out[...] = ref[...]


def merge(name, a, b, after=(), copies=False):
    rows, width = a.shape
    outs = [pltpu.VMEM((2 * rows, width), BF)] + [pltpu.VMEM(a.shape, BF)] * (2 if copies else 0)
    return call(merge_kernel, name, [a, b], outs, after, cost=1000)


def add_kernel(a, b, out):
    out[...] = (a[...] + b[...].astype(F32)).astype(BF)


def add(name, a, b, after=()):
    return call(add_kernel, name, [a, b], [pltpu.VMEM(a.shape, BF)], after)[0]


def image_base_kernel(own, lanes, a_0, a_1, b_0, b_1, base, line):
    half = own.shape[0] // 2
    lines = []
    for k, (p, q) in enumerate(((a_0, a_1), (b_0, b_1))):
        mine = slice(k * half, (k + 1) * half)
        base[mine, :] = own[mine, :] + p[:half, :].astype(F32) + q[:half, :].astype(F32)
        tail = p[half:, :half].astype(F32) + q[half:, :half].astype(F32)
        lines.append(jnp.sum(tail, axis=0, keepdims=True))
    line[...] = jnp.broadcast_to(line_of(lanes[...]) + jnp.concatenate(lines, axis=1), line.shape)


def text_base_kernel(own, more, base):
    base[...] = own[...] + more[...].astype(F32)


def tangent_rows(base, late, unit, factor, out, buf, sem):
    def body(at):
        total = base[at, :] + late[at, :].astype(F32)
        u = unit[at, :]
        along = jnp.sum(u * total, axis=1, keepdims=True)
        buf[at, :] = ((total - u * along) * factor[at, :][:, :1]).astype(BF)
        pltpu.make_async_copy(buf.at[at, :], out.at[at, :], sem).start()

    in_chunks(base.shape[0], body)
    pltpu.make_async_copy(buf, out, sem).wait()


def image_kernel(count, base, line, unit, factor, late, ready, grad_ref, loss_ref, done, buf, sem):
    rows = base.shape[0]
    done[...] = jnp.zeros(done.shape, F32)
    tail = jnp.sum(late[rows:, :rows].astype(F32), axis=0, keepdims=True)
    loss_ref[...] = (line[:1, :] + tail) * (1.0 / count)
    tangent_rows(base, late, unit, factor, grad_ref, buf, sem)


def text_kernel(base, unit, factor, late, done, grad_ref, buf, sem):
    tangent_rows(base, late, unit, factor, grad_ref, buf, sem)


def final(kernel, name, inputs, shape, more):
    return pl.pallas_call(
        kernel,
        name=name,
        in_specs=[VMEM] * len(inputs),
        out_specs=[pl.BlockSpec(memory_space=pl.ANY)] + [VMEM] * len(more),
        out_shape=[jax.ShapeDtypeStruct(shape, BF), *more],
        scratch_shapes=[pltpu.VMEM(shape, BF), pltpu.SemaphoreType.DMA(())],
        cost_estimate=pl.CostEstimate(flops=1000, bytes_accessed=0, transcendentals=0),
        compiler_params=pltpu.CompilerParams(vmem_limit_bytes=8 * 2**20),
    )(*[pltpu.with_memory_space_constraint(x, pltpu.VMEM) for x in inputs])


def per_device(total, image_embeds, text_embeds, log_scale, bias):
    def move(value, dz=0, dy=0, dc=0):
        pairs = [
            (z * 4 + y * 2 + c, (z + dz) % 4 * 4 + (y + dy) % 2 * 2 + (c + dc) % 2)
            for z in range(4)
            for y in range(2)
            for c in range(2)
        ]
        return lax.ppermute(value, "loss", pairs)

    rows, width = image_embeds.shape
    scale = jnp.exp(log_scale[0])
    scal = jnp.stack([scale * (1.0 / math.log(2.0)), bias[0] * (1.0 / math.log(2.0)), scale])
    (txt,) = normalize(text_embeds, "norm_text", False)
    txt_y, txt_c = move(txt, dy=1), move(txt, dc=1)
    own, a, b = normalize(image_embeds, "norm_image", True, after=[txt])
    prev_a, next_b = move(a, dz=1), move(b, dz=-1)
    a, b = hold("hold_last", [a, b], [txt_c])
    prev_b, next_a = move(b, dz=1), move(a, dz=-1)
    near_t = [txt, txt_c]
    (own_0, own_c), s_own = rows_step("own_c", scal, own, near_t, diag=True, after=[a])
    first, prev_a, next_b = merge("merge_first", prev_a, next_b, s_own[1:], copies=True)
    far_a, far_b = move(prev_a, dz=1), move(next_b, dz=-1)
    (first_0, first_c), s_first = rows_step("first_c", scal, first, near_t)
    i_unit, i_factor = prepare(scal, image_embeds, "prep_image", s_first[1:])
    (txt_y,) = hold("hold_text", [txt_y], [i_factor])
    far_t = [txt_y, move(txt_y, dc=1)]
    t_unit, t_factor = prepare(scal, text_embeds, "prep_text", [txt_y])
    (own_y, own_yc), s_own = rows_step("own_y", scal, own, far_t, s_own, after=[t_factor])
    (first_y, first_yc), (g_prev_a, g_next_b) = rows_step(
        "first_y", scal, first, far_t, s_first, finish=2, after=s_own[1:]
    )
    home_a0, home_b0 = move(g_prev_a, dz=-1), move(g_next_b, dz=1)
    (last,) = merge("merge_last", prev_b, next_a, [g_prev_a])
    (last_0, last_c, last_y, last_yc), (g_prev_b, g_next_a) = rows_step(
        "last", scal, last, near_t + far_t, finish=2
    )
    home_b1, home_a1 = move(g_prev_b, dz=-1), move(g_next_a, dz=1)
    (far,) = merge("merge_far", far_a, far_b, [g_prev_b])
    (far_0, far_c, far_y, far_yc), (g_far,) = rows_step("far", scal, far, near_t + far_t, finish=1)
    home_far = move(g_far, dz=2)
    images = [own, first, last, far]
    (gt_yc,) = cols_step(
        "cols_yc", [[own_yc], [first_yc], [last_yc], [far_yc]], images, (BF,), after=[g_far, home_a0, home_b0]
    )
    through_y = move(gt_yc, dc=1)
    (gt_y,) = cols_step("cols_y", [[own_y], [first_y], [last_y], [far_y]], images, (F32,), after=[gt_yc])
    sum_y = add("add_y", gt_y, through_y)
    text_y = move(sum_y, dy=1)
    (gt_c,) = cols_step("cols_c", [[own_c], [first_c], [last_c], [far_c]], images, (BF,), after=[sum_y])
    text_c = move(gt_c, dc=1)
    (gt_own,) = cols_step(
        "cols_own", [[own_0], [first_0], [last_0], [far_0]], images, (F32,), after=[gt_c]
    )
    i_base, line = call(
        image_base_kernel,
        "image_base",
        [*s_own, home_a0, home_a1, home_b0, home_b1],
        [pltpu.VMEM((rows, width), F32), pltpu.VMEM((8, rows), F32)],
        [gt_own],
        cost=1000,
    )
    (t_base,) = call(
        text_base_kernel, "text_base", [gt_own, text_c], [pltpu.VMEM((rows, width), F32)], [line], cost=1000
    )
    grad_image, loss, done = final(
        functools.partial(image_kernel, total),
        "image",
        [i_base, line, i_unit, i_factor, home_far, t_base],
        (rows, width),
        [jax.ShapeDtypeStruct((1, rows), F32), pltpu.VMEM((8, 128), F32)],
    )
    (grad_text,) = final(text_kernel, "text", [t_base, t_unit, t_factor, text_y, done], (rows, width), [])
    return loss.reshape(rows), grad_image, grad_text


def solution(mesh):
    placed = (P(("grp", "loss"), None), P(("grp", "loss"), None), P("grp"), P("grp"))

    def whole(image_embeds, text_embeds, log_scale, bias):
        total = image_embeds.shape[0] // mesh.shape["grp"]
        return jax.shard_map(
            functools.partial(per_device, total),
            mesh=mesh,
            in_specs=placed,
            out_specs=(P(("grp", "loss")), P(("grp", "loss"), None), P(("grp", "loss"), None)),
            check_vma=False,
        )(image_embeds, text_embeds, log_scale, bias)

    return whole
```

```python
import functools
import math

import jax
import jax.numpy as jnp
from jax import lax
from jax.experimental import pallas as pl
from jax.experimental.pallas import tpu as pltpu
from jax.sharding import PartitionSpec as P

BF, F32 = jnp.bfloat16, jnp.float32
SMEM = pl.BlockSpec(memory_space=pltpu.SMEM)
VMEM = pl.BlockSpec(memory_space=pltpu.VMEM)
COST = 2 * 10**10
STEP = 256
CHUNK = 128
PAD = 16
NT = (((1,), (1,)), ((), ()))
TN = (((0,), (0,)), ((), ()))


def call(kernel, name, inputs, outs, after=(), scoped=16, cost=COST, scratch=()):
    count = len(inputs)
    inputs = [*inputs, *after]
    specs = [SMEM if x.ndim == 1 else VMEM for x in inputs]

    def body(*refs):
        kernel(*refs[:count], *refs[len(inputs) :])

    return pl.pallas_call(
        body,
        name=name,
        in_specs=specs,
        out_specs=[VMEM] * len(outs),
        out_shape=outs,
        scratch_shapes=scratch,
        cost_estimate=pl.CostEstimate(flops=cost, bytes_accessed=0, transcendentals=0),
        compiler_params=pltpu.CompilerParams(vmem_limit_bytes=scoped * 2**20),
    )(*[x if x.ndim == 1 else pltpu.with_memory_space_constraint(x, pltpu.VMEM) for x in inputs])


def recip_of(wide):
    return lax.rsqrt(jnp.sum(wide * wide, axis=1, keepdims=True) + 1e-06)


def in_chunks(rows, body):
    lax.fori_loop(0, rows // CHUNK, lambda k, none: body(pl.ds(pl.multiple_of(k * CHUNK, CHUNK), CHUNK)), None)


def normalize_kernel(raw, whole, *halves):
    rows = raw.shape[0]

    def body(at):
        wide = raw[at, :].astype(F32)
        whole[at, :] = (wide * recip_of(wide)).astype(BF)

    in_chunks(rows, body)
    for k, out in enumerate(halves):
        out[...] = whole[k * (rows // 2) : (k + 1) * (rows // 2), :]


def normalize(raw, name, halves, after=()):
    rows, width = raw.shape
    outs = [pltpu.VMEM((rows // p, width), BF) for p in ((1, 2, 2) if halves else (1,))]
    return call(normalize_kernel, name, [raw], outs, after)


def prepare_kernel(scal, raw, unit, factor):
    def body(at):
        wide = raw[at, :].astype(F32)
        recip = recip_of(wide)
        unit[at, :] = wide * recip
        factor[at, :] = jnp.broadcast_to(recip * scal[2], (CHUNK, factor.shape[1]))

    in_chunks(raw.shape[0], body)


def prepare(scal, raw, name, after):
    rows, width = raw.shape
    outs = [pltpu.VMEM((rows, width), F32), pltpu.VMEM((rows, 128), F32)]
    return call(prepare_kernel, name, [scal, raw], outs, after)


def pair_terms(logits, scale, bias, flip):
    z = logits * scale + bias
    if flip is not None:
        z = z * flip
    e = jnp.exp2(z)
    u = 1.0 + e
    w = e * pl.reciprocal(u, approx=True)
    if flip is not None:
        w = w * flip
    half = logits.shape[1] // 2
    terms = jnp.log1p(e[:, :half] + e[:, half:] * u[:, :half])
    total = terms[:, :128]
    for k in range(1, half // 128):
        total = total + terms[:, k * 128 : (k + 1) * 128]
    return w.astype(BF), total


def loss_rows_of(line, width):
    hi = line.astype(BF).astype(F32)
    blank = jnp.zeros((1, width - line.shape[1]), F32)
    hi_row = jnp.concatenate([hi, blank], axis=1)
    lo_row = jnp.concatenate([line - hi, blank], axis=1)
    r = lax.broadcasted_iota(jnp.int32, (PAD, width), 0)
    return jnp.where(r == 0, hi_row, jnp.where(r == 1, lo_row, 0.0)).astype(BF)


def line_of(lanes):
    return jnp.sum(jnp.transpose(lanes), axis=0, keepdims=True)


def rows_kernel(n_t, diag, state, scal, images, *refs):
    texts, refs = refs[:n_t], refs[n_t:]
    given, refs = (refs[:2], refs[2:]) if state else (None, refs)
    w_outs, refs = refs[:n_t], refs[n_t:]
    sums, lanes = refs[-2:]
    half = images.shape[0] // 2
    scale, bias = scal[0], scal[1]
    steps = [(j, c) for j in range(n_t) for c in range(0, texts[j].shape[0], STEP)]

    def text(step):
        j, c = step
        return texts[j][c : c + STEP, :]

    def body(k, none):
        at = pl.multiple_of(k * half, half)
        mine = pl.ds(at, half)
        a = images[mine, :]
        acc = given[0][mine, :] if state else None
        loss = given[1][mine, :] if state else None

        def dot(step):
            return lax.dot_general(a, text(step), NT, preferred_element_type=F32)

        logits, ready = dot(steps[0]), None
        for n, (j, c) in enumerate(steps):
            following = dot(steps[n + 1]) if n + 1 < len(steps) else None
            if ready is not None:
                prod = jnp.dot(ready, text(steps[n - 1]), preferred_element_type=F32)
                acc = prod if acc is None else acc + prod
            flip = None
            if diag and j == 0:
                r = lax.broadcasted_iota(jnp.int32, logits.shape, 0) + at
                q = lax.broadcasted_iota(jnp.int32, logits.shape, 1) + c
                flip = jnp.where(r == q, -1.0, 1.0).astype(F32)
            ready, lane = pair_terms(logits, scale, bias, flip)
            w_outs[j][mine, c : c + STEP] = ready
            loss = lane if loss is None else loss + lane
            logits = following
        sums[mine, :] = acc + jnp.dot(ready, text(steps[-1]), preferred_element_type=F32)
        lanes[mine, :] = loss
        return none

    lax.fori_loop(0, 2, body, None)
    for k, out in enumerate(refs[:-2]):
        rows = out.shape[0] - PAD
        mine = slice(k * rows, (k + 1) * rows)
        out[:rows, :] = sums[mine, :].astype(BF)
        out[rows:, :] = loss_rows_of(line_of(lanes[mine, :]), sums.shape[1])


def rows_step(name, scal, images, texts, state=(), diag=False, finish=0, after=()):
    rows, width = images.shape
    grads = [((rows, width), F32), ((rows, 128), F32)]
    if finish:
        outs, scratch = [((rows // finish + PAD, width), BF)] * finish, grads
    else:
        outs, scratch = grads, []
    outs = call(
        functools.partial(rows_kernel, len(texts), diag, bool(state)),
        name,
        [scal, images, *texts, *state],
        [pltpu.VMEM((rows, t.shape[0]), BF) for t in texts] + [pltpu.VMEM(*g) for g in outs],
        after,
        scratch=[pltpu.VMEM(*g) for g in scratch],
    )
    return outs[: len(texts)], outs[len(texts) :]


def cols_kernel(n_s, n_w, *refs):
    weights, images, outs = refs[: n_s * n_w], refs[n_s * n_w : n_s * (n_w + 1)], refs[n_s * (n_w + 1) :]
    for h in range(n_w):
        acc = None
        for k in range(n_s):
            prod = lax.dot_general(
                weights[k * n_w + h][...], images[k][...], TN, preferred_element_type=F32
            )
            acc = prod if acc is None else acc + prod
        size = acc.shape[0] // len(outs)
        for k, out in enumerate(outs):
            out[h * size : (h + 1) * size, :] = acc[k * size : (k + 1) * size].astype(out.dtype)


def cols_step(name, weights, images, dtypes, after=()):
    width = images[0].shape[1]
    size = sum(w.shape[1] for w in weights[0]) // len(dtypes)
    return call(
        functools.partial(cols_kernel, len(weights), len(weights[0])),
        name,
        [w for group in weights for w in group] + list(images),
        [pltpu.VMEM((size, width), d) for d in dtypes],
        after,
    )


def hold_kernel(*refs):
    count = len(refs) // 2
    for k in range(count):
        refs[count + k][...] = refs[k][...]


def hold(name, values, after):
    return call(hold_kernel, name, list(values), [pltpu.VMEM(v.shape, v.dtype) for v in values], after, cost=1000)


def merge_kernel(a, b, *outs):
    rows = a.shape[0]
    outs[0][:rows, :] = a[...]
    outs[0][rows:, :] = b[...]
    for out, ref in zip(outs[1:], (a, b)):
        out[...] = ref[...]


def merge(name, a, b, after=(), copies=False):
    rows, width = a.shape
    outs = [pltpu.VMEM((2 * rows, width), BF)] + [pltpu.VMEM(a.shape, BF)] * (2 if copies else 0)
    return call(merge_kernel, name, [a, b], outs, after, cost=1000)


def add_kernel(a, b, out):
    out[...] = (a[...] + b[...].astype(F32)).astype(BF)


def add(name, a, b, after=()):
    return call(add_kernel, name, [a, b], [pltpu.VMEM(a.shape, BF)], after)[0]


def sums_kernel(own, lanes, *refs):
    given, outs = refs[:2], refs[2:]
    half = own.shape[0] // 2
    for k in range(2):
        mine = slice(k * half, (k + 1) * half)
        outs[k][:half, :] = (own[mine, :] + given[k][:half, :].astype(F32)).astype(BF)
        tail = jnp.sum(given[k][half:, :half].astype(F32), axis=0, keepdims=True)
        outs[k][half:, :] = loss_rows_of(line_of(lanes[mine, :]) + tail, own.shape[1])


def sums(name, state, given, after):
    return call(sums_kernel, name, [*state, *given], [pltpu.VMEM(g.shape, BF) for g in given], after)


def image_base_kernel(own, lanes, near_a, near_b, base, line):
    half = own.shape[0] // 2
    lines = []
    for k, near in enumerate((near_a, near_b)):
        mine = slice(k * half, (k + 1) * half)
        base[mine, :] = own[mine, :] + near[:half, :].astype(F32)
        lines.append(jnp.sum(near[half:, :half].astype(F32), axis=0, keepdims=True))
    line[...] = jnp.broadcast_to(line_of(lanes[...]) + jnp.concatenate(lines, axis=1), line.shape)


def text_base_kernel(own, more, base):
    base[...] = own[...] + more[...].astype(F32)


def tangent_rows(base, late, unit, factor, out, buf, sem):
    first, size = 0, base.shape[0] // len(late)
    for more in late:

        def body(at, first=first, more=more):
            rows = pl.ds(pl.multiple_of(at.start + first, CHUNK), CHUNK)
            total = base[rows, :] + more[at, :].astype(F32)
            u = unit[rows, :]
            along = jnp.sum(u * total, axis=1, keepdims=True)
            buf[rows, :] = ((total - u * along) * factor[rows, :][:, :1]).astype(BF)
            pltpu.make_async_copy(buf.at[rows, :], out.at[rows, :], sem).start()

        in_chunks(size, body)
        first += size
    pltpu.make_async_copy(buf, out, sem).wait()


def image_kernel(count, base, line, unit, factor, sum_a, sum_b, ready, grad_ref, loss_ref, done, buf, sem):
    half = base.shape[0] // 2
    done[...] = jnp.zeros(done.shape, F32)
    lines = [jnp.sum(s[half:, :half].astype(F32), axis=0, keepdims=True) for s in (sum_a, sum_b)]
    loss_ref[...] = (line[:1, :] + jnp.concatenate(lines, axis=1)) * (1.0 / count)
    tangent_rows(base, [sum_a, sum_b], unit, factor, grad_ref, buf, sem)


def text_kernel(base, unit, factor, late, done, grad_ref, buf, sem):
    tangent_rows(base, [late], unit, factor, grad_ref, buf, sem)


def final(kernel, name, inputs, shape, more):
    return pl.pallas_call(
        kernel,
        name=name,
        in_specs=[VMEM] * len(inputs),
        out_specs=[pl.BlockSpec(memory_space=pl.ANY)] + [VMEM] * len(more),
        out_shape=[jax.ShapeDtypeStruct(shape, BF), *more],
        scratch_shapes=[pltpu.VMEM(shape, BF), pltpu.SemaphoreType.DMA(())],
        cost_estimate=pl.CostEstimate(flops=1000, bytes_accessed=0, transcendentals=0),
        compiler_params=pltpu.CompilerParams(vmem_limit_bytes=8 * 2**20),
    )(*[pltpu.with_memory_space_constraint(x, pltpu.VMEM) for x in inputs])


def per_device(total, image_embeds, text_embeds, log_scale, bias):
    def move(value, dz=0, dy=0, dc=0):
        pairs = [
            (z * 4 + y * 2 + c, (z + dz) % 4 * 4 + (y + dy) % 2 * 2 + (c + dc) % 2)
            for z in range(4)
            for y in range(2)
            for c in range(2)
        ]
        return lax.ppermute(value, "loss", pairs)

    rows, width = image_embeds.shape
    scale = jnp.exp(log_scale[0])
    scal = jnp.stack([scale * (1.0 / math.log(2.0)), bias[0] * (1.0 / math.log(2.0)), scale])
    (txt,) = normalize(text_embeds, "norm_text", False)
    txt_y, txt_c = move(txt, dy=1), move(txt, dc=1)
    own, a, b = normalize(image_embeds, "norm_image", True, after=[txt])
    prev_a, next_b = move(a, dz=1), move(b, dz=-1)
    a, b = hold("hold_last", [a, b], [txt_c])
    prev_b, next_a = move(b, dz=1), move(a, dz=-1)
    near_t = [txt, txt_c]
    (own_0, own_c), s_own = rows_step("own_c", scal, own, near_t, diag=True, after=[a])
    first, prev_a, next_b = merge("merge_first", prev_a, next_b, s_own[1:], copies=True)
    far_a, far_b = move(prev_a, dz=1), move(next_b, dz=-1)
    (first_0, first_c), s_first = rows_step("first_c", scal, first, near_t)
    i_unit, i_factor = prepare(scal, image_embeds, "prep_image", s_first[1:])
    (txt_y,) = hold("hold_text", [txt_y], [i_factor])
    far_t = [txt_y, move(txt_y, dc=1)]
    t_unit, t_factor = prepare(scal, text_embeds, "prep_text", [txt_y])
    (own_y, own_yc), s_own = rows_step("own_y", scal, own, far_t, s_own, after=[t_factor])
    (last,) = merge("merge_last", prev_b, next_a, s_own[1:])
    (last_0, last_c, last_y, last_yc), (g_prev_b, g_next_a) = rows_step(
        "last", scal, last, near_t + far_t, finish=2
    )
    near_b, near_a = move(g_prev_b, dz=-1), move(g_next_a, dz=1)
    (far,) = merge("merge_far", far_a, far_b, [g_prev_b])
    (far_0, far_c, far_y, far_yc), (g_far_a, g_far_b) = rows_step("far", scal, far, near_t + far_t, finish=2)
    through_a, through_b = move(g_far_a, dz=-1), move(g_far_b, dz=1)
    (first_y, first_yc), s_first = rows_step("first_y", scal, first, far_t, s_first, after=[g_far_a])
    images = [own, first, last, far]
    (gt_yc,) = cols_step("cols_yc", [[own_yc], [first_yc], [last_yc], [far_yc]], images, (BF,))
    through_y = move(gt_yc, dc=1)
    (gt_y,) = cols_step("cols_y", [[own_y], [first_y], [last_y], [far_y]], images, (F32,), after=[gt_yc])
    sum_y = add("add_y", gt_y, through_y)
    text_y = move(sum_y, dy=1)
    (gt_c,) = cols_step(
        "cols_c", [[own_c], [first_c], [last_c], [far_c]], images, (BF,), after=[sum_y, near_a, near_b]
    )
    text_c = move(gt_c, dc=1)
    to_prev, to_next = sums("sums", s_first, [through_a, through_b], [gt_c])
    sum_a, sum_b = move(to_prev, dz=-1), move(to_next, dz=1)
    (gt_own,) = cols_step(
        "cols_own", [[own_0], [first_0], [last_0], [far_0]], images, (F32,), after=[to_prev]
    )
    i_base, line = call(
        image_base_kernel,
        "image_base",
        [*s_own, near_a, near_b],
        [pltpu.VMEM((rows, width), F32), pltpu.VMEM((8, rows), F32)],
        [gt_own],
        cost=1000,
    )
    (t_base,) = call(
        text_base_kernel, "text_base", [gt_own, text_c], [pltpu.VMEM((rows, width), F32)], [line], cost=1000
    )
    grad_image, loss, done = final(
        functools.partial(image_kernel, total),
        "image",
        [i_base, line, i_unit, i_factor, sum_a, sum_b, t_base],
        (rows, width),
        [jax.ShapeDtypeStruct((1, rows), F32), pltpu.VMEM((8, 128), F32)],
    )
    (grad_text,) = final(text_kernel, "text", [t_base, t_unit, t_factor, text_y, done], (rows, width), [])
    return loss.reshape(rows), grad_image, grad_text


def solution(mesh):
    placed = (P(("grp", "loss"), None), P(("grp", "loss"), None), P("grp"), P("grp"))

    def whole(image_embeds, text_embeds, log_scale, bias):
        total = image_embeds.shape[0] // mesh.shape["grp"]
        return jax.shard_map(
            functools.partial(per_device, total),
            mesh=mesh,
            in_specs=placed,
            out_specs=(P(("grp", "loss")), P(("grp", "loss"), None), P(("grp", "loss"), None)),
            check_vma=False,
        )(image_embeds, text_embeds, log_scale, bias)

    return whole
```

```python
import functools
import math

import jax
import jax.numpy as jnp
from jax import lax
from jax.experimental import pallas as pl
from jax.experimental.pallas import tpu as pltpu
from jax.sharding import PartitionSpec as P

BF, F32 = jnp.bfloat16, jnp.float32
SMEM = pl.BlockSpec(memory_space=pltpu.SMEM)
VMEM = pl.BlockSpec(memory_space=pltpu.VMEM)
COST = 2 * 10**10
STEP = 256
CHUNK = 128
PAD = 16
NT = (((1,), (1,)), ((), ()))
TN = (((0,), (0,)), ((), ()))


def call(kernel, name, inputs, outs, after=(), scoped=16, cost=COST, scratch=()):
    count = len(inputs)
    inputs = [*inputs, *after]
    specs = [SMEM if x.ndim == 1 else VMEM for x in inputs]

    def body(*refs):
        kernel(*refs[:count], *refs[len(inputs) :])

    return pl.pallas_call(
        body,
        name=name,
        in_specs=specs,
        out_specs=[VMEM] * len(outs),
        out_shape=outs,
        scratch_shapes=scratch,
        cost_estimate=pl.CostEstimate(flops=cost, bytes_accessed=0, transcendentals=0),
        compiler_params=pltpu.CompilerParams(vmem_limit_bytes=scoped * 2**20),
    )(*[x if x.ndim == 1 else pltpu.with_memory_space_constraint(x, pltpu.VMEM) for x in inputs])


def recip_of(wide):
    return lax.rsqrt(jnp.sum(wide * wide, axis=1, keepdims=True) + 1e-06)


def in_chunks(rows, body):
    lax.fori_loop(0, rows // CHUNK, lambda k, none: body(pl.ds(pl.multiple_of(k * CHUNK, CHUNK), CHUNK)), None)


def normalize_kernel(raw, whole, *halves):
    rows = raw.shape[0]

    def body(at):
        wide = raw[at, :].astype(F32)
        whole[at, :] = (wide * recip_of(wide)).astype(BF)

    in_chunks(rows, body)
    for k, out in enumerate(halves):
        out[...] = whole[k * (rows // 2) : (k + 1) * (rows // 2), :]


def normalize(raw, name, halves, after=()):
    rows, width = raw.shape
    outs = [pltpu.VMEM((rows // p, width), BF) for p in ((1, 2, 2) if halves else (1,))]
    return call(normalize_kernel, name, [raw], outs, after)


def normalize_hbm_kernel(raw, whole, buf, sems):
    chunks = [pl.ds(k * CHUNK, CHUNK) for k in range(raw.shape[0] // CHUNK)]
    copies = [pltpu.make_async_copy(raw.at[at, :], buf.at[at, :], sems.at[k]) for k, at in enumerate(chunks)]
    for copy in copies:
        copy.start()
    for at, copy in zip(chunks, copies, strict=True):
        copy.wait()
        wide = buf[at, :].astype(F32)
        whole[at, :] = (wide * recip_of(wide)).astype(BF)


def normalize_hbm(raw, name):
    rows, width = raw.shape
    return pl.pallas_call(
        normalize_hbm_kernel,
        name=name,
        in_specs=[pl.BlockSpec(memory_space=pl.ANY)],
        out_specs=VMEM,
        out_shape=pltpu.VMEM((rows, width), BF),
        scratch_shapes=[pltpu.VMEM((rows, width), BF), pltpu.SemaphoreType.DMA((rows // CHUNK,))],
        cost_estimate=pl.CostEstimate(flops=COST, bytes_accessed=0, transcendentals=0),
        compiler_params=pltpu.CompilerParams(vmem_limit_bytes=8 * 2**20),
    )(pltpu.with_memory_space_constraint(raw, pltpu.HBM))


def prepare_kernel(scal, raw, unit, factor):
    def body(at):
        wide = raw[at, :].astype(F32)
        recip = recip_of(wide)
        unit[at, :] = wide * recip
        factor[at, :] = jnp.broadcast_to(recip * scal[2], (CHUNK, factor.shape[1]))

    in_chunks(raw.shape[0], body)


def prepare(scal, raw, name, after):
    rows, width = raw.shape
    outs = [pltpu.VMEM((rows, width), F32), pltpu.VMEM((rows, 128), F32)]
    return call(prepare_kernel, name, [scal, raw], outs, after)


def pair_terms(logits, scale, bias, flip):
    z = logits * scale + bias
    if flip is not None:
        z = z * flip
    e = jnp.exp2(z)
    u = 1.0 + e
    w = e * pl.reciprocal(u, approx=True)
    if flip is not None:
        w = w * flip
    half = logits.shape[1] // 2
    terms = jnp.log1p(e[:, :half] + e[:, half:] * u[:, :half])
    total = terms[:, :128]
    for k in range(1, half // 128):
        total = total + terms[:, k * 128 : (k + 1) * 128]
    return w.astype(BF), total


def loss_rows_of(line, width):
    hi = line.astype(BF).astype(F32)
    blank = jnp.zeros((1, width - line.shape[1]), F32)
    hi_row = jnp.concatenate([hi, blank], axis=1)
    lo_row = jnp.concatenate([line - hi, blank], axis=1)
    r = lax.broadcasted_iota(jnp.int32, (PAD, width), 0)
    return jnp.where(r == 0, hi_row, jnp.where(r == 1, lo_row, 0.0)).astype(BF)


def line_of(lanes):
    return jnp.sum(jnp.transpose(lanes), axis=0, keepdims=True)


def rows_kernel(n_t, diag, state, scal, images, *refs):
    texts, refs = refs[:n_t], refs[n_t:]
    given, refs = (refs[:2], refs[2:]) if state else (None, refs)
    w_outs, refs = refs[:n_t], refs[n_t:]
    sums, lanes = refs[-2:]
    half = images.shape[0] // 2
    scale, bias = scal[0], scal[1]
    steps = [(j, c) for j in range(n_t) for c in range(0, texts[j].shape[0], STEP)]

    def text(step):
        j, c = step
        return texts[j][c : c + STEP, :]

    def body(k, none):
        at = pl.multiple_of(k * half, half)
        mine = pl.ds(at, half)
        a = images[mine, :]
        acc = given[0][mine, :] if state else None
        loss = given[1][mine, :] if state else None

        def dot(step):
            return lax.dot_general(a, text(step), NT, preferred_element_type=F32)

        logits, ready = dot(steps[0]), None
        for n, (j, c) in enumerate(steps):
            following = dot(steps[n + 1]) if n + 1 < len(steps) else None
            if ready is not None:
                prod = jnp.dot(ready, text(steps[n - 1]), preferred_element_type=F32)
                acc = prod if acc is None else acc + prod
            flip = None
            if diag and j == 0:
                r = lax.broadcasted_iota(jnp.int32, logits.shape, 0) + at
                q = lax.broadcasted_iota(jnp.int32, logits.shape, 1) + c
                flip = jnp.where(r == q, -1.0, 1.0).astype(F32)
            ready, lane = pair_terms(logits, scale, bias, flip)
            w_outs[j][mine, c : c + STEP] = ready
            loss = lane if loss is None else loss + lane
            logits = following
        sums[mine, :] = acc + jnp.dot(ready, text(steps[-1]), preferred_element_type=F32)
        lanes[mine, :] = loss
        return none

    lax.fori_loop(0, 2, body, None)
    for k, out in enumerate(refs[:-2]):
        rows = out.shape[0] - PAD
        mine = slice(k * rows, (k + 1) * rows)
        out[:rows, :] = sums[mine, :].astype(BF)
        out[rows:, :] = loss_rows_of(line_of(lanes[mine, :]), sums.shape[1])


def rows_step(name, scal, images, texts, state=(), diag=False, finish=0, after=()):
    rows, width = images.shape
    grads = [((rows, width), F32), ((rows, 128), F32)]
    if finish:
        outs, scratch = [((rows // finish + PAD, width), BF)] * finish, grads
    else:
        outs, scratch = grads, []
    outs = call(
        functools.partial(rows_kernel, len(texts), diag, bool(state)),
        name,
        [scal, images, *texts, *state],
        [pltpu.VMEM((rows, t.shape[0]), BF) for t in texts] + [pltpu.VMEM(*g) for g in outs],
        after,
        scratch=[pltpu.VMEM(*g) for g in scratch],
    )
    return outs[: len(texts)], outs[len(texts) :]


def cols_kernel(n_s, n_w, *refs):
    weights, images, outs = refs[: n_s * n_w], refs[n_s * n_w : n_s * (n_w + 1)], refs[n_s * (n_w + 1) :]
    for h in range(n_w):
        acc = None
        for k in range(n_s):
            prod = lax.dot_general(
                weights[k * n_w + h][...], images[k][...], TN, preferred_element_type=F32
            )
            acc = prod if acc is None else acc + prod
        size = acc.shape[0] // len(outs)
        for k, out in enumerate(outs):
            out[h * size : (h + 1) * size, :] = acc[k * size : (k + 1) * size].astype(out.dtype)


def cols_step(name, weights, images, dtypes, after=()):
    width = images[0].shape[1]
    size = sum(w.shape[1] for w in weights[0]) // len(dtypes)
    return call(
        functools.partial(cols_kernel, len(weights), len(weights[0])),
        name,
        [w for group in weights for w in group] + list(images),
        [pltpu.VMEM((size, width), d) for d in dtypes],
        after,
    )


def hold_kernel(*refs):
    count = len(refs) // 2
    for k in range(count):
        refs[count + k][...] = refs[k][...]


def hold(name, values, after):
    return call(hold_kernel, name, list(values), [pltpu.VMEM(v.shape, v.dtype) for v in values], after, cost=1000)


def merge_kernel(a, b, *outs):
    rows = a.shape[0]
    outs[0][:rows, :] = a[...]
    outs[0][rows:, :] = b[...]
    for out, ref in zip(outs[1:], (a, b)):
        out[...] = ref[...]


def merge(name, a, b, after=(), copies=False):
    rows, width = a.shape
    outs = [pltpu.VMEM((2 * rows, width), BF)] + [pltpu.VMEM(a.shape, BF)] * (2 if copies else 0)
    return call(merge_kernel, name, [a, b], outs, after, cost=1000)


def add_kernel(a, b, out):
    out[...] = (a[...] + b[...].astype(F32)).astype(BF)


def add(name, a, b, after=()):
    return call(add_kernel, name, [a, b], [pltpu.VMEM(a.shape, BF)], after)[0]


def sums_kernel(own, lanes, *refs):
    given, outs = refs[:2], refs[2:]
    half = own.shape[0] // 2
    for k in range(2):
        mine = slice(k * half, (k + 1) * half)
        outs[k][:half, :] = (own[mine, :] + given[k][:half, :].astype(F32)).astype(BF)
        tail = jnp.sum(given[k][half:, :half].astype(F32), axis=0, keepdims=True)
        outs[k][half:, :] = loss_rows_of(line_of(lanes[mine, :]) + tail, own.shape[1])


def sums(name, state, given, after):
    return call(sums_kernel, name, [*state, *given], [pltpu.VMEM(g.shape, BF) for g in given], after)


def image_base_kernel(own, lanes, near_a, near_b, base, line):
    half = own.shape[0] // 2
    lines = []
    for k, near in enumerate((near_a, near_b)):
        mine = slice(k * half, (k + 1) * half)
        base[mine, :] = own[mine, :] + near[:half, :].astype(F32)
        lines.append(jnp.sum(near[half:, :half].astype(F32), axis=0, keepdims=True))
    line[...] = jnp.broadcast_to(line_of(lanes[...]) + jnp.concatenate(lines, axis=1), line.shape)


def text_base_kernel(own, more, base):
    base[...] = own[...] + more[...].astype(F32)


def tangent_rows(base, late, unit, factor, out, buf, sem):
    first, size = 0, base.shape[0] // len(late)
    for more in late:

        def body(at, first=first, more=more):
            rows = pl.ds(pl.multiple_of(at.start + first, CHUNK), CHUNK)
            total = base[rows, :] + more[at, :].astype(F32)
            u = unit[rows, :]
            along = jnp.sum(u * total, axis=1, keepdims=True)
            buf[rows, :] = ((total - u * along) * factor[rows, :][:, :1]).astype(BF)
            pltpu.make_async_copy(buf.at[rows, :], out.at[rows, :], sem).start()

        in_chunks(size, body)
        first += size
    pltpu.make_async_copy(buf, out, sem).wait()


def image_kernel(count, base, line, unit, factor, sum_a, sum_b, ready, grad_ref, loss_ref, done, buf, sem):
    half = base.shape[0] // 2
    done[...] = jnp.zeros(done.shape, F32)
    lines = [jnp.sum(s[half:, :half].astype(F32), axis=0, keepdims=True) for s in (sum_a, sum_b)]
    loss_ref[...] = (line[:1, :] + jnp.concatenate(lines, axis=1)) * (1.0 / count)
    tangent_rows(base, [sum_a, sum_b], unit, factor, grad_ref, buf, sem)


def text_kernel(base, unit, factor, late, done, grad_ref, buf, sem):
    tangent_rows(base, [late], unit, factor, grad_ref, buf, sem)


def final(kernel, name, inputs, shape, more):
    return pl.pallas_call(
        kernel,
        name=name,
        in_specs=[VMEM] * len(inputs),
        out_specs=[pl.BlockSpec(memory_space=pl.ANY)] + [VMEM] * len(more),
        out_shape=[jax.ShapeDtypeStruct(shape, BF), *more],
        scratch_shapes=[pltpu.VMEM(shape, BF), pltpu.SemaphoreType.DMA(())],
        cost_estimate=pl.CostEstimate(flops=1000, bytes_accessed=0, transcendentals=0),
        compiler_params=pltpu.CompilerParams(vmem_limit_bytes=8 * 2**20),
    )(*[pltpu.with_memory_space_constraint(x, pltpu.VMEM) for x in inputs])


def per_device(total, image_embeds, text_embeds, log_scale, bias):
    def move(value, dz=0, dy=0, dc=0):
        pairs = [
            (z * 4 + y * 2 + c, (z + dz) % 4 * 4 + (y + dy) % 2 * 2 + (c + dc) % 2)
            for z in range(4)
            for y in range(2)
            for c in range(2)
        ]
        return lax.ppermute(value, "loss", pairs)

    rows, width = image_embeds.shape
    scale = jnp.exp(log_scale[0])
    scal = jnp.stack([scale * (1.0 / math.log(2.0)), bias[0] * (1.0 / math.log(2.0)), scale])
    txt = normalize_hbm(text_embeds, "norm_text")
    txt_y, txt_c = move(txt, dy=1), move(txt, dc=1)
    own, a, b = normalize(image_embeds, "norm_image", True, after=[txt])
    prev_a, next_b = move(a, dz=1), move(b, dz=-1)
    a, b = hold("hold_last", [a, b], [txt_c])
    prev_b, next_a = move(b, dz=1), move(a, dz=-1)
    near_t = [txt, txt_c]
    (own_0, own_c), s_own = rows_step("own_c", scal, own, near_t, diag=True, after=[a])
    first, prev_a, next_b = merge("merge_first", prev_a, next_b, s_own[1:], copies=True)
    far_a, far_b = move(prev_a, dz=1), move(next_b, dz=-1)
    (first_0, first_c), s_first = rows_step("first_c", scal, first, near_t)
    i_unit, i_factor = prepare(scal, image_embeds, "prep_image", s_first[1:])
    (txt_y,) = hold("hold_text", [txt_y], [i_factor])
    far_t = [txt_y, move(txt_y, dc=1)]
    t_unit, t_factor = prepare(scal, text_embeds, "prep_text", [txt_y])
    (own_y, own_yc), s_own = rows_step("own_y", scal, own, far_t, s_own, after=[t_factor, i_factor])
    kept = [i_factor, t_factor, s_own[1]]
    (last,) = merge("merge_last", prev_b, next_a, s_own[1:])
    (last_0, last_c, last_y, last_yc), (g_prev_b, g_next_a) = rows_step(
        "last", scal, last, near_t + far_t, finish=2, after=kept
    )
    near_b, near_a = move(g_prev_b, dz=-1), move(g_next_a, dz=1)
    (far,) = merge("merge_far", far_a, far_b, [g_prev_b])
    (far_0, far_c, far_y, far_yc), (g_far_a, g_far_b) = rows_step(
        "far", scal, far, near_t + far_t, finish=2, after=kept
    )
    through_a, through_b = move(g_far_a, dz=-1), move(g_far_b, dz=1)
    (first_y, first_yc), s_first = rows_step("first_y", scal, first, far_t, s_first, after=[g_far_a, *kept])
    images = [own, first, last, far]
    (gt_yc,) = cols_step("cols_yc", [[own_yc], [first_yc], [last_yc], [far_yc]], images, (BF,), after=kept)
    through_y = move(gt_yc, dc=1)
    (gt_y,) = cols_step("cols_y", [[own_y], [first_y], [last_y], [far_y]], images, (F32,), after=[gt_yc, *kept])
    sum_y = add("add_y", gt_y, through_y)
    text_y = move(sum_y, dy=1)
    (gt_c,) = cols_step(
        "cols_c", [[own_c], [first_c], [last_c], [far_c]], images, (BF,), after=[sum_y, near_a, near_b, *kept]
    )
    text_c = move(gt_c, dc=1)
    to_prev, to_next = sums("sums", s_first, [through_a, through_b], [gt_c])
    sum_a, sum_b = move(to_prev, dz=-1), move(to_next, dz=1)
    (gt_own,) = cols_step(
        "cols_own", [[own_0], [first_0], [last_0], [far_0]], images, (F32,), after=[to_prev, *kept]
    )
    i_base, line = call(
        image_base_kernel,
        "image_base",
        [*s_own, near_a, near_b],
        [pltpu.VMEM((rows, width), F32), pltpu.VMEM((8, rows), F32)],
        [gt_own],
        cost=1000,
    )
    (t_base,) = call(
        text_base_kernel, "text_base", [gt_own, text_c], [pltpu.VMEM((rows, width), F32)], [line], cost=1000
    )
    grad_image, loss, done = final(
        functools.partial(image_kernel, total),
        "image",
        [i_base, line, i_unit, i_factor, sum_a, sum_b, t_base],
        (rows, width),
        [jax.ShapeDtypeStruct((1, rows), F32), pltpu.VMEM((8, 128), F32)],
    )
    (grad_text,) = final(text_kernel, "text", [t_base, t_unit, t_factor, text_y, done], (rows, width), [])
    return loss.reshape(rows), grad_image, grad_text


def solution(mesh):
    placed = (P(("grp", "loss"), None), P(("grp", "loss"), None), P("grp"), P("grp"))

    def whole(image_embeds, text_embeds, log_scale, bias):
        total = image_embeds.shape[0] // mesh.shape["grp"]
        return jax.shard_map(
            functools.partial(per_device, total),
            mesh=mesh,
            in_specs=placed,
            out_specs=(P(("grp", "loss")), P(("grp", "loss"), None), P(("grp", "loss"), None)),
            check_vma=False,
        )(image_embeds, text_embeds, log_scale, bias)

    return whole
```

```python
import functools
import math

import jax
import jax.numpy as jnp
from jax import lax
from jax.experimental import pallas as pl
from jax.experimental.pallas import tpu as pltpu
from jax.sharding import PartitionSpec as P

BF, F32 = jnp.bfloat16, jnp.float32
SMEM = pl.BlockSpec(memory_space=pltpu.SMEM)
VMEM = pl.BlockSpec(memory_space=pltpu.VMEM)
COST = 2 * 10**10
STEP = 256
CHUNK = 128
PAD = 16
NT = (((1,), (1,)), ((), ()))
TN = (((0,), (0,)), ((), ()))


def call(kernel, name, inputs, outs, after=(), scoped=16, cost=COST, scratch=()):
    count = len(inputs)
    inputs = [*inputs, *after]
    specs = [SMEM if x.ndim == 1 else VMEM for x in inputs]

    def body(*refs):
        kernel(*refs[:count], *refs[len(inputs) :])

    return pl.pallas_call(
        body,
        name=name,
        in_specs=specs,
        out_specs=[VMEM] * len(outs),
        out_shape=outs,
        scratch_shapes=scratch,
        cost_estimate=pl.CostEstimate(flops=cost, bytes_accessed=0, transcendentals=0),
        compiler_params=pltpu.CompilerParams(vmem_limit_bytes=scoped * 2**20),
    )(*[x if x.ndim == 1 else pltpu.with_memory_space_constraint(x, pltpu.VMEM) for x in inputs])


def recip_of(wide):
    return lax.rsqrt(jnp.sum(wide * wide, axis=1, keepdims=True) + 1e-06)


def in_chunks(rows, body):
    lax.fori_loop(0, rows // CHUNK, lambda k, none: body(pl.ds(pl.multiple_of(k * CHUNK, CHUNK), CHUNK)), None)


def normalize_kernel(raw, whole, *halves):
    rows = raw.shape[0]

    def body(at):
        wide = raw[at, :].astype(F32)
        whole[at, :] = (wide * recip_of(wide)).astype(BF)

    in_chunks(rows, body)
    for k, out in enumerate(halves):
        out[...] = whole[k * (rows // 2) : (k + 1) * (rows // 2), :]


def normalize(raw, name, halves, after=()):
    rows, width = raw.shape
    outs = [pltpu.VMEM((rows // p, width), BF) for p in ((1, 2, 2) if halves else (1,))]
    return call(normalize_kernel, name, [raw], outs, after)


def normalize_hbm_kernel(raw, whole, buf, sems):
    chunks = [pl.ds(k * CHUNK, CHUNK) for k in range(raw.shape[0] // CHUNK)]
    copies = [pltpu.make_async_copy(raw.at[at, :], buf.at[at, :], sems.at[k]) for k, at in enumerate(chunks)]
    for copy in copies:
        copy.start()
    for at, copy in zip(chunks, copies, strict=True):
        copy.wait()
        wide = buf[at, :].astype(F32)
        whole[at, :] = (wide * recip_of(wide)).astype(BF)


def normalize_hbm(raw, name):
    rows, width = raw.shape
    return pl.pallas_call(
        normalize_hbm_kernel,
        name=name,
        in_specs=[pl.BlockSpec(memory_space=pl.ANY)],
        out_specs=VMEM,
        out_shape=pltpu.VMEM((rows, width), BF),
        scratch_shapes=[pltpu.VMEM((rows, width), BF), pltpu.SemaphoreType.DMA((rows // CHUNK,))],
        cost_estimate=pl.CostEstimate(flops=COST, bytes_accessed=0, transcendentals=0),
        compiler_params=pltpu.CompilerParams(vmem_limit_bytes=8 * 2**20),
    )(pltpu.with_memory_space_constraint(raw, pltpu.HBM))


def prepare_kernel(scal, raw, unit, factor):
    def body(at):
        wide = raw[at, :].astype(F32)
        recip = recip_of(wide)
        unit[at, :] = wide * recip
        factor[at, :] = jnp.broadcast_to(recip * scal[2], (CHUNK, factor.shape[1]))

    in_chunks(raw.shape[0], body)


def prepare(scal, raw, name, after):
    rows, width = raw.shape
    outs = [pltpu.VMEM((rows, width), F32), pltpu.VMEM((rows, 128), F32)]
    return call(prepare_kernel, name, [scal, raw], outs, after)


def pair_terms(logits, scale, bias, flip):
    z = logits * scale + bias
    if flip is not None:
        z = z * flip
    e = jnp.exp2(z)
    u = 1.0 + e
    w = e * pl.reciprocal(u, approx=True)
    if flip is not None:
        w = w * flip
    half = logits.shape[1] // 2
    terms = jnp.log1p(e[:, :half] + e[:, half:] * u[:, :half])
    total = terms[:, :128]
    for k in range(1, half // 128):
        total = total + terms[:, k * 128 : (k + 1) * 128]
    return w.astype(BF), total


def loss_rows_of(line, width):
    hi = line.astype(BF).astype(F32)
    blank = jnp.zeros((1, width - line.shape[1]), F32)
    hi_row = jnp.concatenate([hi, blank], axis=1)
    lo_row = jnp.concatenate([line - hi, blank], axis=1)
    r = lax.broadcasted_iota(jnp.int32, (PAD, width), 0)
    return jnp.where(r == 0, hi_row, jnp.where(r == 1, lo_row, 0.0)).astype(BF)


def line_of(lanes):
    return jnp.sum(jnp.transpose(lanes), axis=0, keepdims=True)


def rows_kernel(n_t, diag, state, scal, images, *refs):
    texts, refs = refs[:n_t], refs[n_t:]
    given, refs = (refs[:2], refs[2:]) if state else (None, refs)
    w_outs, refs = refs[:n_t], refs[n_t:]
    sums, lanes = refs[-2:]
    half = images.shape[0] // 2
    scale, bias = scal[0], scal[1]
    steps = [(j, c) for j in range(n_t) for c in range(0, texts[j].shape[0], STEP)]

    def text(step):
        j, c = step
        return texts[j][c : c + STEP, :]

    def body(k, none):
        at = pl.multiple_of(k * half, half)
        mine = pl.ds(at, half)
        a = images[mine, :]
        acc = given[0][mine, :] if state else None
        loss = given[1][mine, :] if state else None

        def dot(step):
            return lax.dot_general(a, text(step), NT, preferred_element_type=F32)

        logits, ready = dot(steps[0]), None
        for n, (j, c) in enumerate(steps):
            following = dot(steps[n + 1]) if n + 1 < len(steps) else None
            if ready is not None:
                prod = jnp.dot(ready, text(steps[n - 1]), preferred_element_type=F32)
                acc = prod if acc is None else acc + prod
            flip = None
            if diag and j == 0:
                r = lax.broadcasted_iota(jnp.int32, logits.shape, 0) + at
                q = lax.broadcasted_iota(jnp.int32, logits.shape, 1) + c
                flip = jnp.where(r == q, -1.0, 1.0).astype(F32)
            ready, lane = pair_terms(logits, scale, bias, flip)
            w_outs[j][mine, c : c + STEP] = ready
            loss = lane if loss is None else loss + lane
            logits = following
        sums[mine, :] = acc + jnp.dot(ready, text(steps[-1]), preferred_element_type=F32)
        lanes[mine, :] = loss
        return none

    lax.fori_loop(0, 2, body, None)
    for k, out in enumerate(refs[:-2]):
        rows = out.shape[0] - PAD
        mine = slice(k * rows, (k + 1) * rows)
        out[:rows, :] = sums[mine, :].astype(BF)
        out[rows:, :] = loss_rows_of(line_of(lanes[mine, :]), sums.shape[1])


def rows_step(name, scal, images, texts, state=(), diag=False, finish=0, after=()):
    rows, width = images.shape
    grads = [((rows, width), F32), ((rows, 128), F32)]
    if finish:
        outs, scratch = [((rows // finish + PAD, width), BF)] * finish, grads
    else:
        outs, scratch = grads, []
    outs = call(
        functools.partial(rows_kernel, len(texts), diag, bool(state)),
        name,
        [scal, images, *texts, *state],
        [pltpu.VMEM((rows, t.shape[0]), BF) for t in texts] + [pltpu.VMEM(*g) for g in outs],
        after,
        scratch=[pltpu.VMEM(*g) for g in scratch],
    )
    return outs[: len(texts)], outs[len(texts) :]


def cols_kernel(n_s, n_w, *refs):
    weights, images, outs = refs[: n_s * n_w], refs[n_s * n_w : n_s * (n_w + 1)], refs[n_s * (n_w + 1) :]
    for h in range(n_w):
        acc = None
        for k in range(n_s):
            prod = lax.dot_general(
                weights[k * n_w + h][...], images[k][...], TN, preferred_element_type=F32
            )
            acc = prod if acc is None else acc + prod
        size = acc.shape[0] // len(outs)
        for k, out in enumerate(outs):
            out[h * size : (h + 1) * size, :] = acc[k * size : (k + 1) * size].astype(out.dtype)


def cols_step(name, weights, images, dtypes, after=()):
    width = images[0].shape[1]
    size = sum(w.shape[1] for w in weights[0]) // len(dtypes)
    return call(
        functools.partial(cols_kernel, len(weights), len(weights[0])),
        name,
        [w for group in weights for w in group] + list(images),
        [pltpu.VMEM((size, width), d) for d in dtypes],
        after,
    )


def hold_kernel(*refs):
    count = len(refs) // 2
    for k in range(count):
        refs[count + k][...] = refs[k][...]


def hold(name, values, after):
    return call(hold_kernel, name, list(values), [pltpu.VMEM(v.shape, v.dtype) for v in values], after, cost=1000)


def merge_kernel(a, b, *outs):
    rows = a.shape[0]
    outs[0][:rows, :] = a[...]
    outs[0][rows:, :] = b[...]
    for out, ref in zip(outs[1:], (a, b)):
        out[...] = ref[...]


def merge(name, a, b, after=(), copies=False):
    rows, width = a.shape
    outs = [pltpu.VMEM((2 * rows, width), BF)] + [pltpu.VMEM(a.shape, BF)] * (2 if copies else 0)
    return call(merge_kernel, name, [a, b], outs, after, cost=1000)


def add_kernel(a, b, out):
    out[...] = (a[...] + b[...].astype(F32)).astype(BF)


def add(name, a, b, after=()):
    return call(add_kernel, name, [a, b], [pltpu.VMEM(a.shape, BF)], after)[0]


def sums_kernel(own, lanes, *refs):
    given, outs = refs[:2], refs[2:]
    half = own.shape[0] // 2
    for k in range(2):
        mine = slice(k * half, (k + 1) * half)
        outs[k][:half, :] = (own[mine, :] + given[k][:half, :].astype(F32)).astype(BF)
        tail = jnp.sum(given[k][half:, :half].astype(F32), axis=0, keepdims=True)
        outs[k][half:, :] = loss_rows_of(line_of(lanes[mine, :]) + tail, own.shape[1])


def sums(name, state, given, after):
    return call(sums_kernel, name, [*state, *given], [pltpu.VMEM(g.shape, BF) for g in given], after)


def image_base_kernel(own, lanes, near_a, near_b, base, line):
    half = own.shape[0] // 2
    lines = []
    for k, near in enumerate((near_a, near_b)):
        mine = slice(k * half, (k + 1) * half)
        base[mine, :] = own[mine, :] + near[:half, :].astype(F32)
        lines.append(jnp.sum(near[half:, :half].astype(F32), axis=0, keepdims=True))
    line[...] = jnp.broadcast_to(line_of(lanes[...]) + jnp.concatenate(lines, axis=1), line.shape)


def text_base_kernel(own, more, base):
    base[...] = own[...] + more[...].astype(F32)


def tangent_rows(base, late, unit, factor, out, buf, sem):
    first, size = 0, base.shape[0] // len(late)
    for more in late:

        def body(at, first=first, more=more):
            rows = pl.ds(pl.multiple_of(at.start + first, CHUNK), CHUNK)
            total = base[rows, :] + more[at, :].astype(F32)
            u = unit[rows, :]
            along = jnp.sum(u * total, axis=1, keepdims=True)
            buf[rows, :] = ((total - u * along) * factor[rows, :][:, :1]).astype(BF)
            pltpu.make_async_copy(buf.at[rows, :], out.at[rows, :], sem).start()

        in_chunks(size, body)
        first += size
    pltpu.make_async_copy(buf, out, sem).wait()


def image_kernel(count, base, line, unit, factor, sum_a, sum_b, ready, grad_ref, loss_ref, done, buf, sem):
    half = base.shape[0] // 2
    done[...] = jnp.zeros(done.shape, F32)
    lines = [jnp.sum(s[half:, :half].astype(F32), axis=0, keepdims=True) for s in (sum_a, sum_b)]
    loss_ref[...] = (line[:1, :] + jnp.concatenate(lines, axis=1)) * (1.0 / count)
    tangent_rows(base, [sum_a, sum_b], unit, factor, grad_ref, buf, sem)


def text_kernel(base, unit, factor, late, done, grad_ref, buf, sem):
    tangent_rows(base, [late], unit, factor, grad_ref, buf, sem)


def final(kernel, name, inputs, shape, more):
    return pl.pallas_call(
        kernel,
        name=name,
        in_specs=[VMEM] * len(inputs),
        out_specs=[pl.BlockSpec(memory_space=pl.ANY)] + [VMEM] * len(more),
        out_shape=[jax.ShapeDtypeStruct(shape, BF), *more],
        scratch_shapes=[pltpu.VMEM(shape, BF), pltpu.SemaphoreType.DMA(())],
        cost_estimate=pl.CostEstimate(flops=1000, bytes_accessed=0, transcendentals=0),
        compiler_params=pltpu.CompilerParams(vmem_limit_bytes=8 * 2**20),
    )(*[pltpu.with_memory_space_constraint(x, pltpu.VMEM) for x in inputs])


def per_device(total, image_embeds, text_embeds, log_scale, bias):
    def move(value, dz=0, dy=0, dc=0):
        pairs = [
            (z * 4 + y * 2 + c, (z + dz) % 4 * 4 + (y + dy) % 2 * 2 + (c + dc) % 2)
            for z in range(4)
            for y in range(2)
            for c in range(2)
        ]
        return lax.ppermute(value, "loss", pairs)

    rows, width = image_embeds.shape
    scale = jnp.exp(log_scale[0])
    scal = jnp.stack([scale * (1.0 / math.log(2.0)), bias[0] * (1.0 / math.log(2.0)), scale])
    txt = normalize_hbm(text_embeds, "norm_text")
    txt_y, txt_c = move(txt, dy=1), move(txt, dc=1)
    own, a, b = normalize(image_embeds, "norm_image", True, after=[txt])
    prev_a, next_b = move(a, dz=1), move(b, dz=-1)
    a, b = hold("hold_last", [a, b], [txt_c])
    prev_b, next_a = move(b, dz=1), move(a, dz=-1)
    near_t = [txt, txt_c]
    (own_0, own_c), s_own = rows_step("own_c", scal, own, near_t, diag=True, after=[a])
    first, prev_a, next_b = merge("merge_first", prev_a, next_b, s_own[1:], copies=True)
    far_a, far_b = move(prev_a, dz=1), move(next_b, dz=-1)
    (first_0, first_c), s_first = rows_step("first_c", scal, first, near_t)
    i_unit, i_factor = prepare(scal, image_embeds, "prep_image", s_first[1:])
    (txt_y,) = hold("hold_text", [txt_y], [i_factor])
    far_t = [txt_y, move(txt_y, dc=1)]
    (own_y,), s_own = rows_step("own_y", scal, own, far_t[:1], s_own, after=[i_factor])
    (own_yc,), s_own = rows_step("own_yc", scal, own, far_t[1:], s_own)
    kept = [i_factor, s_own[1]]
    (last,) = merge("merge_last", prev_b, next_a, s_own[1:])
    (last_0, last_c, last_y, last_yc), (g_prev_b, g_next_a) = rows_step(
        "last", scal, last, near_t + far_t, finish=2, after=kept
    )
    near_b, near_a = move(g_prev_b, dz=-1), move(g_next_a, dz=1)
    (far,) = merge("merge_far", far_a, far_b, [g_prev_b])
    (far_0, far_c, far_y, far_yc), (g_far_a, g_far_b) = rows_step(
        "far", scal, far, near_t + far_t, finish=2, after=kept
    )
    through_a, through_b = move(g_far_a, dz=-1), move(g_far_b, dz=1)
    (first_y, first_yc), s_first = rows_step("first_y", scal, first, far_t, s_first, after=[g_far_a, *kept])
    images = [own, first, last, far]
    (gt_yc,) = cols_step("cols_yc", [[own_yc], [first_yc], [last_yc], [far_yc]], images, (BF,), after=kept)
    through_y = move(gt_yc, dc=1)
    (gt_y,) = cols_step("cols_y", [[own_y], [first_y], [last_y], [far_y]], images, (F32,), after=[gt_yc, *kept])
    sum_y = add("add_y", gt_y, through_y)
    text_y = move(sum_y, dy=1)
    (gt_c,) = cols_step(
        "cols_c", [[own_c], [first_c], [last_c], [far_c]], images, (BF,), after=[sum_y, near_a, near_b, *kept]
    )
    text_c = move(gt_c, dc=1)
    to_prev, to_next = sums("sums", s_first, [through_a, through_b], [gt_c])
    sum_a, sum_b = move(to_prev, dz=-1), move(to_next, dz=1)
    (gt_own,) = cols_step(
        "cols_own", [[own_0], [first_0], [last_0], [far_0]], images, (F32,), after=[to_prev, *kept]
    )
    i_base, line = call(
        image_base_kernel,
        "image_base",
        [*s_own, near_a, near_b],
        [pltpu.VMEM((rows, width), F32), pltpu.VMEM((8, rows), F32)],
        [gt_own],
        cost=1000,
    )
    (t_base,) = call(
        text_base_kernel, "text_base", [gt_own, text_c], [pltpu.VMEM((rows, width), F32)], [line], cost=1000
    )
    t_unit, t_factor = prepare(scal, text_embeds, "prep_text", [t_base])
    grad_image, loss, done = final(
        functools.partial(image_kernel, total),
        "image",
        [i_base, line, i_unit, i_factor, sum_a, sum_b, t_factor],
        (rows, width),
        [jax.ShapeDtypeStruct((1, rows), F32), pltpu.VMEM((8, 128), F32)],
    )
    (grad_text,) = final(text_kernel, "text", [t_base, t_unit, t_factor, text_y, done], (rows, width), [])
    return loss.reshape(rows), grad_image, grad_text


def solution(mesh):
    placed = (P(("grp", "loss"), None), P(("grp", "loss"), None), P("grp"), P("grp"))

    def whole(image_embeds, text_embeds, log_scale, bias):
        total = image_embeds.shape[0] // mesh.shape["grp"]
        return jax.shard_map(
            functools.partial(per_device, total),
            mesh=mesh,
            in_specs=placed,
            out_specs=(P(("grp", "loss")), P(("grp", "loss"), None), P(("grp", "loss"), None)),
            check_vma=False,
        )(image_embeds, text_embeds, log_scale, bias)

    return whole
```

```python
import functools
import math

import jax
import jax.numpy as jnp
from jax import lax
from jax.experimental import pallas as pl
from jax.experimental.pallas import tpu as pltpu
from jax.sharding import PartitionSpec as P

BF, F32 = jnp.bfloat16, jnp.float32
SMEM = pl.BlockSpec(memory_space=pltpu.SMEM)
VMEM = pl.BlockSpec(memory_space=pltpu.VMEM)
COST = 2 * 10**10
STEP = 256
CHUNK = 128
PAD = 16
NT = (((1,), (1,)), ((), ()))
TN = (((0,), (0,)), ((), ()))


def call(kernel, name, inputs, outs, after=(), scoped=16, cost=COST, scratch=()):
    count = len(inputs)
    inputs = [*inputs, *after]
    specs = [SMEM if x.ndim == 1 else VMEM for x in inputs]

    def body(*refs):
        kernel(*refs[:count], *refs[len(inputs) :])

    return pl.pallas_call(
        body,
        name=name,
        in_specs=specs,
        out_specs=[VMEM] * len(outs),
        out_shape=outs,
        scratch_shapes=scratch,
        cost_estimate=pl.CostEstimate(flops=cost, bytes_accessed=0, transcendentals=0),
        compiler_params=pltpu.CompilerParams(vmem_limit_bytes=scoped * 2**20),
    )(*[x if x.ndim == 1 else pltpu.with_memory_space_constraint(x, pltpu.VMEM) for x in inputs])


def recip_of(wide):
    return lax.rsqrt(jnp.sum(wide * wide, axis=1, keepdims=True) + 1e-06)


def in_chunks(rows, body):
    lax.fori_loop(0, rows // CHUNK, lambda k, none: body(pl.ds(pl.multiple_of(k * CHUNK, CHUNK), CHUNK)), None)


def normalize_kernel(raw, whole, *halves):
    rows = raw.shape[0]

    def body(at):
        wide = raw[at, :].astype(F32)
        whole[at, :] = (wide * recip_of(wide)).astype(BF)

    in_chunks(rows, body)
    for k, out in enumerate(halves):
        out[...] = whole[k * (rows // 2) : (k + 1) * (rows // 2), :]


def normalize(raw, name, halves, after=()):
    rows, width = raw.shape
    outs = [pltpu.VMEM((rows // p, width), BF) for p in ((1, 2, 2) if halves else (1,))]
    return call(normalize_kernel, name, [raw], outs, after)


def normalize_hbm_kernel(raw, whole, buf, sems):
    chunks = [pl.ds(k * CHUNK, CHUNK) for k in range(raw.shape[0] // CHUNK)]
    copies = [pltpu.make_async_copy(raw.at[at, :], buf.at[at, :], sems.at[k]) for k, at in enumerate(chunks)]
    for copy in copies:
        copy.start()
    for at, copy in zip(chunks, copies, strict=True):
        copy.wait()
        wide = buf[at, :].astype(F32)
        whole[at, :] = (wide * recip_of(wide)).astype(BF)


def normalize_hbm(raw, name):
    rows, width = raw.shape
    return pl.pallas_call(
        normalize_hbm_kernel,
        name=name,
        in_specs=[pl.BlockSpec(memory_space=pl.ANY)],
        out_specs=VMEM,
        out_shape=pltpu.VMEM((rows, width), BF),
        scratch_shapes=[pltpu.VMEM((rows, width), BF), pltpu.SemaphoreType.DMA((rows // CHUNK,))],
        cost_estimate=pl.CostEstimate(flops=COST, bytes_accessed=0, transcendentals=0),
        compiler_params=pltpu.CompilerParams(vmem_limit_bytes=8 * 2**20),
    )(pltpu.with_memory_space_constraint(raw, pltpu.HBM))


def prepare_kernel(scal, raw, unit, factor):
    def body(at):
        wide = raw[at, :].astype(F32)
        recip = recip_of(wide)
        unit[at, :] = wide * recip
        factor[at, :] = jnp.broadcast_to(recip * scal[2], (CHUNK, factor.shape[1]))

    in_chunks(raw.shape[0], body)


def prepare(scal, raw, name, after):
    rows, width = raw.shape
    outs = [pltpu.VMEM((rows, width), F32), pltpu.VMEM((rows, 128), F32)]
    return call(prepare_kernel, name, [scal, raw], outs, after)


def pair_terms(logits, scale, bias, flip):
    z = logits * scale + bias
    if flip is not None:
        z = z * flip
    e = jnp.exp2(z)
    u = 1.0 + e
    w = e * pl.reciprocal(u, approx=True)
    if flip is not None:
        w = w * flip
    half = logits.shape[1] // 2
    terms = jnp.log1p(e[:, :half] + e[:, half:] * u[:, :half])
    total = terms[:, :128]
    for k in range(1, half // 128):
        total = total + terms[:, k * 128 : (k + 1) * 128]
    return w.astype(BF), total


def loss_rows_of(line, width):
    hi = line.astype(BF).astype(F32)
    blank = jnp.zeros((1, width - line.shape[1]), F32)
    hi_row = jnp.concatenate([hi, blank], axis=1)
    lo_row = jnp.concatenate([line - hi, blank], axis=1)
    r = lax.broadcasted_iota(jnp.int32, (PAD, width), 0)
    return jnp.where(r == 0, hi_row, jnp.where(r == 1, lo_row, 0.0)).astype(BF)


def line_of(lanes):
    return jnp.sum(jnp.transpose(lanes), axis=0, keepdims=True)


def rows_kernel(n_t, diag, state, scal, images, *refs):
    texts, refs = refs[:n_t], refs[n_t:]
    given, refs = (refs[:2], refs[2:]) if state else (None, refs)
    w_outs, refs = refs[:n_t], refs[n_t:]
    sums, lanes = refs[-2:]
    half = images.shape[0] // 2
    scale, bias = scal[0], scal[1]
    steps = [(j, c) for j in range(n_t) for c in range(0, texts[j].shape[0], STEP)]

    def text(step):
        j, c = step
        return texts[j][c : c + STEP, :]

    def body(k, none):
        at = pl.multiple_of(k * half, half)
        mine = pl.ds(at, half)
        a = images[mine, :]
        acc = given[0][mine, :] if state else None
        loss = given[1][mine, :] if state else None

        def dot(step):
            return lax.dot_general(a, text(step), NT, preferred_element_type=F32)

        logits, ready = dot(steps[0]), None
        for n, (j, c) in enumerate(steps):
            following = dot(steps[n + 1]) if n + 1 < len(steps) else None
            if ready is not None:
                prod = jnp.dot(ready, text(steps[n - 1]), preferred_element_type=F32)
                acc = prod if acc is None else acc + prod
            flip = None
            if diag and j == 0:
                r = lax.broadcasted_iota(jnp.int32, logits.shape, 0) + at
                q = lax.broadcasted_iota(jnp.int32, logits.shape, 1) + c
                flip = jnp.where(r == q, -1.0, 1.0).astype(F32)
            ready, lane = pair_terms(logits, scale, bias, flip)
            w_outs[j][mine, c : c + STEP] = ready
            loss = lane if loss is None else loss + lane
            logits = following
        sums[mine, :] = acc + jnp.dot(ready, text(steps[-1]), preferred_element_type=F32)
        lanes[mine, :] = loss
        return none

    lax.fori_loop(0, 2, body, None)
    for k, out in enumerate(refs[:-2]):
        rows = out.shape[0] - PAD
        mine = slice(k * rows, (k + 1) * rows)
        out[:rows, :] = sums[mine, :].astype(BF)
        out[rows:, :] = loss_rows_of(line_of(lanes[mine, :]), sums.shape[1])


def rows_step(name, scal, images, texts, state=(), diag=False, finish=0, after=()):
    rows, width = images.shape
    grads = [((rows, width), F32), ((rows, 128), F32)]
    if finish:
        outs, scratch = [((rows // finish + PAD, width), BF)] * finish, grads
    else:
        outs, scratch = grads, []
    outs = call(
        functools.partial(rows_kernel, len(texts), diag, bool(state)),
        name,
        [scal, images, *texts, *state],
        [pltpu.VMEM((rows, t.shape[0]), BF) for t in texts] + [pltpu.VMEM(*g) for g in outs],
        after,
        scratch=[pltpu.VMEM(*g) for g in scratch],
    )
    return outs[: len(texts)], outs[len(texts) :]


def cols_kernel(n_s, n_w, *refs):
    weights, images, outs = refs[: n_s * n_w], refs[n_s * n_w : n_s * (n_w + 1)], refs[n_s * (n_w + 1) :]
    for h in range(n_w):
        acc = None
        for k in range(n_s):
            prod = lax.dot_general(
                weights[k * n_w + h][...], images[k][...], TN, preferred_element_type=F32
            )
            acc = prod if acc is None else acc + prod
        size = acc.shape[0] // len(outs)
        for k, out in enumerate(outs):
            out[h * size : (h + 1) * size, :] = acc[k * size : (k + 1) * size].astype(out.dtype)


def cols_step(name, weights, images, dtypes, after=()):
    width = images[0].shape[1]
    size = sum(w.shape[1] for w in weights[0]) // len(dtypes)
    return call(
        functools.partial(cols_kernel, len(weights), len(weights[0])),
        name,
        [w for group in weights for w in group] + list(images),
        [pltpu.VMEM((size, width), d) for d in dtypes],
        after,
    )


def hold_kernel(*refs):
    count = len(refs) // 2
    for k in range(count):
        refs[count + k][...] = refs[k][...]


def hold(name, values, after):
    return call(hold_kernel, name, list(values), [pltpu.VMEM(v.shape, v.dtype) for v in values], after, cost=1000)


def merge_kernel(a, b, *outs):
    rows = a.shape[0]
    outs[0][:rows, :] = a[...]
    outs[0][rows:, :] = b[...]
    for out, ref in zip(outs[1:], (a, b)):
        out[...] = ref[...]


def merge(name, a, b, after=(), copies=False):
    rows, width = a.shape
    outs = [pltpu.VMEM((2 * rows, width), BF)] + [pltpu.VMEM(a.shape, BF)] * (2 if copies else 0)
    return call(merge_kernel, name, [a, b], outs, after, cost=1000)


def add_kernel(a, b, out):
    out[...] = (a[...] + b[...].astype(F32)).astype(BF)


def add(name, a, b, after=()):
    return call(add_kernel, name, [a, b], [pltpu.VMEM(a.shape, BF)], after)[0]


def sums_kernel(own, lanes, *refs):
    given, outs = refs[:2], refs[2:]
    half = own.shape[0] // 2
    for k in range(2):
        mine = slice(k * half, (k + 1) * half)
        outs[k][:half, :] = (own[mine, :] + given[k][:half, :].astype(F32)).astype(BF)
        tail = jnp.sum(given[k][half:, :half].astype(F32), axis=0, keepdims=True)
        outs[k][half:, :] = loss_rows_of(line_of(lanes[mine, :]) + tail, own.shape[1])


def sums(name, state, given, after):
    return call(sums_kernel, name, [*state, *given], [pltpu.VMEM(g.shape, BF) for g in given], after)


def image_base_kernel(own, lanes, near_a, near_b, base, line):
    half = own.shape[0] // 2
    lines = []
    for k, near in enumerate((near_a, near_b)):
        mine = slice(k * half, (k + 1) * half)
        base[mine, :] = own[mine, :] + near[:half, :].astype(F32)
        lines.append(jnp.sum(near[half:, :half].astype(F32), axis=0, keepdims=True))
    line[...] = jnp.broadcast_to(line_of(lanes[...]) + jnp.concatenate(lines, axis=1), line.shape)


def text_base_kernel(own, more, base):
    base[...] = own[...] + more[...].astype(F32)


def tangent_rows(base, late, unit, factor, out, buf, sem):
    first, size = 0, base.shape[0] // len(late)
    for more in late:

        def body(at, first=first, more=more):
            rows = pl.ds(pl.multiple_of(at.start + first, CHUNK), CHUNK)
            total = base[rows, :] + more[at, :].astype(F32)
            u = unit[rows, :]
            along = jnp.sum(u * total, axis=1, keepdims=True)
            buf[rows, :] = ((total - u * along) * factor[rows, :][:, :1]).astype(BF)
            pltpu.make_async_copy(buf.at[rows, :], out.at[rows, :], sem).start()

        in_chunks(size, body)
        first += size
    pltpu.make_async_copy(buf, out, sem).wait()


def image_kernel(count, base, line, unit, factor, sum_a, sum_b, ready, grad_ref, loss_ref, done, buf, sem):
    half = base.shape[0] // 2
    done[...] = jnp.zeros(done.shape, F32)
    lines = [jnp.sum(s[half:, :half].astype(F32), axis=0, keepdims=True) for s in (sum_a, sum_b)]
    loss_ref[...] = (line[:1, :] + jnp.concatenate(lines, axis=1)) * (1.0 / count)
    tangent_rows(base, [sum_a, sum_b], unit, factor, grad_ref, buf, sem)


def text_kernel(base, unit, factor, late, done, grad_ref, buf, sem):
    tangent_rows(base, [late], unit, factor, grad_ref, buf, sem)


def final(kernel, name, inputs, shape, more):
    return pl.pallas_call(
        kernel,
        name=name,
        in_specs=[VMEM] * len(inputs),
        out_specs=[pl.BlockSpec(memory_space=pl.ANY)] + [VMEM] * len(more),
        out_shape=[jax.ShapeDtypeStruct(shape, BF), *more],
        scratch_shapes=[pltpu.VMEM(shape, BF), pltpu.SemaphoreType.DMA(())],
        cost_estimate=pl.CostEstimate(flops=1000, bytes_accessed=0, transcendentals=0),
        compiler_params=pltpu.CompilerParams(vmem_limit_bytes=8 * 2**20),
    )(*[pltpu.with_memory_space_constraint(x, pltpu.VMEM) for x in inputs])


def per_device(total, image_embeds, text_embeds, log_scale, bias):
    def move(value, dz=0, dy=0, dc=0):
        pairs = [
            (z * 4 + y * 2 + c, (z + dz) % 4 * 4 + (y + dy) % 2 * 2 + (c + dc) % 2)
            for z in range(4)
            for y in range(2)
            for c in range(2)
        ]
        return lax.ppermute(value, "loss", pairs)

    rows, width = image_embeds.shape
    scale = jnp.exp(log_scale[0])
    scal = jnp.stack([scale * (1.0 / math.log(2.0)), bias[0] * (1.0 / math.log(2.0)), scale])
    txt = normalize_hbm(text_embeds, "norm_text")
    txt_y, txt_c = move(txt, dy=1), move(txt, dc=1)
    own, a, b = normalize(image_embeds, "norm_image", True, after=[txt])
    prev_a, next_b = move(a, dz=1), move(b, dz=-1)
    a, b = hold("hold_last", [a, b], [txt_c])
    prev_b, next_a = move(b, dz=1), move(a, dz=-1)
    near_t = [txt, txt_c]
    (own_0, own_c), s_own = rows_step("own_c", scal, own, near_t, diag=True, after=[a])
    first, prev_a, next_b = merge("merge_first", prev_a, next_b, s_own[1:], copies=True)
    far_a, far_b = move(prev_a, dz=1), move(next_b, dz=-1)
    (first_0, first_c), s_first = rows_step("first_c", scal, first, near_t)
    (txt_y,) = hold("hold_text", [txt_y], s_first[1:])
    far_t = [txt_y, move(txt_y, dc=1)]
    (own_y,), s_own = rows_step("own_y", scal, own, far_t[:1], s_own, after=[txt_y])
    (own_yc,), s_own = rows_step("own_yc", scal, own, far_t[1:], s_own)
    kept = [s_own[1]]
    (last,) = merge("merge_last", prev_b, next_a, s_own[1:])
    (last_0, last_c, last_y, last_yc), (g_prev_b, g_next_a) = rows_step(
        "last", scal, last, near_t + far_t, finish=2, after=kept
    )
    near_b, near_a = move(g_prev_b, dz=-1), move(g_next_a, dz=1)
    (far,) = merge("merge_far", far_a, far_b, [g_prev_b])
    (far_0, far_c, far_y, far_yc), (g_far_a, g_far_b) = rows_step(
        "far", scal, far, near_t + far_t, finish=2, after=kept
    )
    through_a, through_b = move(g_far_a, dz=-1), move(g_far_b, dz=1)
    (first_y, first_yc), s_first = rows_step("first_y", scal, first, far_t, s_first, after=[g_far_a, *kept])
    images = [own, first, last, far]
    (gt_yc,) = cols_step("cols_yc", [[own_yc], [first_yc], [last_yc], [far_yc]], images, (BF,), after=kept)
    through_y = move(gt_yc, dc=1)
    (gt_y,) = cols_step("cols_y", [[own_y], [first_y], [last_y], [far_y]], images, (F32,), after=[gt_yc, *kept])
    sum_y = add("add_y", gt_y, through_y)
    text_y = move(sum_y, dy=1)
    (gt_c,) = cols_step(
        "cols_c", [[own_c], [first_c], [last_c], [far_c]], images, (BF,), after=[sum_y, near_a, near_b, *kept]
    )
    text_c = move(gt_c, dc=1)
    to_prev, to_next = sums("sums", s_first, [through_a, through_b], [gt_c])
    sum_a, sum_b = move(to_prev, dz=-1), move(to_next, dz=1)
    (gt_own,) = cols_step(
        "cols_own", [[own_0], [first_0], [last_0], [far_0]], images, (F32,), after=[to_prev, *kept]
    )
    i_base, line = call(
        image_base_kernel,
        "image_base",
        [*s_own, near_a, near_b],
        [pltpu.VMEM((rows, width), F32), pltpu.VMEM((8, rows), F32)],
        [gt_own],
        cost=1000,
    )
    (t_base,) = call(
        text_base_kernel, "text_base", [gt_own, text_c], [pltpu.VMEM((rows, width), F32)], [line], cost=1000
    )
    i_unit, i_factor = prepare(scal, image_embeds, "prep_image", [t_base])
    t_unit, t_factor = prepare(scal, text_embeds, "prep_text", [i_factor])
    grad_image, loss, done = final(
        functools.partial(image_kernel, total),
        "image",
        [i_base, line, i_unit, i_factor, sum_a, sum_b, t_factor],
        (rows, width),
        [jax.ShapeDtypeStruct((1, rows), F32), pltpu.VMEM((8, 128), F32)],
    )
    (grad_text,) = final(text_kernel, "text", [t_base, t_unit, t_factor, text_y, done], (rows, width), [])
    return loss.reshape(rows), grad_image, grad_text


def solution(mesh):
    placed = (P(("grp", "loss"), None), P(("grp", "loss"), None), P("grp"), P("grp"))

    def whole(image_embeds, text_embeds, log_scale, bias):
        total = image_embeds.shape[0] // mesh.shape["grp"]
        return jax.shard_map(
            functools.partial(per_device, total),
            mesh=mesh,
            in_specs=placed,
            out_specs=(P(("grp", "loss")), P(("grp", "loss"), None), P(("grp", "loss"), None)),
            check_vma=False,
        )(image_embeds, text_embeds, log_scale, bias)

    return whole
```
